32 devices in a mesh: ex: 4 (over z), row: 4 (over y, x), col: 2 (over core).
Axes of the slice: x: 2, y: 2, z: 4, core: 2. Of those that a mesh axis runs over, the one named last changes fastest.
Arguments:
- x_in: bfloat16 [4096, 768], P(('ex', 'row')), may hold values from -6 to 6
- gain_attn: float32 [768], replicated, may hold values from 0.25 to 1.75
- w_qkv: float32 [3, 768, 768], P(None, ('ex', 'row'), 'col'), may hold values from -0.21875 to 0.21875
- rel_bias: float32 [32, 12], P(None, 'col'), may hold values from -4 to 4
- w_out: float32 [768, 768], P('col', ('ex', 'row')), may hold values from -1.75 to 1.75
- gain_ffn: float32 [768], replicated, may hold values from 0.25 to 1.75
- w_router: float32 [768, 16], P(('ex', 'row')), may hold values from -0.109375 to 0.109375
- w_up: float32 [16, 768, 3072], P(('ex', 'row'), None, 'col'), may hold values from -0.21875 to 0.21875
- w_down: float32 [16, 3072, 768], P(('ex', 'row'), 'col'), may hold values from -2.5 to 2.5
- seg_ids: int32 [16, 256], P(('ex', 'row')), may hold values from 0 to 3, never falling along the last dimension, each value on 1 to 128 neighbouring positions
- expert_ids: int32 [4096], P(('ex', 'row')), may hold values from 0 to 15, as said below
- slot_ids: int32 [4096], P(('ex', 'row')), may hold values from 0 to 19, as said below
- drop_flags: int32 [4096], P(('ex', 'row')), may hold values from 0 to 1, as said below
- d_out: bfloat16 [4096, 768], P(('ex', 'row'), 'col'), may hold values from -6 to 6
Outputs:
- layer_out: bfloat16 [4096, 768], P(('ex', 'row'), 'col')
- grad_x: bfloat16 [4096, 768], P(('ex', 'row'))
- grad_gain_attn: float32 [768], replicated
- grad_w_qkv: float32 [3, 768, 768], P(None, ('ex', 'row'), 'col')
- grad_rel_bias: float32 [32, 12], P(None, 'col')
- grad_w_out: float32 [768, 768], P('col', ('ex', 'row'))
- grad_gain_ffn: float32 [768], replicated
- grad_w_router: float32 [768, 16], P(('ex', 'row'))
- grad_w_up: float32 [16, 768, 3072], P(('ex', 'row'), None, 'col')
- grad_w_down: float32 [16, 3072, 768], P(('ex', 'row'), 'col')
The draws below stay inside these ranges and needn't reach their ends.
Inputs may be any that keep to these rules, and one draw needn't show every extreme that they name: `expert_ids`: within the 256 tokens of one sequence, the kept tokens that chose one expert hold slots 0, 1, 2, ... in token order. In every draw one expert receives 20 kept tokens from every sequence. `slot_ids`: A kept token's slot is the number of earlier tokens of its sequence that chose its expert. `drop_flags`: A token is dropped exactly when 20 earlier tokens of its sequence chose its expert. `seg_ids`: document numbers never fall along a sequence; each of the 4 documents of a sequence has a token.
All inputs are finite; a program needn't handle non-finite values.
Results may differ from the reference program's by a relative error of at most 0.022.
Values may be sent and summed in bfloat16 or wider, within the bound.
No kernel may reach another device: no remote copies, remote signals or barrier semaphores. Data moves between devices by JAX's collectives and lax.ppermute only.
A program may use at most 128 MiB of HBM per device.

```python
import math
from functools import partial
import jax
import jax.numpy as jnp
import numpy as np
from jax import lax

D = 768
H = 12
HEAD = 64
FF = 3072
BUCKETS = 32
LEN = 256
SEQS = 16
EXPERTS = 16
CAP = 20
TOKENS = 4096


def route_table(key):
    base_key = jax.random.fold_in(key, 7301)
    key_perm = jax.random.fold_in(base_key, 1)
    key_first = jax.random.fold_in(base_key, 2)
    key_second = jax.random.fold_in(base_key, 3)
    key_shuffle = jax.random.fold_in(base_key, 4)
    blocks = TOKENS // LEN
    expert_order = jax.random.permutation(key_perm, EXPERTS).astype(jnp.int32)
    first_pick = jax.random.randint(key_first, (blocks, LEN), 0, EXPERTS, dtype=jnp.int32)
    second = jax.random.randint(key_second, (blocks, LEN), 0, EXPERTS, dtype=jnp.int32)
    skewed = expert_order[jnp.minimum(first_pick, second)].astype(jnp.int32)
    forced = jnp.arange(LEN, dtype=jnp.int32)[None, :] < 2 * CAP
    chosen = jnp.where(forced, expert_order[0], skewed).astype(jnp.int32)
    shuffle_keys = jax.random.split(key_shuffle, blocks)
    shuffled = jax.vmap(jax.random.permutation)(shuffle_keys, chosen).astype(jnp.int32)
    onehot = (shuffled[:, :, None] == jnp.arange(EXPERTS, dtype=jnp.int32)[None, None, :]).astype(jnp.int32)
    running = jnp.cumsum(onehot, axis=1).astype(jnp.int32)
    rank_in = jnp.sum(onehot * (running - 1), axis=2).astype(jnp.int32)
    return (shuffled.reshape(TOKENS).astype(jnp.int32), rank_in.reshape(TOKENS).astype(jnp.int32))


def draw_expert_ids(key, part):
    return route_table(key)[0]


def draw_slot_ids(key, part):
    return jnp.minimum(route_table(key)[1], CAP - 1).astype(jnp.int32)


def draw_drop_flags(key, part):
    return (route_table(key)[1] >= CAP).astype(jnp.int32)


def block_levels(own_key, extent, shards, low, high):
    def one(axis_at, shards_of):
        steps = jax.random.uniform(jax.random.fold_in(jax.random.fold_in(own_key, 6), axis_at), (shards_of,), jnp.float32, low / len(shards), high / len(shards))
        return jnp.repeat(jnp.exp(steps), extent[axis_at] // shards_of).reshape((-1,) + (1,) * (len(extent) - axis_at - 1))

    loudness = one(*shards[0])
    for cut in shards[1:]:
        loudness = loudness * one(*cut)
    return loudness


def split_up(number_of, total, limit, skew):
    weights = [(1 << 20) // math.isqrt(grade ** skew) + 1 for grade in range(2, number_of + 1)]
    surplus, given = total - limit - (number_of - 1), [1] * (number_of - 1)
    while surplus > 0:
        candidates = [i for i in range(number_of - 1) if given[i] < limit]
        mass, budget = sum([weights[i] for i in candidates]), surplus
        for i in candidates:
            more = min(limit - given[i], max(1, budget * weights[i] // mass), surplus)
            given[i] = given[i] + more
            surplus = surplus - more
    return np.array([limit] + given)


def ragged_sizes(rng, count, total, bound, skew):
    if count == 2:
        one = jax.random.randint(rng, (), max(1, total - bound), min(bound, total - 1) + 1)
        return jnp.stack([one, total - one])
    sizes = jnp.asarray(split_up(count, total, bound, skew), jnp.int32)
    pairs = (count - 1) // 2
    donor, taker = sizes[1:1 + 2 * pairs:2], sizes[2:2 + 2 * pairs:2]
    margin = jnp.minimum(donor - 1, bound - taker)
    moved = jax.random.randint(jax.random.fold_in(rng, 1), (pairs,), 0, 1 << 20) % (margin + 1)
    sizes = sizes.at[1:1 + 2 * pairs:2].set(donor - moved).at[2:2 + 2 * pairs:2].set(taker + moved)
    return sizes[jax.random.permutation(jax.random.fold_in(rng, 2), count)]


def centred(rng, dims, scale, limit, pieces=(), kind=jnp.bfloat16):
    entries = jax.random.normal(rng, dims, jnp.float32) * scale
    if len(pieces) > 0:
        entries = block_levels(rng, dims, pieces, -0.22, 0.18) * entries
    return jnp.clip(entries, min=-limit, max=limit).astype(kind)


def setup_inputs(seed: int = 0) -> dict:
    seeds = jax.random.split(jax.random.key(seed), 15)
    x_in = centred(seeds[0], (TOKENS, D), 1.0, 6.0, ((0, 16),))
    gain_attn = jnp.clip(1.0 + 0.15 * jax.random.normal(seeds[1], (D,), jnp.float32), 0.25, 1.75)
    w_qkv = centred(seeds[2], (3, D, H * HEAD), D ** -0.5, 0.21875, ((1, 16), (2, 2)), jnp.float32)
    rel_bias = centred(seeds[3], (BUCKETS, H), 1.0, 4.0, ((1, 2),), jnp.float32)
    w_out = centred(seeds[4], (H * HEAD, D), (max(1, 4 * H * HEAD // LEN)) ** -0.5, 1.75, ((0, 2), (1, 16)), jnp.float32)
    gain_ffn = jnp.clip(1.0 + 0.15 * jax.random.normal(seeds[5], (D,), jnp.float32), 0.25, 1.75)
    w_router = centred(seeds[6], (D, EXPERTS), (4 * D) ** -0.5, 0.109375, ((0, 16),), jnp.float32)
    w_up = centred(seeds[7], (EXPERTS, D, FF), D ** -0.5, 0.21875, ((0, 16), (2, 2)), jnp.float32)
    w_down = centred(seeds[8], (EXPERTS, FF, D), (EXPERTS * (FF // 2) ** -0.5), 2.5, ((0, 16), (1, 2)), jnp.float32)
    seg_ids = jax.vmap(lambda own: jnp.searchsorted(jnp.cumsum(ragged_sizes(own, 4, LEN, LEN // 2, 2)), jnp.arange(LEN), side="right"))(jax.random.split(seeds[9], SEQS)).reshape((SEQS, LEN)).astype(jnp.int32)
    expert_ids = draw_expert_ids(jax.random.fold_in(seeds[14], 71), 0)
    slot_ids = draw_slot_ids(jax.random.fold_in(seeds[14], 71), 0)
    drop_flags = draw_drop_flags(jax.random.fold_in(seeds[14], 71), 0)
    d_out = centred(seeds[13], (TOKENS, D), 1.0, 6.0, ((0, 16), (1, 2)))
    return {"x_in": x_in, "gain_attn": gain_attn, "w_qkv": w_qkv, "rel_bias": rel_bias, "w_out": w_out, "gain_ffn": gain_ffn, "w_router": w_router, "w_up": w_up, "w_down": w_down, "seg_ids": seg_ids, "expert_ids": expert_ids, "slot_ids": slot_ids, "drop_flags": drop_flags, "d_out": d_out}


norm_eps = 1e-06
bucket_edges = (12, 16, 23, 32, 46, 64, 91)
highest = lax.Precision.HIGHEST

@jax.custom_vjp
def low(v):
    return lax.optimization_barrier(v.astype(jnp.bfloat16)).astype(jnp.float32)

@jax.custom_vjp
def low_back(v):
    return v

def low_keep(v):
    return (low(v), None)

def low_pass(kept, grad):
    return (grad,)

def back_keep(v):
    return (v, None)

def back_low(kept, grad):
    return (low(grad),)
low.defvjp(low_keep, low_pass)
low_back.defvjp(back_keep, back_low)

def bucket_of(offset):
    distance = jnp.abs(offset).astype(jnp.int32)
    far_part = jnp.zeros(distance.shape, jnp.int32)
    for edge_at in bucket_edges:
        far_part = far_part + (distance >= edge_at).astype(jnp.int32)
    inside = jnp.where(distance < 8, distance, far_part + jnp.int32(8)).astype(jnp.int32)
    upper = jnp.where(offset > 0, jnp.int32(BUCKETS // 2), jnp.int32(0)).astype(jnp.int32)
    return (inside + upper).astype(jnp.int32)

def rms_scale(values):
    return lax.rsqrt(lax.optimization_barrier(jnp.mean(values * values, axis=-1, keepdims=True)) + norm_eps)

def masked_softmax(scores, counted):
    peak = lax.optimization_barrier(jnp.max(jnp.where(counted, scores, jnp.float32(-1000000000.0)), axis=-1, keepdims=True))
    shifted = jnp.where(counted, scores - peak, jnp.float32(0.0))
    expo = jnp.where(counted, jnp.exp(shifted), jnp.float32(0.0))
    return expo / lax.optimization_barrier(jnp.sum(expo, axis=-1, keepdims=True))

def attend_group(group_parts, bias_full):
    q_part, k_part, v_part, seg_part = group_parts
    scores = jnp.einsum('sqhe,skhe->shqk', q_part, k_part, precision=highest) * 0.125 + bias_full[None]
    scores = low_back(scores)
    same_doc = seg_part[:, None, :, None] == seg_part[:, None, None, :]
    weights = low(masked_softmax(scores, same_doc))
    return jnp.einsum('shqk,skhe->sqhe', weights, v_part, precision=highest)

def expert_pass(expert_parts):
    rows_in, up_master, down_master = expert_parts
    pre_act = low_back(jnp.dot(rows_in, low(up_master), precision=highest))
    act_b = low(jax.nn.gelu(pre_act, approximate=False))
    return low_back(low(jnp.dot(act_b, low(down_master), precision=highest)))

def layer_forward(x_in, gain_attn, w_qkv, rel_bias, w_out, gain_ffn, w_router, w_up, w_down, seg_ids, expert_ids, slot_ids, drop_flags):
    normed_one = x_in * rms_scale(x_in) * gain_attn
    h_one = low(normed_one)
    qkv_vals = low_back(low(jnp.einsum('td,sde->ste', h_one, low(w_qkv), precision=highest)))
    group_size = math.gcd(SEQS, max(1, 4096 // LEN))
    shaped = qkv_vals.reshape(3, SEQS // group_size, group_size, LEN, H, HEAD)
    seg_groups = seg_ids.astype(jnp.int32).reshape(SEQS // group_size, group_size, LEN)
    positions = jnp.arange(LEN, dtype=jnp.int32)
    buckets = bucket_of(positions[None, :] - positions[:, None])
    bucket_hot = (buckets[:, :, None] == jnp.arange(BUCKETS, dtype=jnp.int32)[None, None, :]).astype(jnp.float32)
    bias_full = jnp.einsum('qkb,bh->hqk', bucket_hot, rel_bias, precision=highest)
    context = lax.map(jax.checkpoint(partial(attend_group, bias_full=bias_full)), (shaped[0], shaped[1], shaped[2], seg_groups))
    context = low_back(low(context.reshape(TOKENS, H * HEAD)))
    attn_out = low_back(jnp.dot(context, low(w_out), precision=highest))
    x_one = x_in + attn_out
    h_two = low(x_one * rms_scale(x_one) * gain_ffn)
    logits = low_back(jnp.dot(h_two, low(w_router), precision=highest))
    peak = lax.optimization_barrier(jnp.max(logits, axis=-1, keepdims=True))
    expo = jnp.exp(logits - peak)
    router_probs = expo / lax.optimization_barrier(jnp.sum(expo, axis=-1, keepdims=True))
    expert_hot = (expert_ids.astype(jnp.int32)[:, None] == jnp.arange(EXPERTS, dtype=jnp.int32)[None, :]).astype(jnp.float32)
    gate_prob = lax.optimization_barrier(jnp.sum(router_probs * expert_hot, axis=-1))
    keep_flag = (1 - drop_flags.astype(jnp.int32)).astype(jnp.float32)
    seq_of = (jnp.arange(TOKENS, dtype=jnp.int32) // LEN).astype(jnp.int32)
    dest_row = jnp.where(drop_flags.astype(jnp.int32) == 1, jnp.int32(EXPERTS * SEQS * CAP), (expert_ids.astype(jnp.int32) * SEQS + seq_of) * CAP + slot_ids.astype(jnp.int32)).astype(jnp.int32)
    buffer_rows = jnp.zeros((EXPERTS * SEQS * CAP + 1, D), jnp.float32).at[dest_row].add(h_two)
    expert_in = low_back(buffer_rows[:EXPERTS * SEQS * CAP].reshape(EXPERTS, SEQS * CAP, D))
    expert_out = lax.map(jax.checkpoint(expert_pass), (expert_in, w_up, w_down))
    flat_out = jnp.concatenate([expert_out.reshape(EXPERTS * SEQS * CAP, D), jnp.zeros((1, D), jnp.float32)], axis=0)
    picked = flat_out[dest_row]
    return x_one + picked * (gate_prob * keep_flag)[:, None]

def reference(x_in, gain_attn, w_qkv, rel_bias, w_out, gain_ffn, w_router, w_up, w_down, seg_ids, expert_ids, slot_ids, drop_flags, d_out):
    floats = (x_in.astype(jnp.float32), gain_attn.astype(jnp.float32), w_qkv.astype(jnp.float32), rel_bias.astype(jnp.float32), w_out.astype(jnp.float32), gain_ffn.astype(jnp.float32), w_router.astype(jnp.float32), w_up.astype(jnp.float32), w_down.astype(jnp.float32))
    forward = partial(layer_forward, seg_ids=seg_ids, expert_ids=expert_ids, slot_ids=slot_ids, drop_flags=drop_flags)
    layer_out, pull_back = jax.vjp(forward, *floats)
    grad_list = pull_back(d_out.astype(jnp.float32))
    return (layer_out.astype(jnp.bfloat16), grad_list[0].astype(jnp.bfloat16), grad_list[1], grad_list[2], grad_list[3], grad_list[4], grad_list[5], grad_list[6], grad_list[7], grad_list[8])
```

```python
import math

import jax
import jax.numpy as jnp
from jax import lax
from jax.sharding import PartitionSpec as P

HEAD = 64
BUCKETS = 32

norm_eps = 1e-06
bucket_edges = (12, 16, 23, 32, 46, 64, 91)
highest = lax.Precision.HIGHEST
bf16 = jnp.bfloat16
f32 = jnp.float32


def bucket_of(offset):
    distance = jnp.abs(offset)
    far_part = jnp.zeros(distance.shape, jnp.int32)
    for edge_at in bucket_edges:
        far_part = far_part + (distance >= edge_at).astype(jnp.int32)
    inside = jnp.where(distance < 8, distance, far_part + jnp.int32(8))
    upper = jnp.where(offset > 0, jnp.int32(BUCKETS // 2), jnp.int32(0))
    return inside + upper


def rms_scale(values):
    return lax.rsqrt(jnp.mean(values * values, axis=-1, keepdims=True) + norm_eps)


def gelu_slope(values):
    cdf_vals = 0.5 * (1.0 + lax.erf(values * (1.0 / math.sqrt(2.0))))
    pdf_vals = jnp.exp(-0.5 * values * values) * (1.0 / math.sqrt(2.0 * math.pi))
    return cdf_vals + values * pdf_vals


def spread_offsets(per_offset, q_rows, seq_len):
    span_len = seq_len + q_rows - 1
    tiled_rows = jnp.tile(per_offset, (1, q_rows))
    tiled_rows = jnp.pad(tiled_rows, ((0, 0), (0, q_rows)))
    shaped = tiled_rows.reshape(per_offset.shape[0], q_rows, span_len + 1)[:, :, :seq_len]
    return shaped[:, ::-1, :]


def diagonal_sums(block_vals, q_rows, seq_len):
    span_len = seq_len + q_rows - 1
    heads_here = block_vals.shape[0]
    flipped = block_vals[:, ::-1, :]
    padded = jnp.pad(flipped, ((0, 0), (0, 0), (0, q_rows)))
    flat_vals = padded.reshape(heads_here, q_rows * (span_len + 1))[:, : q_rows * span_len]
    return jnp.sum(flat_vals.reshape(heads_here, q_rows, span_len), axis=1)


def dot(a, b, ca, cb):
    return lax.dot_general(a, b, (((ca,), (cb,)), ((), ())), preferred_element_type=f32)


def swap_cores(values):
    return lax.ppermute(values, "col", [(0, 1), (1, 0)])


def make_per_device(mesh):
    n_ex, n_row = mesh.shape["ex"], mesh.shape["row"]
    groups = n_ex * n_row

    def gather_groups(shard):
        rows, width = shard.shape
        part = lax.all_gather(shard, "ex", axis=0)
        part = jnp.broadcast_to(part[None], (n_row, n_ex, rows, width))
        part = lax.all_to_all(part, "row", split_axis=0, concat_axis=0, tiled=True)
        return part.transpose(1, 0, 2, 3).reshape(groups * rows, width)

    def scatter_groups(terms):
        _, rows, width = terms.shape
        part = terms.reshape(n_ex, n_row, rows, width).transpose(1, 0, 2, 3)
        part = lax.all_to_all(part, "row", split_axis=0, concat_axis=0, tiled=True)
        part = jnp.sum(part.astype(f32), axis=0).astype(bf16)
        part = lax.all_to_all(part, "ex", split_axis=0, concat_axis=0, tiled=True)
        return jnp.sum(part.astype(f32), axis=0)

    def per_device(
        x_in,
        gain_attn,
        w_qkv,
        rel_bias,
        w_out,
        gain_ffn,
        w_router,
        w_up,
        w_down,
        seg_ids,
        expert_ids,
        slot_ids,
        drop_flags,
        d_out,
    ):
        seq_len, width = x_in.shape
        heads_here = rel_bias.shape[1]
        inner = w_qkv.shape[2]
        own_rows = w_qkv.shape[1]
        experts = w_router.shape[1]
        capacity = 5 * seq_len // (4 * experts)
        slots = -(-capacity // 8) * 8
        slot_total = experts * slots
        half = d_out.shape[1]
        col_at = lax.axis_index("col")
        expert_at = lax.axis_index("ex") * n_row + lax.axis_index("row")

        packed = jnp.concatenate(
            [
                w_qkv.astype(bf16).transpose(1, 0, 2).reshape(own_rows, 3 * inner),
                w_out.astype(bf16).T,
                w_router.astype(bf16),
            ],
            axis=1,
        )
        full = gather_groups(packed)
        qkv_w = full[:, : 3 * inner]
        out_wt = full[:, 3 * inner : 4 * inner]
        router_w = full[:, 4 * inner :]

        x_float = x_in.astype(f32)
        scale_one = rms_scale(x_float)
        normed_one = x_float * scale_one
        h_one = (normed_one * gain_attn).astype(bf16)
        qkv = dot(h_one, qkv_w, 1, 0).astype(bf16)
        split = lambda v: v.reshape(seq_len, heads_here, HEAD)
        queries, keys, values = (split(qkv[:, i * inner : (i + 1) * inner]) for i in range(3))
        doc_ids = seg_ids[0]
        offsets = jnp.arange(2 * seq_len - 1, dtype=jnp.int32) - (seq_len - 1)
        offset_hot = (
            bucket_of(offsets)[:, None] == jnp.arange(BUCKETS, dtype=jnp.int32)[None, :]
        ).astype(f32)
        per_offset = jnp.einsum("bh,ob->ho", rel_bias, offset_hot, precision=highest)
        same_doc = (doc_ids[:, None] == doc_ids[None, :])[None]
        scores = jnp.einsum("qhe,khe->hqk", queries, keys, preferred_element_type=f32) * 0.125
        scores = scores + spread_offsets(per_offset, seq_len, seq_len)
        scores = jnp.where(same_doc, scores, -1e30)
        peak = jnp.max(scores, axis=-1, keepdims=True)
        expo = jnp.exp(scores - peak)
        probs = expo / jnp.sum(expo, axis=-1, keepdims=True)
        probs_b = probs.astype(bf16)
        context = (
            jnp.einsum("hqk,khe->qhe", probs_b, values, preferred_element_type=f32)
            .reshape(seq_len, inner)
            .astype(bf16)
        )
        attn_part = dot(context, out_wt, 1, 1).astype(bf16)
        attn_out = attn_part.astype(f32) + swap_cores(attn_part).astype(f32)
        x_one = x_float + attn_out
        scale_two = rms_scale(x_one)
        normed_two = x_one * scale_two
        h_two = (normed_two * gain_ffn).astype(bf16)

        slot_of = jnp.where(drop_flags == 1, slot_total, expert_ids * slots + slot_ids)
        place = (slot_of[:, None] == jnp.arange(slot_total, dtype=jnp.int32)[None, :]).astype(bf16)
        mine = lambda v: jnp.where(col_at == 0, v[:, :half], v[:, half:])
        other = lambda v: jnp.where(col_at == 0, v[:, half:], v[:, :half])
        send = dot(place, jnp.concatenate([mine(h_two), d_out], axis=1), 0, 0).astype(bf16)
        got = lax.all_to_all(
            send.reshape(experts, slots, 2 * half), ("ex", "row"), 0, 0, tiled=True
        ).reshape(slot_total, 2 * half)
        both = lax.all_gather(got, "col", axis=0)
        rows = jnp.concatenate([both[0, :, :half], both[1, :, :half]], axis=1)
        g_rows = jnp.concatenate([both[0, :, half:], both[1, :, half:]], axis=1)

        up_w = w_up[0].astype(bf16)
        down_w = w_down[0].astype(bf16)
        router_probs = jax.nn.softmax(dot(rows, router_w, 1, 0), axis=-1)
        chosen = (jnp.arange(experts, dtype=jnp.int32) == expert_at).astype(f32)[None, :]
        gate = jnp.sum(router_probs * chosen, axis=-1, keepdims=True)
        d_y = (g_rows.astype(f32) * gate).astype(bf16)
        pre_act = dot(rows, up_w, 1, 0)
        act_b = jax.nn.gelu(pre_act, approximate=False).astype(bf16)
        y_part = dot(act_b, down_w, 1, 0)
        gate_part = jnp.sum(g_rows.astype(f32) * y_part, axis=-1, keepdims=True)
        d_pre = (dot(d_y, down_w, 1, 1) * gelu_slope(pre_act)).astype(bf16)
        d_in_part = dot(d_pre, up_w, 1, 1)
        crossing = jnp.concatenate([other(y_part), other(d_in_part)], axis=1).astype(bf16)
        crossed = swap_cores(crossing).astype(f32)
        d_gate = gate_part + swap_cores(gate_part)
        d_logits = (d_gate * gate * (chosen - router_probs)).astype(bf16)
        d_router_in = dot(d_logits, router_w, 1, 1)
        y_gated = gate * (mine(y_part) + crossed[:, :half])
        d_in = mine(d_in_part) + crossed[:, half:] + mine(d_router_in)
        back = jnp.concatenate([y_gated, d_in], axis=1).astype(bf16)
        home = lax.all_to_all(
            back.reshape(experts, slots, 2 * half), ("ex", "row"), 0, 0, tiled=True
        ).reshape(slot_total, 2 * half)
        grad_down = dot(act_b, d_y, 0, 0)
        grad_up = dot(rows, d_pre, 0, 0)
        grad_router = dot(rows, d_logits, 0, 0)

        home_tok = dot(place, home, 1, 0)
        layer_out = (mine(x_one) + home_tok[:, :half]).astype(bf16)
        cross_back = jnp.concatenate([home_tok[:, half:].astype(bf16), d_out], axis=1)
        both_back = lax.all_gather(cross_back, "col", axis=0).astype(f32)
        d_h_two = jnp.concatenate([both_back[0, :, :half], both_back[1, :, :half]], axis=1)
        g_full = jnp.concatenate([both_back[0, :, half:], both_back[1, :, half:]], axis=1)

        grad_gain_ffn = jnp.sum(d_h_two * normed_two, axis=0)
        d_norm_two = d_h_two * gain_ffn
        d_x_one = g_full + scale_two * (
            d_norm_two - normed_two * jnp.mean(d_norm_two * normed_two, axis=-1, keepdims=True)
        )
        d_attn_b = d_x_one.astype(bf16)
        grad_out_t = dot(d_attn_b, context, 0, 0)
        d_context = split(dot(d_attn_b, out_wt, 1, 0).astype(bf16))
        d_probs = jnp.einsum("qhe,khe->hqk", d_context, values, preferred_element_type=f32)
        row_delta = jnp.sum(probs * d_probs, axis=-1, keepdims=True)
        d_scores = (probs * (d_probs - row_delta)).astype(bf16)
        d_vals = jnp.einsum("hqk,qhe->khe", probs_b, d_context, preferred_element_type=f32)
        d_keys = jnp.einsum("hqk,qhe->khe", d_scores, queries, preferred_element_type=f32) * 0.125
        d_quer = jnp.einsum("hqk,khe->qhe", d_scores, keys, preferred_element_type=f32) * 0.125
        d_qkv = jnp.concatenate(
            [v.reshape(seq_len, inner) for v in (d_quer, d_keys, d_vals)], axis=1
        ).astype(bf16)
        grad_offset = diagonal_sums(d_scores.astype(f32), seq_len, seq_len)
        grad_rel = jnp.einsum("ho,ob->bh", grad_offset, offset_hot, precision=highest)
        grad_qkv = dot(h_one, d_qkv, 0, 0)
        d_h_one_part = dot(d_qkv, qkv_w, 1, 1).astype(bf16)
        d_h_one = d_h_one_part.astype(f32) + swap_cores(d_h_one_part).astype(f32)
        grad_gain_attn = jnp.sum(d_h_one * normed_one, axis=0)
        d_norm_one = d_h_one * gain_attn
        grad_x = d_x_one + scale_one * (
            d_norm_one - normed_one * jnp.mean(d_norm_one * normed_one, axis=-1, keepdims=True)
        )

        terms = jnp.concatenate([grad_qkv, grad_out_t, grad_router], axis=1).astype(bf16)
        sums = scatter_groups(terms.reshape(groups, own_rows, 4 * inner + experts))
        small = jnp.concatenate([grad_gain_attn, grad_gain_ffn, grad_rel.reshape(-1)])[None]
        small = jnp.broadcast_to(small, (groups, small.shape[1]))
        small = jnp.sum(lax.all_to_all(small, ("ex", "row"), 0, 0, tiled=True), axis=0)
        return (
            layer_out,
            grad_x.astype(bf16),
            small[:width],
            sums[:, : 3 * inner].reshape(own_rows, 3, inner).transpose(1, 0, 2),
            small[2 * width :].reshape(BUCKETS, heads_here),
            sums[:, 3 * inner : 4 * inner].T,
            small[width : 2 * width],
            sums[:, 4 * inner :],
            grad_up[None],
            grad_down[None],
        )

    return per_device


def solution(mesh):
    return jax.shard_map(
        make_per_device(mesh),
        mesh=mesh,
        in_specs=(
            P(("ex", "row"), None),
            P(),
            P(None, ("ex", "row"), "col"),
            P(None, "col"),
            P("col", ("ex", "row")),
            P(),
            P(("ex", "row"), None),
            P(("ex", "row"), None, "col"),
            P(("ex", "row"), "col", None),
            P(("ex", "row"), None),
            P(("ex", "row")),
            P(("ex", "row")),
            P(("ex", "row")),
            P(("ex", "row"), "col"),
        ),
        out_specs=(
            P(("ex", "row"), "col"),
            P(("ex", "row"), None),
            P(),
            P(None, ("ex", "row"), "col"),
            P(None, "col"),
            P("col", ("ex", "row")),
            P(),
            P(("ex", "row"), None),
            P(("ex", "row"), None, "col"),
            P(("ex", "row"), "col", None),
        ),
        check_vma=False,
    )
```

```python
import functools
import math

import jax
import jax.numpy as jnp
from jax import lax
from jax.experimental import pallas as pl
from jax.experimental.pallas import tpu as pltpu
from jax.sharding import PartitionSpec as P

HEAD = 64
BUCKETS = 32

norm_eps = 1e-06
bucket_edges = (12, 16, 23, 32, 46, 64, 91)
highest = lax.Precision.HIGHEST
bf16 = jnp.bfloat16
f32 = jnp.float32

GATHER_ORDER = tuple(((k, m),) for m in range(4) for k in range(4))
SCATTER_ORDER = (
    ((0, 0), (1, 0), (2, 0), (3, 0)),
    ((0, 1), (1, 1)),
    ((2, 1), (3, 1)),
    ((0, 2), (1, 2)),
    ((2, 2), (3, 2)),
    ((0, 3), (1, 3)),
    ((2, 3), (3, 3)),
)


def bucket_of(offset):
    distance = jnp.abs(offset)
    far_part = jnp.zeros(distance.shape, jnp.int32)
    for edge_at in bucket_edges:
        far_part = far_part + (distance >= edge_at).astype(jnp.int32)
    inside = jnp.where(distance < 8, distance, far_part + jnp.int32(8))
    upper = jnp.where(offset > 0, jnp.int32(BUCKETS // 2), jnp.int32(0))
    return inside + upper


def rms_scale(values):
    return lax.rsqrt(jnp.mean(values * values, axis=-1, keepdims=True) + norm_eps)


def dot(a, b, ca, cb):
    return lax.dot_general(a, b, (((ca,), (cb,)), ((), ())), preferred_element_type=f32)


def swap_cores(values):
    return lax.ppermute(values, "col", [(0, 1), (1, 0)])


def shape(dims, dtype):
    return jax.ShapeDtypeStruct(tuple(dims), dtype)


def vmem_call(kernel, out_shape, flops, *args, scalars=(), scratch=(), limit=12):
    nbytes = sum(math.prod(v.shape) * v.dtype.itemsize for v in (*args, *out_shape))
    spec = pl.BlockSpec(memory_space=pltpu.VMEM)
    limit = limit if nbytes < 16 * 2**20 else 48
    return pl.pallas_call(
        kernel,
        out_shape=out_shape,
        in_specs=[pl.BlockSpec(memory_space=pltpu.SMEM)] * len(scalars) + [spec] * len(args),
        out_specs=[spec] * len(out_shape),
        scratch_shapes=scratch,
        compiler_params=pltpu.CompilerParams(vmem_limit_bytes=limit * 2**20),
        cost_estimate=pl.CostEstimate(flops=flops, bytes_accessed=nbytes, transcendentals=0),
    )(*scalars, *args)


def block_rows(at_ref, order, count):
    if order is None:
        return [pl.ds(0, count)]
    ex_at, row_at = at_ref[0], at_ref[1]
    return [
        pl.ds(pl.multiple_of(((ex_at ^ k) * 4 + (row_at ^ m)) * count, 16), count)
        for part in order
        for k, m in part
    ]


def take_blocks(at_ref, order, full_ref, block_refs):
    rows = iter(block_rows(at_ref, order, block_refs[0].shape[1]))
    for block_ref in block_refs:
        for i in range(block_ref.shape[0]):
            block_ref[i] = full_ref[next(rows), :]


def eye(size):
    dims = (size, size)
    same = lax.broadcasted_iota(jnp.int32, dims, 0) == lax.broadcasted_iota(jnp.int32, dims, 1)
    return same.astype(bf16)


def pack_weights(qkv_ref, out_ref, router_ref, packed_ref):
    inner, experts = qkv_ref.shape[2], router_ref.shape[1]
    for part in range(3):
        packed_ref[:, part * inner : (part + 1) * inner] = qkv_ref[part].astype(bf16)
    turned = dot(out_ref[...].astype(bf16), eye(inner), 0, 0)
    packed_ref[:, 3 * inner : 4 * inner] = turned.astype(bf16)
    packed_ref[:, 4 * inner :] = jnp.zeros((packed_ref.shape[0], packed_ref.shape[1] - 4 * inner), bf16)
    packed_ref[:, 4 * inner : 4 * inner + experts] = router_ref[...].astype(bf16)


def attend_forward(order, at_ref, x_ref, gain_ref, offset_ref, seg_ref, *refs):
    *block_refs, part_ref, h_ref, qkv_ref, probs_ref, ctx_ref, w_ref, out_w_ref, router_ref = refs
    seq_len = x_ref.shape[0]
    heads, inner = probs_ref.shape[0], ctx_ref.shape[1]
    for rows, block_ref in zip(block_rows(at_ref, order, block_refs[0].shape[0]), block_refs):
        w_ref[rows, :] = block_ref[:, : 3 * inner]
        out_w_ref[rows, :] = block_ref[:, 3 * inner : 4 * inner]
        router_ref[rows, :] = block_ref[:, 4 * inner :]
    x_float = x_ref[...].astype(f32)
    h_one = (x_float * rms_scale(x_float) * gain_ref[...]).astype(bf16)
    h_ref[...] = h_one
    documents = lax.broadcasted_iota(jnp.int32, (8, seq_len), 0) == seg_ref[...]
    same_doc = dot(documents.astype(bf16), documents.astype(bf16), 0, 0) > 0.5
    qkv_ref[...] = dot(h_one, w_ref[...], 1, 0).astype(bf16)
    span = offset_ref.shape[1]
    for at in range(heads):
        take = lambda part: qkv_ref[:, part * inner + at * HEAD : part * inner + (at + 1) * HEAD]
        spread = jnp.broadcast_to(offset_ref[at : at + 1, :], (seq_len, span))
        bias = pltpu.roll(spread, span - seq_len + 1, 1, stride=1, stride_axis=0)[:, :seq_len]
        scores = jnp.where(same_doc, dot(take(0), take(1), 1, 1) * 0.125 + bias, -1e30)
        expo = jnp.exp(scores - jnp.max(scores, axis=1, keepdims=True))
        probs = expo / jnp.sum(expo, axis=1, keepdims=True)
        probs_ref[at] = probs
        ctx = dot(probs.astype(bf16), take(2), 1, 0)
        ctx_ref[:, at * HEAD : (at + 1) * HEAD] = ctx.astype(bf16)
    part_ref[...] = dot(ctx_ref[...], out_w_ref[...], 1, 1).astype(bf16)


def dispatch(at_ref, x_ref, part_ref, peer_ref, gain_ref, slot_ref, g_ref, send_ref):
    half = g_ref.shape[1]
    x_one = x_ref[...].astype(f32) + (part_ref[...].astype(f32) + peer_ref[...].astype(f32))
    h_two = (x_one * rms_scale(x_one) * gain_ref[...]).astype(bf16)
    mine = jnp.where(at_ref[2] == 0, h_two[:, :half], h_two[:, half:])
    dims = (send_ref.shape[0], x_ref.shape[0])
    place = (lax.broadcasted_iota(jnp.int32, dims, 0) == slot_ref[...]).astype(bf16)
    send_ref[:, :half] = dot(place, mine, 1, 0).astype(bf16)
    send_ref[:, half:] = dot(place, g_ref[...], 1, 0).astype(bf16)


def run_expert(
    experts, row_size, at_ref, got_ref, peer_ref, router_ref, up_ref, down_ref,
    cross_ref, mine_ref, probs_ref, gate_part_ref, rows_ref, d_y_ref, act_ref, d_pre_ref, d_in_ref,
):
    half = got_ref.shape[1] // 2
    hidden = up_ref.shape[1]
    first_core = at_ref[2] == 0
    for at, refs in ((0, (got_ref, peer_ref)), (1, (peer_ref, got_ref))):
        pick = lambda lo: jnp.where(first_core, refs[0][:, lo : lo + half], refs[1][:, lo : lo + half])
        rows_ref[:, at * half : (at + 1) * half] = pick(0)
        d_y_ref[:, at * half : (at + 1) * half] = pick(half)
    rows, g_rows = rows_ref[...], d_y_ref[...].astype(f32)
    logits = dot(rows, router_ref[...], 1, 0)[:, :experts]
    expo = jnp.exp(logits - jnp.max(logits, axis=1, keepdims=True))
    probs = expo / jnp.sum(expo, axis=1, keepdims=True)
    probs_ref[...] = probs
    expert_at = at_ref[0] * row_size + at_ref[1]
    chosen = lax.broadcasted_iota(jnp.int32, probs.shape, 1) == expert_at
    gate = jnp.sum(jnp.where(chosen, probs, 0.0), axis=1, keepdims=True)
    d_y_ref[...] = (g_rows * gate).astype(bf16)
    step = 512 if hidden % 512 == 0 else hidden
    y_part = None
    for lo in range(0, hidden, step):
        cols = pl.ds(lo, step)
        pre_act = dot(rows_ref[...], up_ref[:, cols], 1, 0)
        cdf = 0.5 * (1.0 + lax.erf(pre_act * (1.0 / math.sqrt(2.0))))
        pdf = jnp.exp(-0.5 * pre_act * pre_act) * (1.0 / math.sqrt(2.0 * math.pi))
        act = (pre_act * cdf).astype(bf16)
        act_ref[:, cols] = act
        y_more = dot(act, down_ref[cols, :], 1, 0)
        d_pre = (dot(d_y_ref[...], down_ref[cols, :], 1, 1) * (cdf + pre_act * pdf)).astype(bf16)
        d_pre_ref[:, cols] = d_pre
        d_more = dot(d_pre, up_ref[:, cols], 1, 1)
        if lo == 0:
            y_part = y_more
            d_in_ref[...] = d_more
        else:
            y_part = y_part + y_more
            d_in_ref[...] += d_more
    gate_part_ref[...] = jnp.sum(g_rows * y_part, axis=1, keepdims=True)
    d_in = d_in_ref[...]
    mine_ref[:, :half] = jnp.where(first_core, y_part[:, :half], y_part[:, half:])
    mine_ref[:, half:] = jnp.where(first_core, d_in[:, :half], d_in[:, half:])
    cross_ref[:, :half] = jnp.where(first_core, y_part[:, half:], y_part[:, :half]).astype(bf16)
    cross_ref[:, half:] = jnp.where(first_core, d_in[:, half:], d_in[:, :half]).astype(bf16)


def settle(
    row_size, at_ref, mine_ref, crossed_ref, probs_ref, gate_part_ref, gate_peer_ref, router_ref,
    back_ref, d_logits_ref,
):
    half = mine_ref.shape[1] // 2
    probs = probs_ref[...]
    expert_at = at_ref[0] * row_size + at_ref[1]
    chosen = (lax.broadcasted_iota(jnp.int32, probs.shape, 1) == expert_at).astype(f32)
    gate = jnp.sum(probs * chosen, axis=1, keepdims=True)
    d_gate = gate_part_ref[...] + gate_peer_ref[...]
    d_logits = (d_gate * gate * (chosen - probs)).astype(bf16)
    d_logits_ref[...] = d_logits
    router_w = router_ref[...][:, : probs.shape[1]]
    router_mine = jnp.where(at_ref[2] == 0, router_w[:half], router_w[half:])
    back_ref[:, :half] = (gate * (mine_ref[:, :half] + crossed_ref[:, :half].astype(f32))).astype(bf16)
    d_in = mine_ref[:, half:] + crossed_ref[:, half:].astype(f32)
    back_ref[:, half:] = (d_in + dot(d_logits, router_mine, 1, 1)).astype(bf16)


def come_home(
    order, at_ref, home_ref, peer_ref, slot_ref, x_ref, part_ref, part_peer_ref, g_ref, g_peer_ref,
    gain_ref, out_w_ref, ctx_ref, router_ref, layer_ref, d_x_ref, gain_grad_ref, d_ctx_ref, *refs,
):
    *block_refs, grads_ref = refs
    half = g_ref.shape[1]
    inner = ctx_ref.shape[1]
    first_core = at_ref[2] == 0
    both = lambda a, b: jnp.concatenate(
        [jnp.where(first_core, a, b), jnp.where(first_core, b, a)], axis=1
    )
    dims = (home_ref.shape[0], x_ref.shape[0])
    place = (lax.broadcasted_iota(jnp.int32, dims, 0) == slot_ref[...]).astype(bf16)
    d_h = both(dot(place, home_ref[:, half:], 0, 0), dot(place, peer_ref[...], 0, 0))
    x_one = x_ref[...].astype(f32) + (part_ref[...].astype(f32) + part_peer_ref[...].astype(f32))
    g_full = both(g_ref[...], g_peer_ref[...]).astype(f32)
    scale = rms_scale(x_one)
    normed = x_one * scale
    gain_grad_ref[...] = jnp.sum(d_h * normed, axis=0, keepdims=True)
    d_norm = d_h * gain_ref[...]
    d_x = g_full + scale * (d_norm - normed * jnp.mean(d_norm * normed, axis=-1, keepdims=True))
    d_x_ref[...] = d_x
    d_x_b = d_x.astype(bf16)
    d_ctx_ref[...] = dot(d_x_b, out_w_ref[...], 1, 0).astype(bf16)
    grads_ref[:, :inner] = dot(d_x_b, ctx_ref[...], 0, 0).astype(bf16)
    grads_ref[:, inner:] = router_ref[...].astype(bf16)
    take_blocks(at_ref, order, grads_ref, block_refs)
    y_home = dot(place, home_ref[:, :half], 0, 0)
    x_mine = jnp.where(first_core, x_one[:, :half], x_one[:, half:])
    layer_ref[...] = (x_mine + y_home).astype(bf16)


def attend_backward(order, at_ref, d_ctx_ref, qkv_ref, probs_ref, h_ref, w_ref, d_h_ref, grad_offset_ref, *refs):
    *block_refs, d_qkv_ref, grads_ref = refs
    heads, seq_len, _ = probs_ref.shape
    inner = d_ctx_ref.shape[1]
    span = grad_offset_ref.shape[1]
    flip = (
        lax.broadcasted_iota(jnp.int32, (seq_len, seq_len), 0)
        + lax.broadcasted_iota(jnp.int32, (seq_len, seq_len), 1)
        == seq_len - 1
    ).astype(bf16)
    for at in range(heads):
        cols = lambda part: pl.ds(part * inner + at * HEAD, HEAD)
        d_ctx = d_ctx_ref[:, at * HEAD : (at + 1) * HEAD]
        probs = probs_ref[at]
        d_probs = dot(d_ctx, qkv_ref[:, cols(2)], 1, 1)
        row_delta = jnp.sum(probs * d_probs, axis=1, keepdims=True)
        d_scores = (probs * (d_probs - row_delta)).astype(bf16)
        d_qkv_ref[:, cols(0)] = (dot(d_scores, qkv_ref[:, cols(1)], 1, 0) * 0.125).astype(bf16)
        d_qkv_ref[:, cols(1)] = (dot(d_scores, qkv_ref[:, cols(0)], 0, 0) * 0.125).astype(bf16)
        d_qkv_ref[:, cols(2)] = dot(probs.astype(bf16), d_ctx, 0, 0).astype(bf16)
        turned = jnp.concatenate(
            [dot(flip, d_scores, 1, 0), jnp.zeros((seq_len, span - seq_len), f32)], axis=1
        )
        lined = pltpu.roll(turned, 0, 1, stride=1, stride_axis=0)
        grad_offset_ref[at : at + 1, :] = jnp.sum(lined, axis=0, keepdims=True)
    grads_ref[...] = dot(h_ref[...], d_qkv_ref[...], 0, 0).astype(bf16)
    take_blocks(at_ref, order, grads_ref, block_refs)
    d_h_ref[...] = dot(d_qkv_ref[...], w_ref[...], 1, 1).astype(bf16)


def experts_pad(experts):
    return -(-experts // 128) * 128


def make_per_device(mesh):
    n_ex, n_row = mesh.shape["ex"], mesh.shape["row"]
    groups = n_ex * n_row

    def hop(values, axis, step):
        return lax.ppermute(values, axis, [(i, i ^ step) for i in range(mesh.shape[axis])])

    def whole_cube(rows):
        return n_ex == 4 and n_row == 4 and rows % 16 == 0

    def gather_blocks(shard):
        rows, width = shard.shape
        if whole_cube(rows):
            line = [shard] + [hop(shard, "ex", k) for k in (1, 2, 3)]
            xs = [hop(part, "row", 1) for part in line]
            ys = [hop(part, "row", 2) for part in line]
            diagonal = [
                hop(ys[k], "row", 1) if k % 2 else hop(xs[k], "row", 2) for k in range(4)
            ]
            return [*line, *xs, *ys, *diagonal]
        part = lax.all_gather(shard, "ex", axis=0)
        part = jnp.broadcast_to(part[None], (n_row, n_ex, rows, width))
        part = lax.all_to_all(part, "row", split_axis=0, concat_axis=0, tiled=True)
        return [part.transpose(1, 0, 2, 3).reshape(groups * rows, width)]

    def block_shapes(rows, width):
        if whole_cube(rows):
            return [shape((len(part), rows, width), bf16) for part in SCATTER_ORDER]
        return [shape((1, groups * rows, width), bf16)]

    def scatter_blocks(parts, rows):
        if whole_cube(rows):
            here, x_low, x_high, y_low, y_high, d_low, d_high = parts
            from_x, from_y = hop(d_low, "row", 1), hop(d_high, "row", 2)
            x_first, y_first = hop(x_low, "row", 1), hop(y_high, "row", 2)
            x_last = hop(x_high + from_y, "row", 1)
            y_last = hop(y_low + from_x, "row", 2)
            low = here[:2].astype(f32) + x_first.astype(f32) + y_last.astype(f32)
            high = here[2:].astype(f32) + y_first.astype(f32) + x_last.astype(f32)
            return (
                low[0]
                + hop(low[1].astype(bf16), "ex", 1).astype(f32)
                + hop(high[0].astype(bf16), "ex", 2).astype(f32)
                + hop(high[1].astype(bf16), "ex", 3).astype(f32)
            )
        part = parts[0].reshape(n_ex, n_row, rows, -1).transpose(1, 0, 2, 3)
        part = lax.all_to_all(part, "row", split_axis=0, concat_axis=0, tiled=True)
        part = jnp.sum(part.astype(f32), axis=0).astype(bf16)
        part = lax.all_to_all(part, "ex", split_axis=0, concat_axis=0, tiled=True)
        return jnp.sum(part.astype(f32), axis=0)

    def sum_groups(values):
        for axis in ("row", "ex"):
            step = 1
            while step < mesh.shape[axis]:
                values = values + hop(values, axis, step)
                step *= 2
        return values

    def per_device(
        x_in,
        gain_attn,
        w_qkv,
        rel_bias,
        w_out,
        gain_ffn,
        w_router,
        w_up,
        w_down,
        seg_ids,
        expert_ids,
        slot_ids,
        drop_flags,
        d_out,
    ):
        seq_len, width = x_in.shape
        heads_here = rel_bias.shape[1]
        inner = w_qkv.shape[2]
        own_rows = w_qkv.shape[1]
        experts = w_router.shape[1]
        wide = inner + experts_pad(experts)
        capacity = 5 * seq_len // (4 * experts)
        slots = -(-capacity // 8) * 8
        slot_total = experts * slots
        half = d_out.shape[1]
        hidden = w_up.shape[2]
        device_at = jnp.stack([lax.axis_index(axis).astype(jnp.int32) for axis in ("ex", "row", "col")])
        device_at, w_qkv = lax.optimization_barrier((device_at, w_qkv))
        gather_order = GATHER_ORDER if whole_cube(own_rows) else None
        scatter_order = SCATTER_ORDER if whole_cube(own_rows) else None

        (packed,) = vmem_call(
            pack_weights,
            (shape((own_rows, 3 * inner + wide), bf16),),
            0,
            w_qkv,
            w_out,
            w_router,
        )
        blocks = gather_blocks(packed)
        up_w = w_up[0].astype(bf16)
        down_w = w_down[0].astype(bf16)
        *blocks, up_w, down_w = lax.optimization_barrier((*blocks, up_w, down_w))
        g_peer = swap_cores(d_out)

        span = 2 * seq_len
        offsets = jnp.arange(span, dtype=jnp.int32) - (seq_len - 1)
        offset_hot = (
            bucket_of(offsets)[:, None] == jnp.arange(BUCKETS, dtype=jnp.int32)[None, :]
        ).astype(f32)
        per_offset = jnp.einsum("bh,ob->ho", rel_bias, offset_hot, precision=highest)
        square = seq_len * seq_len * heads_here * HEAD
        attn_part, h_one, qkv, probs, context, qkv_w, out_w, router_w = vmem_call(
            functools.partial(attend_forward, gather_order),
            (
                shape((seq_len, width), bf16),
                shape((seq_len, width), bf16),
                shape((seq_len, 3 * inner), bf16),
                shape((heads_here, seq_len, seq_len), f32),
                shape((seq_len, inner), bf16),
                shape((width, 3 * inner), bf16),
                shape((width, inner), bf16),
                shape((width, wide - inner), bf16),
            ),
            8 * seq_len * width * inner + 4 * square,
            x_in,
            gain_attn[None],
            per_offset,
            seg_ids,
            *blocks,
            scalars=(device_at,),
        )
        attn_peer = swap_cores(attn_part)
        slot_of = jnp.where(drop_flags == 1, slot_total, expert_ids * slots + slot_ids)[None]
        (send,) = vmem_call(
            dispatch,
            (shape((slot_total, width), bf16),),
            2 * seq_len * slot_total * width,
            x_in,
            attn_part,
            attn_peer,
            gain_ffn[None],
            slot_of,
            d_out,
            scalars=(device_at,),
        )
        got = lax.all_to_all(
            send.reshape(experts, slots, width), ("ex", "row"), 0, 0, tiled=True
        ).reshape(slot_total, width)
        crossing, mine, router_probs, gate_part, rows, d_y, act_b, d_pre = vmem_call(
            functools.partial(run_expert, experts, n_row),
            (
                shape((slot_total, width), bf16),
                shape((slot_total, width), f32),
                shape((slot_total, experts), f32),
                shape((slot_total, 1), f32),
                shape((slot_total, width), bf16),
                shape((slot_total, width), bf16),
                shape((slot_total, hidden), bf16),
                shape((slot_total, hidden), bf16),
            ),
            8 * slot_total * width * hidden,
            got,
            swap_cores(got),
            router_w,
            up_w,
            down_w,
            scalars=(device_at,),
            scratch=(pltpu.VMEM((slot_total, width), f32),),
        )
        back, d_logits = vmem_call(
            functools.partial(settle, n_row),
            (shape((slot_total, width), bf16), shape((slot_total, experts), bf16)),
            2 * slot_total * half * experts,
            mine,
            swap_cores(crossing),
            router_probs,
            gate_part,
            swap_cores(gate_part),
            router_w,
            scalars=(device_at,),
        )
        home = lax.all_to_all(
            back.reshape(experts, slots, width), ("ex", "row"), 0, 0, tiled=True
        ).reshape(slot_total, width)
        grad_down = dot(act_b, d_y, 0, 0)
        grad_up = dot(rows, d_pre, 0, 0)
        grad_router = jnp.pad(dot(rows, d_logits, 0, 0), ((0, 0), (0, wide - inner - experts)))
        home, grad_down, grad_up = lax.optimization_barrier((home, grad_down, grad_up))

        layer_out, d_x_one, grad_gain_ffn, d_context, *out_terms = vmem_call(
            functools.partial(come_home, scatter_order),
            (
                shape((seq_len, half), bf16),
                shape((seq_len, width), f32),
                shape((1, width), f32),
                shape((seq_len, inner), bf16),
                *block_shapes(own_rows, wide),
            ),
            2 * seq_len * (slot_total * 3 * half + 2 * width * inner),
            home,
            swap_cores(home[:, half:]),
            slot_of,
            x_in,
            attn_part,
            attn_peer,
            d_out,
            g_peer,
            gain_ffn[None],
            out_w,
            context,
            grad_router,
            scalars=(device_at,),
            scratch=(pltpu.VMEM((width, wide), bf16),),
        )
        out_sums = scatter_blocks(out_terms, own_rows)
        d_h_part, grad_offset, *qkv_terms = vmem_call(
            functools.partial(attend_backward, scatter_order),
            (
                shape((seq_len, width), bf16),
                shape((heads_here, span), f32),
                *block_shapes(own_rows, 3 * inner),
            ),
            12 * seq_len * width * inner + 10 * square,
            d_context,
            qkv,
            probs,
            h_one,
            qkv_w,
            scalars=(device_at,),
            scratch=(
                pltpu.VMEM((seq_len, 3 * inner), bf16),
                pltpu.VMEM((width, 3 * inner), bf16),
            ),
        )
        qkv_sums = scatter_blocks(qkv_terms, own_rows)
        grad_rel = jnp.einsum("ho,ob->bh", grad_offset, offset_hot, precision=highest)
        d_h_one = d_h_part.astype(f32) + swap_cores(d_h_part).astype(f32)
        x_float = x_in.astype(f32)
        scale_one = rms_scale(x_float)
        normed_one = x_float * scale_one
        grad_gain_attn = jnp.sum(d_h_one * normed_one, axis=0)
        d_norm_one = d_h_one * gain_attn
        grad_x = d_x_one + scale_one * (
            d_norm_one - normed_one * jnp.mean(d_norm_one * normed_one, axis=-1, keepdims=True)
        )
        small = sum_groups(
            jnp.concatenate([grad_gain_attn, grad_gain_ffn[0], grad_rel.reshape(-1)])
        )
        return (
            layer_out,
            grad_x.astype(bf16),
            small[:width],
            qkv_sums.reshape(own_rows, 3, inner).transpose(1, 0, 2),
            small[2 * width :].reshape(BUCKETS, heads_here),
            out_sums[:, :inner].T,
            small[width : 2 * width],
            out_sums[:, inner : inner + experts],
            grad_up[None],
            grad_down[None],
        )

    return per_device


def solution(mesh):
    return jax.shard_map(
        make_per_device(mesh),
        mesh=mesh,
        in_specs=(
            P(("ex", "row"), None),
            P(),
            P(None, ("ex", "row"), "col"),
            P(None, "col"),
            P("col", ("ex", "row")),
            P(),
            P(("ex", "row"), None),
            P(("ex", "row"), None, "col"),
            P(("ex", "row"), "col", None),
            P(("ex", "row"), None),
            P(("ex", "row")),
            P(("ex", "row")),
            P(("ex", "row")),
            P(("ex", "row"), "col"),
        ),
        out_specs=(
            P(("ex", "row"), "col"),
            P(("ex", "row"), None),
            P(),
            P(None, ("ex", "row"), "col"),
            P(None, "col"),
            P("col", ("ex", "row")),
            P(),
            P(("ex", "row"), None),
            P(("ex", "row"), None, "col"),
            P(("ex", "row"), "col", None),
        ),
        check_vma=False,
    )
```

```python
import functools
import math

import jax
import jax.numpy as jnp
from jax import lax
from jax.experimental import pallas as pl
from jax.experimental.pallas import tpu as pltpu
from jax.sharding import PartitionSpec as P

HEAD = 64
BUCKETS = 32

norm_eps = 1e-06
bucket_edges = (12, 16, 23, 32, 46, 64, 91)
highest = lax.Precision.HIGHEST
bf16 = jnp.bfloat16
f32 = jnp.float32

GATHER_ORDER = tuple(((k, m),) for m in range(4) for k in range(4))

def bucket_of(offset):
    distance = jnp.abs(offset)
    far_part = jnp.zeros(distance.shape, jnp.int32)
    for edge_at in bucket_edges:
        far_part = far_part + (distance >= edge_at).astype(jnp.int32)
    inside = jnp.where(distance < 8, distance, far_part + jnp.int32(8))
    upper = jnp.where(offset > 0, jnp.int32(BUCKETS // 2), jnp.int32(0))
    return inside + upper


def rms_scale(values):
    return lax.rsqrt(jnp.mean(values * values, axis=-1, keepdims=True) + norm_eps)


def dot(a, b, ca, cb):
    return lax.dot_general(a, b, (((ca,), (cb,)), ((), ())), preferred_element_type=f32)


def swap_cores(values):
    return lax.ppermute(values, "col", [(0, 1), (1, 0)])


def shape(dims, dtype):
    return jax.ShapeDtypeStruct(tuple(dims), dtype)


def vmem_call(kernel, out_shape, flops, *args, scalars=(), scratch=(), limit=12):
    nbytes = sum(math.prod(v.shape) * v.dtype.itemsize for v in (*args, *out_shape))
    spec = pl.BlockSpec(memory_space=pltpu.VMEM)
    limit = limit if nbytes < 16 * 2**20 else 48
    return pl.pallas_call(
        kernel,
        out_shape=out_shape,
        in_specs=[pl.BlockSpec(memory_space=pltpu.SMEM)] * len(scalars) + [spec] * len(args),
        out_specs=[spec] * len(out_shape),
        scratch_shapes=scratch,
        compiler_params=pltpu.CompilerParams(vmem_limit_bytes=limit * 2**20),
        cost_estimate=pl.CostEstimate(flops=flops, bytes_accessed=nbytes, transcendentals=0),
    )(*scalars, *args)


def block_rows(at_ref, order, count):
    if order is None:
        return [pl.ds(0, count)]
    ex_at, row_at = at_ref[0], at_ref[1]
    return [
        pl.ds(pl.multiple_of(((ex_at ^ k) * 4 + (row_at ^ m)) * count, 16), count)
        for part in order
        for k, m in part
    ]


def eye(size):
    dims = (size, size)
    same = lax.broadcasted_iota(jnp.int32, dims, 0) == lax.broadcasted_iota(jnp.int32, dims, 1)
    return same.astype(bf16)


def pack_weights(qkv_ref, out_turned_ref, router_turned_ref, packed_ref):
    inner, experts = qkv_ref.shape[2], router_turned_ref.shape[0]
    for part in range(3):
        packed_ref[:, part * inner : (part + 1) * inner] = qkv_ref[part].astype(bf16)
    packed_ref[:, 3 * inner : 4 * inner] = out_turned_ref[...].astype(bf16)
    packed_ref[:, 4 * inner :] = jnp.zeros((packed_ref.shape[0], packed_ref.shape[1] - 4 * inner), bf16)
    router = dot(router_turned_ref[...].astype(bf16), eye(experts), 0, 0)
    packed_ref[:, 4 * inner : 4 * inner + experts] = router.astype(bf16)


def turn_normed(at_ref, x_ref, gain_ref, turned_ref, mine_ref):
    x_float = x_ref[...].astype(f32)
    h_one = (x_float * rms_scale(x_float) * gain_ref[...]).astype(bf16)
    turned_ref[...] = dot(h_one, eye(h_one.shape[0]), 0, 0).astype(bf16)
    half = mine_ref.shape[0]
    mine_ref[...] = jnp.where(at_ref[2] == 0, turned_ref[:half, :], turned_ref[half:, :])


def attend_forward(order, at_ref, x_ref, gain_ref, offset_ref, seg_ref, *refs):
    *block_refs, part_ref, qkv_ref, probs_ref, ctx_ref, w_ref, out_w_ref, router_ref = refs
    seq_len = x_ref.shape[0]
    heads, inner = probs_ref.shape[0], ctx_ref.shape[1]
    for rows, block_ref in zip(block_rows(at_ref, order, block_refs[0].shape[0]), block_refs):
        w_ref[rows, :] = block_ref[:, : 3 * inner]
        out_w_ref[rows, :] = block_ref[:, 3 * inner : 4 * inner]
        router_ref[rows, :] = block_ref[:, 4 * inner :]
    x_float = x_ref[...].astype(f32)
    h_one = (x_float * rms_scale(x_float) * gain_ref[...]).astype(bf16)
    documents = lax.broadcasted_iota(jnp.int32, (8, seq_len), 0) == seg_ref[...]
    same_doc = dot(documents.astype(bf16), documents.astype(bf16), 0, 0) > 0.5
    qkv_ref[...] = dot(h_one, w_ref[...], 1, 0).astype(bf16)
    span = offset_ref.shape[1]
    for at in range(heads):
        take = lambda part: qkv_ref[:, part * inner + at * HEAD : part * inner + (at + 1) * HEAD]
        spread = jnp.broadcast_to(offset_ref[at : at + 1, :], (seq_len, span))
        bias = pltpu.roll(spread, span - seq_len + 1, 1, stride=1, stride_axis=0)[:, :seq_len]
        scores = jnp.where(same_doc, dot(take(0), take(1), 1, 1) * 0.125 + bias, -1e30)
        expo = jnp.exp(scores - jnp.max(scores, axis=1, keepdims=True))
        probs = expo / jnp.sum(expo, axis=1, keepdims=True)
        probs_ref[at] = probs
        ctx = dot(probs.astype(bf16), take(2), 1, 0)
        ctx_ref[:, at * HEAD : (at + 1) * HEAD] = ctx.astype(bf16)
    part_ref[...] = dot(ctx_ref[...], out_w_ref[...], 1, 1).astype(bf16)


def dispatch(at_ref, x_ref, part_ref, peer_ref, gain_ref, slot_ref, g_ref, send_ref):
    half = g_ref.shape[1]
    x_one = x_ref[...].astype(f32) + (part_ref[...].astype(f32) + peer_ref[...].astype(f32))
    h_two = (x_one * rms_scale(x_one) * gain_ref[...]).astype(bf16)
    mine = jnp.where(at_ref[2] == 0, h_two[:, :half], h_two[:, half:])
    dims = (send_ref.shape[0], x_ref.shape[0])
    place = (lax.broadcasted_iota(jnp.int32, dims, 0) == slot_ref[...]).astype(bf16)
    send_ref[:, :half] = dot(place, mine, 1, 0).astype(bf16)
    send_ref[:, half:] = dot(place, g_ref[...], 1, 0).astype(bf16)


def run_expert(
    experts, row_size, at_ref, got_ref, peer_ref, router_ref, up_ref, down_ref,
    cross_ref, mine_ref, probs_ref, gate_part_ref, rows_ref, d_y_ref, act_ref, d_pre_ref, d_in_ref,
):
    half = got_ref.shape[1] // 2
    hidden = up_ref.shape[1]
    first_core = at_ref[2] == 0
    for at, refs in ((0, (got_ref, peer_ref)), (1, (peer_ref, got_ref))):
        pick = lambda lo: jnp.where(first_core, refs[0][:, lo : lo + half], refs[1][:, lo : lo + half])
        rows_ref[:, at * half : (at + 1) * half] = pick(0)
        d_y_ref[:, at * half : (at + 1) * half] = pick(half)
    rows, g_rows = rows_ref[...], d_y_ref[...].astype(f32)
    logits = dot(rows, router_ref[...], 1, 0)[:, :experts]
    expo = jnp.exp(logits - jnp.max(logits, axis=1, keepdims=True))
    probs = expo / jnp.sum(expo, axis=1, keepdims=True)
    probs_ref[...] = probs
    expert_at = at_ref[0] * row_size + at_ref[1]
    chosen = lax.broadcasted_iota(jnp.int32, probs.shape, 1) == expert_at
    gate = jnp.sum(jnp.where(chosen, probs, 0.0), axis=1, keepdims=True)
    d_y_ref[...] = (g_rows * gate).astype(bf16)
    step = 512 if hidden % 512 == 0 else hidden
    y_part = None
    for lo in range(0, hidden, step):
        cols = pl.ds(lo, step)
        pre_act = dot(rows_ref[...], up_ref[:, cols], 1, 0)
        cdf = 0.5 * (1.0 + lax.erf(pre_act * (1.0 / math.sqrt(2.0))))
        pdf = jnp.exp(-0.5 * pre_act * pre_act) * (1.0 / math.sqrt(2.0 * math.pi))
        act = (pre_act * cdf).astype(bf16)
        act_ref[:, cols] = act
        y_more = dot(act, down_ref[cols, :], 1, 0)
        d_pre = (dot(d_y_ref[...], down_ref[cols, :], 1, 1) * (cdf + pre_act * pdf)).astype(bf16)
        d_pre_ref[:, cols] = d_pre
        d_more = dot(d_pre, up_ref[:, cols], 1, 1)
        if lo == 0:
            y_part = y_more
            d_in_ref[...] = d_more
        else:
            y_part = y_part + y_more
            d_in_ref[...] += d_more
    gate_part_ref[...] = jnp.sum(g_rows * y_part, axis=1, keepdims=True)
    d_in = d_in_ref[...]
    mine_ref[:, :half] = jnp.where(first_core, y_part[:, :half], y_part[:, half:])
    mine_ref[:, half:] = jnp.where(first_core, d_in[:, :half], d_in[:, half:])
    cross_ref[:, :half] = jnp.where(first_core, y_part[:, half:], y_part[:, :half]).astype(bf16)
    cross_ref[:, half:] = jnp.where(first_core, d_in[:, half:], d_in[:, :half]).astype(bf16)


def settle(
    row_size, at_ref, mine_ref, crossed_ref, probs_ref, gate_part_ref, gate_peer_ref, router_ref, rows_ref,
    back_ref, grad_router_ref,
):
    half = mine_ref.shape[1] // 2
    probs = probs_ref[...]
    expert_at = at_ref[0] * row_size + at_ref[1]
    chosen = (lax.broadcasted_iota(jnp.int32, probs.shape, 1) == expert_at).astype(f32)
    gate = jnp.sum(probs * chosen, axis=1, keepdims=True)
    d_gate = gate_part_ref[...] + gate_peer_ref[...]
    d_logits = (d_gate * gate * (chosen - probs)).astype(bf16)
    router_w = router_ref[...][:, : probs.shape[1]]
    router_mine = jnp.where(at_ref[2] == 0, router_w[:half], router_w[half:])
    back_ref[:, :half] = (gate * (mine_ref[:, :half] + crossed_ref[:, :half].astype(f32))).astype(bf16)
    d_in = mine_ref[:, half:] + crossed_ref[:, half:].astype(f32)
    back_ref[:, half:] = (d_in + dot(d_logits, router_mine, 1, 1)).astype(bf16)
    grad_router_ref[...] = dot(d_logits, rows_ref[...], 0, 0)


def come_home(
    cube, at_ref, home_ref, peer_ref, slot_ref, x_ref, part_ref, part_peer_ref, g_ref, g_peer_ref,
    gain_ref, out_w_ref, ctx_ref, layer_ref, d_x_ref, gain_grad_ref, d_ctx_ref, *refs,
):
    *piece_refs, grads_ref = refs
    half = g_ref.shape[1]
    first_core = at_ref[2] == 0
    both = lambda a, b: jnp.concatenate(
        [jnp.where(first_core, a, b), jnp.where(first_core, b, a)], axis=1
    )
    dims = (home_ref.shape[0], x_ref.shape[0])
    place = (lax.broadcasted_iota(jnp.int32, dims, 0) == slot_ref[...]).astype(bf16)
    d_h = both(dot(place, home_ref[:, half:], 0, 0), dot(place, peer_ref[...], 0, 0))
    x_one = x_ref[...].astype(f32) + (part_ref[...].astype(f32) + part_peer_ref[...].astype(f32))
    g_full = both(g_ref[...], g_peer_ref[...]).astype(f32)
    scale = rms_scale(x_one)
    normed = x_one * scale
    gain_grad_ref[...] = jnp.sum(d_h * normed, axis=0, keepdims=True)
    d_norm = d_h * gain_ref[...]
    d_x = g_full + scale * (d_norm - normed * jnp.mean(d_norm * normed, axis=-1, keepdims=True))
    d_x_ref[...] = d_x
    d_x_b = d_x.astype(bf16)
    d_ctx_ref[...] = dot(d_x_b, out_w_ref[...], 1, 0).astype(bf16)
    grads_ref[...] = dot(d_x_b, ctx_ref[...], 0, 0).astype(bf16)
    rows = grads_ref.shape[0] // 16
    for m, piece_ref in enumerate(piece_refs):
        if not cube:
            piece_ref[...] = grads_ref[...]
            continue
        for k in range(4):
            start = pl.multiple_of(((at_ref[0] ^ k) * 4 + (at_ref[1] ^ m)) * rows, 16)
            piece_ref[k * rows : (k + 1) * rows, :] = grads_ref[pl.ds(start, rows), :]
    y_home = dot(place, home_ref[:, :half], 0, 0)
    x_mine = jnp.where(first_core, x_one[:, :half], x_one[:, half:])
    layer_ref[...] = (x_mine + y_home).astype(bf16)


def attend_backward(cube, at_ref, d_ctx_ref, qkv_ref, probs_ref, w_ref, d_h_ref, grad_offset_ref, *refs):
    *piece_refs, turned_ref = refs
    heads, seq_len, _ = probs_ref.shape
    inner = d_ctx_ref.shape[1]
    span = grad_offset_ref.shape[1]
    flip = (
        lax.broadcasted_iota(jnp.int32, (seq_len, seq_len), 0)
        + lax.broadcasted_iota(jnp.int32, (seq_len, seq_len), 1)
        == seq_len - 1
    ).astype(bf16)
    grad_offset_ref[...] = jnp.zeros(grad_offset_ref.shape, f32)
    for at in range(heads):
        cols = lambda part: pl.ds(part * inner + at * HEAD, HEAD)
        d_ctx = d_ctx_ref[:, at * HEAD : (at + 1) * HEAD]
        probs = probs_ref[at]
        d_probs = dot(d_ctx, qkv_ref[:, cols(2)], 1, 1)
        row_delta = jnp.sum(probs * d_probs, axis=1, keepdims=True)
        d_scores = (probs * (d_probs - row_delta)).astype(bf16)
        turned_ref[cols(0), :] = (dot(qkv_ref[:, cols(1)], d_scores, 0, 1) * 0.125).astype(bf16)
        turned_ref[cols(1), :] = (dot(qkv_ref[:, cols(0)], d_scores, 0, 0) * 0.125).astype(bf16)
        turned_ref[cols(2), :] = dot(d_ctx, probs.astype(bf16), 0, 0).astype(bf16)
        flipped = jnp.concatenate(
            [dot(flip, d_scores, 1, 0), jnp.zeros((seq_len, span - seq_len), f32)], axis=1
        )
        lined = pltpu.roll(flipped, 0, 1, stride=1, stride_axis=0)
        grad_offset_ref[at : at + 1, :] = jnp.sum(lined, axis=0, keepdims=True)
    size = piece_refs[0].shape[0]
    for m, piece_ref in enumerate(piece_refs):
        start = pl.multiple_of((at_ref[1] ^ m) * size, 16) if cube else 0
        piece_ref[...] = turned_ref[pl.ds(start, size), :]
    d_h_ref[...] = dot(turned_ref[...], w_ref[...], 0, 1).astype(bf16)


def qkv_terms(at_ref, turned_ref, small_ref, router_ref, *refs):
    mine_ref, peer_ref, piece_refs, block_refs, grads_ref = refs[0], refs[1], refs[2:6], refs[6:10], refs[10]
    half = mine_ref.shape[0] // 3
    from_mine = from_peer = 0.0
    for m in range(1, 4):
        rows = slice((m - 1) * half, m * half)
        from_mine = from_mine + dot(mine_ref[rows, :], piece_refs[m][...], 1, 1)
        from_peer = from_peer + dot(peer_ref[rows, :], piece_refs[m][...], 1, 1)
    own = dot(turned_ref[...], piece_refs[0][...], 1, 1)
    first_core = at_ref[2] == 0
    grads_ref[:half, :] = (own[:half] + jnp.where(first_core, from_mine, from_peer)).astype(bf16)
    grads_ref[half:, :] = (own[half:] + jnp.where(first_core, from_peer, from_mine)).astype(bf16)
    rows, size = block_refs[0].shape[0] - 8, grads_ref.shape[1]
    width = small_ref.shape[1]
    part = width // 4
    for k, block_ref in enumerate(block_refs):
        block_ref[rows:, :width] = small_ref[...].astype(bf16)
        router = jnp.zeros((router_ref.shape[0], part), f32)
        for z in range(4):
            router = jnp.where((at_ref[0] ^ k) == z, router_ref[:, z * part : (z + 1) * part], router)
        for i in range(2):
            low = width + i * part
            block_ref[rows:, low : low + part] = router[i * 8 : (i + 1) * 8].astype(bf16)
        for m in range(4):
            start = ((at_ref[0] ^ k) * 4 + (at_ref[1] ^ m)) * rows
            block_ref[:rows, m * size : (m + 1) * size] = grads_ref[pl.ds(pl.multiple_of(start, 16), rows), :]


def pair_sum(refs):
    a, b, c, d = (ref[...].astype(f32) for ref in refs)
    return (a + b) + (c + d)


def join_line(at_ref, *refs):
    total = pair_sum(refs[:4])
    rows = refs[4].shape[0]
    size = total.shape[1] // 4
    width = size * 8 // 3
    part = width // 16
    extra = total[rows:]
    for m, piece_ref in enumerate(refs[4:]):
        piece_ref[...] = jnp.zeros(piece_ref.shape, bf16)
        piece_ref[:, :size] = total[:rows, m * size : (m + 1) * size].astype(bf16)
        for i in range(2):
            for j in range(width // 128):
                line = extra[6 + i : 7 + i, j * 128 : (j + 1) * 128]
                piece_ref[i * 8 + j : i * 8 + j + 1, 384:] = line.astype(bf16)
            router = jnp.zeros((8, part), f32)
            for row in range(4):
                low = width + i * 4 * part + row * part
                router = jnp.where((at_ref[1] ^ m) == row, extra[:, low : low + part], router)
            piece_ref[32 + i * 8 : 40 + i * 8, 384 : 384 + part] = router.astype(bf16)
        piece_ref[16:24, 384:] = extra[:, :128].astype(bf16)


def join_plane(at_ref, *refs):
    piece_refs, (out_ref, gain_one_ref, gain_two_ref, rel_ref, router_ref, line_ref) = refs[:4], refs[4:]
    size = line_ref.shape[1] // 4
    for quarter in range(4):
        piece = 0.0
        for m, piece_ref in enumerate(piece_refs):
            piece = jnp.where((at_ref[1] ^ m) == quarter, piece_ref[:, :size].astype(f32), piece)
        line_ref[:, quarter * size : (quarter + 1) * size] = piece
    inner = out_ref.shape[2]
    for part in range(3):
        out_ref[part] = line_ref[:, part * inner : (part + 1) * inner]
    extra = pair_sum([ref.at[:, 384:] for ref in piece_refs])
    for i, gain_ref in enumerate((gain_one_ref, gain_two_ref)):
        for j in range(gain_ref.shape[1] // 128):
            gain_ref[:, j * 128 : (j + 1) * 128] = extra[i * 8 + j : i * 8 + j + 1]
    rel_ref[...] = extra[16 : 16 + rel_ref.shape[0], : rel_ref.shape[1]]
    router_ref[...] = extra[32 : 32 + router_ref.shape[0], : router_ref.shape[1]]


def join_blocks(*refs):
    total = pair_sum(refs[:4])
    rows = total.shape[0] // 4
    for k, block_ref in enumerate(refs[4:]):
        block_ref[...] = total[k * rows : (k + 1) * rows].astype(bf16)


def finish(
    d_h_ref, peer_ref, x_ref, d_x_ref, gain_ref, gain_grad_ref, grad_offset_ref, hot_ref, grad_x_ref, small_ref,
):
    d_h = d_h_ref[...].astype(f32) + peer_ref[...].astype(f32)
    x_float = x_ref[...].astype(f32)
    scale = rms_scale(x_float)
    normed = x_float * scale
    d_norm = d_h * gain_ref[...]
    grad_x = d_x_ref[...] + scale * (
        d_norm - normed * jnp.mean(d_norm * normed, axis=-1, keepdims=True)
    )
    grad_x_ref[...] = grad_x.astype(bf16)
    heads, buckets = grad_offset_ref.shape[0] - 2, hot_ref.shape[1]
    small_ref[...] = jnp.zeros(small_ref.shape, f32)
    grad_rel = lax.dot_general(
        grad_offset_ref[...], hot_ref[...], (((1,), (0,)), ((), ())), precision=highest, preferred_element_type=f32
    )
    small_ref[:, :buckets] = grad_rel
    small_ref[heads : heads + 1, :] = jnp.sum(d_h * normed, axis=0, keepdims=True)
    small_ref[heads + 1 : heads + 2, :] = gain_grad_ref[...]


def expert_grads(rows_ref, d_y_ref, act_ref, d_pre_ref, down_ref, up_ref, held_ref, sems):
    (hidden, width), steps = down_ref.shape, 3
    copies = []
    chunk = 0
    for left_ref, right_ref, out_ref in ((act_ref, d_y_ref, down_ref), (rows_ref, d_pre_ref, up_ref)):
        count = out_ref.shape[0] // steps
        for at in range(steps):
            rows = pl.ds(at * count, count)
            slot = chunk % 3
            if chunk >= 3:
                copies[chunk - 3].wait()
            held = held_ref.at[slot, pl.ds(0, count), pl.ds(0, out_ref.shape[1])]
            held[...] = dot(left_ref[:, rows], right_ref[...], 0, 0)
            copies.append(pltpu.make_async_copy(held, out_ref.at[rows, :], sems.at[chunk]))
            copies[-1].start()
            chunk += 1
    for copy in copies[-3:]:
        copy.wait()


def experts_pad(experts):
    return -(-experts // 128) * 128


def make_per_device(mesh):
    n_ex, n_row = mesh.shape["ex"], mesh.shape["row"]
    groups = n_ex * n_row

    def hop(values, axis, step):
        return lax.ppermute(values, axis, [(i, i ^ step) for i in range(mesh.shape[axis])])

    def whole_cube(rows):
        return n_ex == 4 and n_row == 4 and rows == 48

    def gather_blocks(shard):
        rows, width = shard.shape
        if whole_cube(rows):
            line = [shard] + [hop(shard, "ex", k) for k in (1, 2, 3)]
            xs = [hop(part, "row", 1) for part in line]
            ys = [hop(part, "row", 2) for part in line]
            diagonal = [
                hop(ys[k], "row", 1) if k % 2 else hop(xs[k], "row", 2) for k in range(4)
            ]
            return [*line, *xs, *ys, *diagonal]
        part = lax.all_gather(shard, "ex", axis=0)
        part = jnp.broadcast_to(part[None], (n_row, n_ex, rows, width))
        part = lax.all_to_all(part, "row", split_axis=0, concat_axis=0, tiled=True)
        return [part.transpose(1, 0, 2, 3).reshape(groups * rows, width)]

    def scatter_groups(grads, rows):
        part = grads.astype(bf16).reshape(n_ex, n_row, rows, -1).transpose(1, 0, 2, 3)
        part = lax.all_to_all(part, "row", split_axis=0, concat_axis=0, tiled=True)
        part = jnp.sum(part.astype(f32), axis=0).astype(bf16)
        part = lax.all_to_all(part, "ex", split_axis=0, concat_axis=0, tiled=True)
        return jnp.sum(part.astype(f32), axis=0)

    def plane_hops(parts):
        return [hop(part, "row", m + 1) for m, part in enumerate(parts)]

    def line_hops(parts):
        return [hop(part, "ex", k + 1) for k, part in enumerate(parts)]

    def sum_groups(values):
        for axis in ("row", "ex"):
            step = 1
            while step < mesh.shape[axis]:
                values = values + hop(values, axis, step)
                step *= 2
        return values

    def per_device(
        x_in,
        gain_attn,
        w_qkv,
        rel_bias,
        w_out,
        gain_ffn,
        w_router,
        w_up,
        w_down,
        seg_ids,
        expert_ids,
        slot_ids,
        drop_flags,
        d_out,
    ):
        seq_len, width = x_in.shape
        heads_here = rel_bias.shape[1]
        inner = w_qkv.shape[2]
        own_rows = w_qkv.shape[1]
        experts = w_router.shape[1]
        wide = inner + experts_pad(experts)
        capacity = 5 * seq_len // (4 * experts)
        slots = -(-capacity // 8) * 8
        slot_total = experts * slots
        half = d_out.shape[1]
        hidden = w_up.shape[2]
        device_at = jnp.stack([lax.axis_index(axis).astype(jnp.int32) for axis in ("ex", "row", "col")])
        device_at, w_qkv = lax.optimization_barrier((device_at, w_qkv))
        cube = whole_cube(own_rows)
        gather_order = GATHER_ORDER if cube else None

        (packed,) = vmem_call(
            pack_weights,
            (shape((own_rows, 3 * inner + wide), bf16),),
            0,
            w_qkv,
            w_out.T,
            w_router.T,
        )
        blocks = gather_blocks(packed)
        normed_turned, normed_mine = vmem_call(
            turn_normed,
            (shape((width, seq_len), bf16), shape((half, seq_len), bf16)),
            0,
            x_in,
            gain_attn[None],
            scalars=(device_at,),
        )
        up_w = w_up[0].astype(bf16)
        down_w = w_down[0].astype(bf16)
        *blocks, up_w, down_w, normed_mine, normed_turned = lax.optimization_barrier(
            (*blocks, up_w, down_w, normed_mine, normed_turned)
        )
        g_peer = swap_cores(d_out)

        span = 2 * seq_len
        offsets = jnp.arange(span, dtype=jnp.int32) - (seq_len - 1)
        offset_hot = (
            bucket_of(offsets)[:, None] == jnp.arange(BUCKETS, dtype=jnp.int32)[None, :]
        ).astype(f32)
        per_offset = jnp.einsum("bh,ob->ho", rel_bias, offset_hot, precision=highest)
        square = seq_len * seq_len * heads_here * HEAD
        attn_part, qkv, probs, context, qkv_w, out_w, router_w = vmem_call(
            functools.partial(attend_forward, gather_order),
            (
                shape((seq_len, width), bf16),
                shape((seq_len, 3 * inner), bf16),
                shape((heads_here, seq_len, seq_len), f32),
                shape((seq_len, inner), bf16),
                shape((width, 3 * inner), bf16),
                shape((width, inner), bf16),
                shape((width, wide - inner), bf16),
            ),
            8 * seq_len * width * inner + 4 * square,
            x_in,
            gain_attn[None],
            per_offset,
            seg_ids,
            *blocks,
            scalars=(device_at,),
        )
        attn_peer = swap_cores(attn_part)
        slot_of = jnp.where(drop_flags == 1, slot_total, expert_ids * slots + slot_ids)[None]
        (send,) = vmem_call(
            dispatch,
            (shape((slot_total, width), bf16),),
            2 * seq_len * slot_total * width,
            x_in,
            attn_part,
            attn_peer,
            gain_ffn[None],
            slot_of,
            d_out,
            scalars=(device_at,),
        )
        got = lax.all_to_all(
            send.reshape(experts, slots, width), ("ex", "row"), 0, 0, tiled=True
        ).reshape(slot_total, width)
        if cube:
            later_normed, got = lax.optimization_barrier((normed_mine, got))
            normed_hops = plane_hops([later_normed] * 2)
        crossing, mine, router_probs, gate_part, rows, d_y, act_b, d_pre = vmem_call(
            functools.partial(run_expert, experts, n_row),
            (
                shape((slot_total, width), bf16),
                shape((slot_total, width), f32),
                shape((slot_total, experts), f32),
                shape((slot_total, 1), f32),
                shape((slot_total, width), bf16),
                shape((slot_total, width), bf16),
                shape((slot_total, hidden), bf16),
                shape((slot_total, hidden), bf16),
            ),
            8 * slot_total * width * hidden,
            got,
            swap_cores(got),
            router_w,
            up_w,
            down_w,
            scalars=(device_at,),
            scratch=(pltpu.VMEM((slot_total, width), f32),),
        )
        if cube:
            crossing, gate_part, *normed_hops = lax.optimization_barrier((crossing, gate_part, *normed_hops))
            from_x, from_y = normed_hops
            normed_hops += [hop(from_x[: half // 2], "row", 2), hop(from_y[half // 2 :], "row", 1)]
        back, grad_router = vmem_call(
            functools.partial(settle, n_row),
            (shape((slot_total, width), bf16), shape((experts, width), f32)),
            2 * slot_total * half * experts,
            mine,
            swap_cores(crossing),
            router_probs,
            gate_part,
            swap_cores(gate_part),
            router_w,
            rows,
            scalars=(device_at,),
        )
        if cube:
            back, *normed_hops = lax.optimization_barrier((back, *normed_hops))
        home = lax.all_to_all(
            back.reshape(experts, slots, width), ("ex", "row"), 0, 0, tiled=True
        ).reshape(slot_total, width)
        def grads_of_expert(rows, d_y, act_b, d_pre):
            return pl.pallas_call(
                expert_grads,
                out_shape=(shape((hidden, width), f32), shape((width, hidden), f32)),
                in_specs=[pl.BlockSpec(memory_space=pltpu.VMEM)] * 4,
                out_specs=[pl.BlockSpec(memory_space=pltpu.HBM)] * 2,
                scratch_shapes=[
                    pltpu.VMEM((3, max(hidden, width) // 3, max(hidden, width)), f32),
                    pltpu.SemaphoreType.DMA((6,)),
                ],
                compiler_params=pltpu.CompilerParams(vmem_limit_bytes=24 * 2**20),
                cost_estimate=pl.CostEstimate(
                    flops=4 * slot_total * width * hidden, bytes_accessed=12 * width * hidden, transcendentals=0
                ),
            )(rows, d_y, act_b, d_pre)

        quarter = (width // 4, 3 * inner // 4) if cube else (width, 3 * inner)
        pieces = 4 if cube else 1
        layer_out, d_x_one, grad_gain_ffn, d_context, *out_pieces = vmem_call(
            functools.partial(come_home, cube),
            (
                shape((seq_len, half), bf16),
                shape((seq_len, width), f32),
                shape((1, width), f32),
                shape((seq_len, inner), bf16),
                *[shape((quarter[0], inner), bf16)] * pieces,
            ),
            2 * seq_len * (slot_total * 3 * half + 2 * width * inner),
            home,
            swap_cores(home[:, half:]),
            slot_of,
            x_in,
            attn_part,
            attn_peer,
            d_out,
            g_peer,
            gain_ffn[None],
            out_w,
            context,
            scalars=(device_at,),
            scratch=(pltpu.VMEM((width, inner), bf16),),
        )
        d_h_part, grad_offset, *d_qkv_turned = vmem_call(
            functools.partial(attend_backward, cube),
            (
                shape((seq_len, width), bf16),
                shape((heads_here + 2, span), f32),
                *[shape((quarter[1], seq_len), bf16)] * pieces,
            ),
            6 * seq_len * width * inner + 10 * square,
            d_context,
            qkv,
            probs,
            qkv_w,
            scalars=(device_at,),
            scratch=(pltpu.VMEM((3 * inner, seq_len), bf16),),
        )
        grad_x, small = vmem_call(
            finish,
            (shape((seq_len, width), bf16), shape((heads_here + 2, width), f32)),
            0,
            d_h_part,
            swap_cores(d_h_part),
            x_in,
            d_x_one,
            gain_attn[None],
            grad_gain_ffn,
            grad_offset,
            offset_hot,
        )
        if cube:
            *normed_hops, _ = lax.optimization_barrier((*normed_hops, d_h_part))
            normed_near = jnp.concatenate(normed_hops, axis=0)
            normed_peer = swap_cores(normed_near)
            terms = vmem_call(
                qkv_terms,
                [shape((own_rows + 8, 3 * inner), bf16)] * 4,
                6 * seq_len * width * inner,
                normed_turned,
                small,
                grad_router,
                normed_near,
                normed_peer,
                d_qkv_turned[0],
                *plane_hops(d_qkv_turned[1:]),
                scalars=(device_at,),
                scratch=(pltpu.VMEM((width, quarter[1]), bf16),),
            )
            line = line_hops(terms[1:])
            first_line = line[0]
            rows, d_y, act_b, d_pre, _ = lax.optimization_barrier((rows, d_y, act_b, d_pre, terms[0]))
            grad_down, grad_up = grads_of_expert(rows, d_y, act_b, d_pre)
            *line, grad_down, grad_up = lax.optimization_barrier((*line, grad_down, grad_up))
            split = vmem_call(
                join_line,
                [shape((own_rows, 512), bf16)] * 4,
                0,
                terms[0],
                *line,
                scalars=(device_at,),
            )
            last = plane_hops(split[1:])
            grad_qkv, gain_one, gain_two, grad_rel, grad_router = vmem_call(
                join_plane,
                (
                    shape((3, own_rows, inner), f32),
                    shape((1, width), f32),
                    shape((1, width), f32),
                    shape((heads_here, BUCKETS), f32),
                    shape((experts, own_rows), f32),
                ),
                0,
                split[0],
                *last,
                scalars=(device_at,),
                scratch=(pltpu.VMEM((own_rows, 3 * inner), f32),),
            )
            *out_pieces, _ = lax.optimization_barrier((*out_pieces, first_line))
            out_hops = plane_hops(out_pieces[1:])
            out_blocks = vmem_call(
                join_blocks,
                [shape((own_rows, inner), bf16)] * 4,
                0,
                out_pieces[0],
                *out_hops,
            )
            *out_blocks, _ = lax.optimization_barrier((*out_blocks, last[0]))
            out_blocks = (out_blocks[0], *line_hops(out_blocks[1:]))
            grad_out = sum(part.astype(f32) for part in out_blocks)
        else:
            grad_down, grad_up = grads_of_expert(rows, d_y, act_b, d_pre)
            grad_qkv = scatter_groups(dot(normed_turned, d_qkv_turned[0], 1, 1), own_rows)
            grad_qkv = grad_qkv.reshape(own_rows, 3, inner).transpose(1, 0, 2)
            grad_out = scatter_groups(out_pieces[0], own_rows)
            small = sum_groups(jnp.concatenate([small, grad_router]))
            gain_one, gain_two = small[heads_here], small[heads_here + 1]
            grad_rel = small[:heads_here, :BUCKETS]
            own_at = (device_at[0] * n_row + device_at[1]) * own_rows
            grad_router = lax.dynamic_slice(small, (heads_here + 2, own_at), (experts, own_rows))
        return (
            layer_out,
            grad_x,
            gain_one.reshape(width),
            grad_qkv,
            grad_rel.T,
            grad_out.T,
            gain_two.reshape(width),
            grad_router.T,
            grad_up[None],
            grad_down[None],
        )

    return per_device


def solution(mesh):
    return jax.shard_map(
        make_per_device(mesh),
        mesh=mesh,
        in_specs=(
            P(("ex", "row"), None),
            P(),
            P(None, ("ex", "row"), "col"),
            P(None, "col"),
            P("col", ("ex", "row")),
            P(),
            P(("ex", "row"), None),
            P(("ex", "row"), None, "col"),
            P(("ex", "row"), "col", None),
            P(("ex", "row"), None),
            P(("ex", "row")),
            P(("ex", "row")),
            P(("ex", "row")),
            P(("ex", "row"), "col"),
        ),
        out_specs=(
            P(("ex", "row"), "col"),
            P(("ex", "row"), None),
            P(),
            P(None, ("ex", "row"), "col"),
            P(None, "col"),
            P("col", ("ex", "row")),
            P(),
            P(("ex", "row"), None),
            P(("ex", "row"), None, "col"),
            P(("ex", "row"), "col", None),
        ),
        check_vma=False,
    )
```

```python
import functools
import math

import jax
import jax.numpy as jnp
from jax import lax
from jax.experimental import pallas as pl
from jax.experimental.pallas import tpu as pltpu
from jax.sharding import PartitionSpec as P

HEAD = 64
BUCKETS = 32

norm_eps = 1e-06
bucket_edges = (12, 16, 23, 32, 46, 64, 91)
highest = lax.Precision.HIGHEST
bf16 = jnp.bfloat16
f32 = jnp.float32

GATHER_ORDER = tuple(((k, m),) for m in range(4) for k in range(4))

def bucket_of(offset):
    distance = jnp.abs(offset)
    far_part = jnp.zeros(distance.shape, jnp.int32)
    for edge_at in bucket_edges:
        far_part = far_part + (distance >= edge_at).astype(jnp.int32)
    inside = jnp.where(distance < 8, distance, far_part + jnp.int32(8))
    upper = jnp.where(offset > 0, jnp.int32(BUCKETS // 2), jnp.int32(0))
    return inside + upper


def rms_scale(values):
    return lax.rsqrt(jnp.mean(values * values, axis=-1, keepdims=True) + norm_eps)


def dot(a, b, ca, cb):
    return lax.dot_general(a, b, (((ca,), (cb,)), ((), ())), preferred_element_type=f32)


def swap_cores(values):
    return lax.ppermute(values, "col", [(0, 1), (1, 0)])


def shape(dims, dtype):
    return jax.ShapeDtypeStruct(tuple(dims), dtype)


def vmem_call(kernel, out_shape, flops, *args, scalars=(), scratch=(), limit=12):
    nbytes = sum(math.prod(v.shape) * v.dtype.itemsize for v in (*args, *out_shape))
    spec = pl.BlockSpec(memory_space=pltpu.VMEM)
    limit = limit if nbytes < 16 * 2**20 else 48
    return pl.pallas_call(
        kernel,
        out_shape=out_shape,
        in_specs=[pl.BlockSpec(memory_space=pltpu.SMEM)] * len(scalars) + [spec] * len(args),
        out_specs=[spec] * len(out_shape),
        scratch_shapes=scratch,
        compiler_params=pltpu.CompilerParams(vmem_limit_bytes=limit * 2**20),
        cost_estimate=pl.CostEstimate(flops=flops, bytes_accessed=nbytes, transcendentals=0),
    )(*scalars, *args)


def block_rows(at_ref, order, count):
    if order is None:
        return [pl.ds(0, count)]
    ex_at, row_at = at_ref[0], at_ref[1]
    return [
        pl.ds(pl.multiple_of(((ex_at ^ k) * 4 + (row_at ^ m)) * count, 16), count)
        for part in order
        for k, m in part
    ]


def eye(size):
    dims = (size, size)
    same = lax.broadcasted_iota(jnp.int32, dims, 0) == lax.broadcasted_iota(jnp.int32, dims, 1)
    return same.astype(bf16)


def pack_weights(qkv_ref, out_turned_ref, router_turned_ref, packed_ref):
    inner, experts = qkv_ref.shape[2], router_turned_ref.shape[0]
    for part in range(3):
        packed_ref[:, part * inner : (part + 1) * inner] = qkv_ref[part].astype(bf16)
    packed_ref[:, 3 * inner : 4 * inner] = out_turned_ref[...].astype(bf16)
    packed_ref[:, 4 * inner :] = jnp.zeros((packed_ref.shape[0], packed_ref.shape[1] - 4 * inner), bf16)
    router = dot(router_turned_ref[...].astype(bf16), eye(experts), 0, 0)
    packed_ref[:, 4 * inner : 4 * inner + experts] = router.astype(bf16)


def turn_normed(at_ref, x_ref, gain_ref, turned_ref, mine_ref):
    x_float = x_ref[...].astype(f32)
    h_one = (x_float * rms_scale(x_float) * gain_ref[...]).astype(bf16)
    turned_ref[...] = dot(h_one, eye(h_one.shape[0]), 0, 0).astype(bf16)
    half = mine_ref.shape[0]
    mine_ref[...] = jnp.where(at_ref[2] == 0, turned_ref[:half, :], turned_ref[half:, :])


def attend_forward(order, at_ref, x_ref, gain_ref, offset_ref, seg_ref, *refs):
    *block_refs, part_ref, qkv_ref, probs_ref, ctx_ref, w_ref, out_w_ref, router_ref = refs
    seq_len = x_ref.shape[0]
    heads, inner = probs_ref.shape[0], ctx_ref.shape[1]
    for rows, block_ref in zip(block_rows(at_ref, order, block_refs[0].shape[0]), block_refs):
        w_ref[rows, :] = block_ref[:, : 3 * inner]
        out_w_ref[rows, :] = block_ref[:, 3 * inner : 4 * inner]
        router_ref[rows, :] = block_ref[:, 4 * inner :]
    x_float = x_ref[...].astype(f32)
    h_one = (x_float * rms_scale(x_float) * gain_ref[...]).astype(bf16)
    documents = lax.broadcasted_iota(jnp.int32, (8, seq_len), 0) == seg_ref[...]
    same_doc = dot(documents.astype(bf16), documents.astype(bf16), 0, 0) > 0.5
    qkv_ref[...] = dot(h_one, w_ref[...], 1, 0).astype(bf16)
    span = offset_ref.shape[1]
    for at in range(heads):
        take = lambda part: qkv_ref[:, part * inner + at * HEAD : part * inner + (at + 1) * HEAD]
        spread = jnp.broadcast_to(offset_ref[at : at + 1, :], (seq_len, span))
        bias = pltpu.roll(spread, span - seq_len + 1, 1, stride=1, stride_axis=0)[:, :seq_len]
        scores = jnp.where(same_doc, dot(take(0), take(1), 1, 1) * 0.125 + bias, -1e30)
        expo = jnp.exp(scores - jnp.max(scores, axis=1, keepdims=True))
        probs = expo / jnp.sum(expo, axis=1, keepdims=True)
        probs_ref[at] = probs
        ctx = dot(probs.astype(bf16), take(2), 1, 0)
        ctx_ref[:, at * HEAD : (at + 1) * HEAD] = ctx.astype(bf16)
    part_ref[...] = dot(ctx_ref[...], out_w_ref[...], 1, 1).astype(bf16)


def spare_rows(experts, chunk):
    dims = (experts * 24, experts * 4)
    row, column = lax.broadcasted_iota(jnp.int32, dims, 0), lax.broadcasted_iota(jnp.int32, dims, 1)
    expert = lax.shift_right_logical(row * 2731, 16)
    inside = row - expert * 24
    wanted = expert * 4 + (inside - chunk * 4)
    return ((column == wanted) & (inside >= chunk * 4) & (inside < chunk * 4 + 4)).astype(bf16)


def pack_slots(values, packed_ref):
    if len(packed_ref.shape) == 2:
        packed_ref[...] = values.astype(bf16)
        return
    experts, chunks = packed_ref.shape[0], values.shape[1] // 128
    values = values.astype(bf16)
    spare = 0.0
    for c in range(chunks):
        chunk = values[:, c * 128 : (c + 1) * 128]
        for e in range(experts):
            packed_ref[e, c * 16 : (c + 1) * 16, :] = chunk[e * 16 : (e + 1) * 16]
        spare = spare + dot(spare_rows(experts, c), chunk[experts * 16 :], 1, 0)
    for e in range(experts):
        packed_ref[e, chunks * 16 :, :] = spare[e * 24 : (e + 1) * 24].astype(bf16)


def unpack_slots(packed_ref, low, target_ref, spare_ref):
    experts, chunks = packed_ref.shape[0], target_ref.shape[1] // 128
    first = (packed_ref.shape[1] - 24) // 16 * 16
    for e in range(experts):
        spare_ref[e * 24 : (e + 1) * 24, :] = packed_ref[e, first:, :].astype(f32)
    spare = spare_ref[...].astype(bf16)
    for c in range(chunks):
        lanes = slice(c * 128, (c + 1) * 128)
        for e in range(experts):
            rows = slice((low + c) * 16, (low + c + 1) * 16)
            target_ref[e * 16 : (e + 1) * 16, lanes] = packed_ref[e, rows, :]
        target_ref[experts * 16 :, lanes] = dot(spare_rows(experts, low + c), spare, 0, 0).astype(bf16)


def dispatch(at_ref, x_ref, part_ref, peer_ref, gain_ref, slot_ref, g_ref, send_ref):
    half = g_ref.shape[1]
    x_one = x_ref[...].astype(f32) + (part_ref[...].astype(f32) + peer_ref[...].astype(f32))
    h_two = (x_one * rms_scale(x_one) * gain_ref[...]).astype(bf16)
    mine = jnp.where(at_ref[2] == 0, h_two[:, :half], h_two[:, half:])
    slots = send_ref.shape[0] * (1 if len(send_ref.shape) == 2 else 20)
    dims = (slots, x_ref.shape[0])
    place = (lax.broadcasted_iota(jnp.int32, dims, 0) == slot_ref[...]).astype(bf16)
    sent = jnp.concatenate([dot(place, mine, 1, 0), dot(place, g_ref[...], 1, 0)], axis=1)
    pack_slots(sent, send_ref)


def run_expert(
    experts, row_size, at_ref, got_ref, peer_ref, router_ref, up_ref, down_ref,
    cross_ref, mine_ref, probs_ref, gate_part_ref, rows_ref, d_y_ref, act_ref, d_pre_ref, d_in_ref,
    got_rows_ref, peer_rows_ref, spare_ref,
):
    half = rows_ref.shape[1] // 2
    if len(got_ref.shape) == 3:
        unpack_slots(got_ref, 0, got_rows_ref, spare_ref)
        unpack_slots(peer_ref, 0, peer_rows_ref, spare_ref)
        got_ref, peer_ref = got_rows_ref, peer_rows_ref
    hidden = up_ref.shape[1]
    first_core = at_ref[2] == 0
    for at, refs in ((0, (got_ref, peer_ref)), (1, (peer_ref, got_ref))):
        pick = lambda lo: jnp.where(first_core, refs[0][:, lo : lo + half], refs[1][:, lo : lo + half])
        rows_ref[:, at * half : (at + 1) * half] = pick(0)
        d_y_ref[:, at * half : (at + 1) * half] = pick(half)
    rows, g_rows = rows_ref[...], d_y_ref[...].astype(f32)
    logits = dot(rows, router_ref[...], 1, 0)[:, :experts]
    expo = jnp.exp(logits - jnp.max(logits, axis=1, keepdims=True))
    probs = expo / jnp.sum(expo, axis=1, keepdims=True)
    probs_ref[...] = probs
    expert_at = at_ref[0] * row_size + at_ref[1]
    chosen = lax.broadcasted_iota(jnp.int32, probs.shape, 1) == expert_at
    gate = jnp.sum(jnp.where(chosen, probs, 0.0), axis=1, keepdims=True)
    d_y_ref[...] = (g_rows * gate).astype(bf16)
    step = 512 if hidden % 512 == 0 else hidden
    y_part = None
    for lo in range(0, hidden, step):
        cols = pl.ds(lo, step)
        pre_act = dot(rows_ref[...], up_ref[:, cols], 1, 0)
        cdf = 0.5 * (1.0 + lax.erf(pre_act * (1.0 / math.sqrt(2.0))))
        pdf = jnp.exp(-0.5 * pre_act * pre_act) * (1.0 / math.sqrt(2.0 * math.pi))
        act = (pre_act * cdf).astype(bf16)
        act_ref[:, cols] = act
        y_more = dot(act, down_ref[cols, :], 1, 0)
        d_pre = (dot(d_y_ref[...], down_ref[cols, :], 1, 1) * (cdf + pre_act * pdf)).astype(bf16)
        d_pre_ref[:, cols] = d_pre
        d_more = dot(d_pre, up_ref[:, cols], 1, 1)
        if lo == 0:
            y_part = y_more
            d_in_ref[...] = d_more
        else:
            y_part = y_part + y_more
            d_in_ref[...] += d_more
    gate_part_ref[...] = jnp.sum(g_rows * y_part, axis=1, keepdims=True)
    d_in = d_in_ref[...]
    mine_ref[:, :half] = jnp.where(first_core, y_part[:, :half], y_part[:, half:])
    mine_ref[:, half:] = jnp.where(first_core, d_in[:, :half], d_in[:, half:])
    cross_ref[:, :half] = jnp.where(first_core, y_part[:, half:], y_part[:, :half]).astype(bf16)
    cross_ref[:, half:] = jnp.where(first_core, d_in[:, half:], d_in[:, :half]).astype(bf16)


def settle(
    row_size, at_ref, mine_ref, crossed_ref, probs_ref, gate_part_ref, gate_peer_ref, router_ref, rows_ref,
    back_ref, grad_router_ref,
):
    half = mine_ref.shape[1] // 2
    probs = probs_ref[...]
    expert_at = at_ref[0] * row_size + at_ref[1]
    chosen = (lax.broadcasted_iota(jnp.int32, probs.shape, 1) == expert_at).astype(f32)
    gate = jnp.sum(probs * chosen, axis=1, keepdims=True)
    d_gate = gate_part_ref[...] + gate_peer_ref[...]
    d_logits = (d_gate * gate * (chosen - probs)).astype(bf16)
    router_w = router_ref[...][:, : probs.shape[1]]
    router_mine = jnp.where(at_ref[2] == 0, router_w[:half], router_w[half:])
    y_gated = gate * (mine_ref[:, :half] + crossed_ref[:, :half].astype(f32))
    d_in = mine_ref[:, half:] + crossed_ref[:, half:].astype(f32) + dot(d_logits, router_mine, 1, 1)
    pack_slots(jnp.concatenate([y_gated, d_in], axis=1), back_ref)
    grad_router_ref[...] = dot(d_logits, rows_ref[...], 0, 0)


def arrive(at_ref, home_ref, slot_ref, x_ref, part_ref, peer_ref, layer_ref, d_h_ref, rows_ref, spare_ref):
    half = layer_ref.shape[1]
    if len(home_ref.shape) == 3:
        unpack_slots(home_ref, 0, rows_ref, spare_ref)
        home_ref = rows_ref
    dims = (home_ref.shape[0], x_ref.shape[0])
    place = (lax.broadcasted_iota(jnp.int32, dims, 0) == slot_ref[...]).astype(bf16)
    d_h_ref[...] = dot(place, home_ref[:, half:], 0, 0).astype(bf16)
    y_home = dot(place, home_ref[:, :half], 0, 0)
    mine = lambda ref: jnp.where(at_ref[2] == 0, ref[:, :half], ref[:, half:]).astype(f32)
    layer_ref[...] = (mine(x_ref) + (mine(part_ref) + mine(peer_ref)) + y_home).astype(bf16)


def come_home(
    cube, at_ref, mine_ref, peer_ref, x_ref, part_ref, part_peer_ref, g_ref, g_peer_ref,
    gain_ref, out_w_ref, ctx_ref, d_x_ref, gain_grad_ref, d_ctx_ref, *refs,
):
    *piece_refs, grads_ref = refs
    first_core = at_ref[2] == 0
    both = lambda a, b: jnp.concatenate(
        [jnp.where(first_core, a, b), jnp.where(first_core, b, a)], axis=1
    )
    d_h = both(mine_ref[...], peer_ref[...]).astype(f32)
    x_one = x_ref[...].astype(f32) + (part_ref[...].astype(f32) + part_peer_ref[...].astype(f32))
    g_full = both(g_ref[...], g_peer_ref[...]).astype(f32)
    scale = rms_scale(x_one)
    normed = x_one * scale
    gain_grad_ref[...] = jnp.sum(d_h * normed, axis=0, keepdims=True)
    d_norm = d_h * gain_ref[...]
    d_x = g_full + scale * (d_norm - normed * jnp.mean(d_norm * normed, axis=-1, keepdims=True))
    d_x_ref[...] = d_x
    d_x_b = d_x.astype(bf16)
    d_ctx_ref[...] = dot(d_x_b, out_w_ref[...], 1, 0).astype(bf16)
    grads_ref[...] = dot(d_x_b, ctx_ref[...], 0, 0).astype(bf16)
    rows = grads_ref.shape[0] // 16
    for m, piece_ref in enumerate(piece_refs):
        if not cube:
            piece_ref[...] = grads_ref[...]
            continue
        for k in range(4):
            start = pl.multiple_of(((at_ref[0] ^ k) * 4 + (at_ref[1] ^ m)) * rows, 16)
            piece_ref[k * rows : (k + 1) * rows, :] = grads_ref[pl.ds(start, rows), :]


def attend_backward(cube, at_ref, d_ctx_ref, qkv_ref, probs_ref, w_ref, d_h_ref, grad_offset_ref, *refs):
    *piece_refs, turned_ref = refs
    heads, seq_len, _ = probs_ref.shape
    inner = d_ctx_ref.shape[1]
    span = grad_offset_ref.shape[1]
    flip = (
        lax.broadcasted_iota(jnp.int32, (seq_len, seq_len), 0)
        + lax.broadcasted_iota(jnp.int32, (seq_len, seq_len), 1)
        == seq_len - 1
    ).astype(bf16)
    grad_offset_ref[...] = jnp.zeros(grad_offset_ref.shape, f32)
    for at in range(heads):
        cols = lambda part: pl.ds(part * inner + at * HEAD, HEAD)
        d_ctx = d_ctx_ref[:, at * HEAD : (at + 1) * HEAD]
        probs = probs_ref[at]
        d_probs = dot(d_ctx, qkv_ref[:, cols(2)], 1, 1)
        row_delta = jnp.sum(probs * d_probs, axis=1, keepdims=True)
        d_scores = (probs * (d_probs - row_delta)).astype(bf16)
        turned_ref[cols(0), :] = (dot(qkv_ref[:, cols(1)], d_scores, 0, 1) * 0.125).astype(bf16)
        turned_ref[cols(1), :] = (dot(qkv_ref[:, cols(0)], d_scores, 0, 0) * 0.125).astype(bf16)
        turned_ref[cols(2), :] = dot(d_ctx, probs.astype(bf16), 0, 0).astype(bf16)
        flipped = jnp.concatenate(
            [dot(flip, d_scores, 1, 0), jnp.zeros((seq_len, span - seq_len), f32)], axis=1
        )
        lined = pltpu.roll(flipped, 0, 1, stride=1, stride_axis=0)
        grad_offset_ref[at : at + 1, :] = jnp.sum(lined, axis=0, keepdims=True)
    size = piece_refs[0].shape[0]
    for m, piece_ref in enumerate(piece_refs):
        start = pl.multiple_of((at_ref[1] ^ m) * size, 16) if cube else 0
        piece_ref[...] = turned_ref[pl.ds(start, size), :]
    d_h_ref[...] = dot(turned_ref[...], w_ref[...], 0, 1).astype(bf16)


def qkv_terms(at_ref, turned_ref, small_ref, router_ref, *refs):
    mine_ref, peer_ref, piece_refs, block_refs, grads_ref = refs[0], refs[1], refs[2:6], refs[6:10], refs[10]
    half = mine_ref.shape[0] // 3
    from_mine = from_peer = 0.0
    for m in range(1, 4):
        rows = slice((m - 1) * half, m * half)
        from_mine = from_mine + dot(mine_ref[rows, :], piece_refs[m][...], 1, 1)
        from_peer = from_peer + dot(peer_ref[rows, :], piece_refs[m][...], 1, 1)
    own = dot(turned_ref[...], piece_refs[0][...], 1, 1)
    first_core = at_ref[2] == 0
    grads_ref[:half, :] = (own[:half] + jnp.where(first_core, from_mine, from_peer)).astype(bf16)
    grads_ref[half:, :] = (own[half:] + jnp.where(first_core, from_peer, from_mine)).astype(bf16)
    rows, size = block_refs[0].shape[0] - 8, grads_ref.shape[1]
    width = small_ref.shape[1]
    part = width // 4
    for k, block_ref in enumerate(block_refs):
        block_ref[rows:, :width] = small_ref[...].astype(bf16)
        router = jnp.zeros((router_ref.shape[0], part), f32)
        for z in range(4):
            router = jnp.where((at_ref[0] ^ k) == z, router_ref[:, z * part : (z + 1) * part], router)
        for i in range(2):
            low = width + i * part
            block_ref[rows:, low : low + part] = router[i * 8 : (i + 1) * 8].astype(bf16)
        for m in range(4):
            start = ((at_ref[0] ^ k) * 4 + (at_ref[1] ^ m)) * rows
            block_ref[:rows, m * size : (m + 1) * size] = grads_ref[pl.ds(pl.multiple_of(start, 16), rows), :]


def pair_sum(refs):
    a, b, c, d = (ref[...].astype(f32) for ref in refs)
    return (a + b) + (c + d)


def join_line(at_ref, *refs):
    total = pair_sum(refs[:4])
    rows = refs[4].shape[0]
    size = total.shape[1] // 4
    width = size * 8 // 3
    part = width // 16
    extra = total[rows:]
    for m, piece_ref in enumerate(refs[4:]):
        piece_ref[...] = jnp.zeros(piece_ref.shape, bf16)
        piece_ref[:, :size] = total[:rows, m * size : (m + 1) * size].astype(bf16)
        for i in range(2):
            for j in range(width // 128):
                line = extra[6 + i : 7 + i, j * 128 : (j + 1) * 128]
                piece_ref[i * 8 + j : i * 8 + j + 1, 384:] = line.astype(bf16)
            router = jnp.zeros((8, part), f32)
            for row in range(4):
                low = width + i * 4 * part + row * part
                router = jnp.where((at_ref[1] ^ m) == row, extra[:, low : low + part], router)
            piece_ref[32 + i * 8 : 40 + i * 8, 384 : 384 + part] = router.astype(bf16)
        piece_ref[16:24, 384:] = extra[:, :128].astype(bf16)


def join_plane(at_ref, *refs):
    piece_refs, (out_ref, gain_one_ref, gain_two_ref, rel_ref, router_ref, line_ref) = refs[:4], refs[4:]
    size = line_ref.shape[1] // 4
    for quarter in range(4):
        piece = 0.0
        for m, piece_ref in enumerate(piece_refs):
            piece = jnp.where((at_ref[1] ^ m) == quarter, piece_ref[:, :size].astype(f32), piece)
        line_ref[:, quarter * size : (quarter + 1) * size] = piece
    inner = out_ref.shape[2]
    for part in range(3):
        out_ref[part] = line_ref[:, part * inner : (part + 1) * inner]
    extra = pair_sum([ref.at[:, 384:] for ref in piece_refs])
    for i, gain_ref in enumerate((gain_one_ref, gain_two_ref)):
        for j in range(gain_ref.shape[1] // 128):
            gain_ref[:, j * 128 : (j + 1) * 128] = extra[i * 8 + j : i * 8 + j + 1]
    rel_ref[...] = extra[16 : 16 + rel_ref.shape[0], : rel_ref.shape[1]]
    router_ref[...] = extra[32 : 32 + router_ref.shape[0], : router_ref.shape[1]]


def join_blocks(*refs):
    total = pair_sum(refs[:4])
    rows = total.shape[0] // 4
    for k, block_ref in enumerate(refs[4:]):
        block_ref[...] = total[k * rows : (k + 1) * rows].astype(bf16)


def finish(
    d_h_ref, peer_ref, x_ref, d_x_ref, gain_ref, gain_grad_ref, grad_offset_ref, hot_ref, grad_x_ref, small_ref,
):
    d_h = d_h_ref[...].astype(f32) + peer_ref[...].astype(f32)
    x_float = x_ref[...].astype(f32)
    scale = rms_scale(x_float)
    normed = x_float * scale
    d_norm = d_h * gain_ref[...]
    grad_x = d_x_ref[...] + scale * (
        d_norm - normed * jnp.mean(d_norm * normed, axis=-1, keepdims=True)
    )
    grad_x_ref[...] = grad_x.astype(bf16)
    heads, buckets = grad_offset_ref.shape[0] - 2, hot_ref.shape[1]
    small_ref[...] = jnp.zeros(small_ref.shape, f32)
    grad_rel = lax.dot_general(
        grad_offset_ref[...], hot_ref[...], (((1,), (0,)), ((), ())), precision=highest, preferred_element_type=f32
    )
    small_ref[:, :buckets] = grad_rel
    small_ref[heads : heads + 1, :] = jnp.sum(d_h * normed, axis=0, keepdims=True)
    small_ref[heads + 1 : heads + 2, :] = gain_grad_ref[...]


def expert_grads(rows_ref, d_y_ref, act_ref, d_pre_ref, down_ref, up_ref, held_ref, sems):
    (hidden, width), steps = down_ref.shape, 3
    copies = []
    chunk = 0
    for left_ref, right_ref, out_ref in ((act_ref, d_y_ref, down_ref), (rows_ref, d_pre_ref, up_ref)):
        count = out_ref.shape[0] // steps
        for at in range(steps):
            rows = pl.ds(at * count, count)
            slot = chunk % 3
            if chunk >= 3:
                copies[chunk - 3].wait()
            held = held_ref.at[slot, pl.ds(0, count), pl.ds(0, out_ref.shape[1])]
            held[...] = dot(left_ref[:, rows], right_ref[...], 0, 0)
            copies.append(pltpu.make_async_copy(held, out_ref.at[rows, :], sems.at[chunk]))
            copies[-1].start()
            chunk += 1
    for copy in copies[-3:]:
        copy.wait()


def experts_pad(experts):
    return -(-experts // 128) * 128


def make_per_device(mesh):
    n_ex, n_row = mesh.shape["ex"], mesh.shape["row"]
    groups = n_ex * n_row

    def hop(values, axis, step):
        return lax.ppermute(values, axis, [(i, i ^ step) for i in range(mesh.shape[axis])])

    def whole_cube(rows):
        return n_ex == 4 and n_row == 4 and rows == 48

    def gather_blocks(shard):
        rows, width = shard.shape
        if whole_cube(rows):
            line = [shard] + [hop(shard, "ex", k) for k in (1, 2, 3)]
            xs = [hop(part, "row", 1) for part in line]
            ys = [hop(part, "row", 2) for part in line]
            diagonal = [
                hop(ys[k], "row", 1) if k % 2 else hop(xs[k], "row", 2) for k in range(4)
            ]
            return [*line, *xs, *ys, *diagonal]
        part = lax.all_gather(shard, "ex", axis=0)
        part = jnp.broadcast_to(part[None], (n_row, n_ex, rows, width))
        part = lax.all_to_all(part, "row", split_axis=0, concat_axis=0, tiled=True)
        return [part.transpose(1, 0, 2, 3).reshape(groups * rows, width)]

    def scatter_groups(grads, rows):
        part = grads.astype(bf16).reshape(n_ex, n_row, rows, -1).transpose(1, 0, 2, 3)
        part = lax.all_to_all(part, "row", split_axis=0, concat_axis=0, tiled=True)
        part = jnp.sum(part.astype(f32), axis=0).astype(bf16)
        part = lax.all_to_all(part, "ex", split_axis=0, concat_axis=0, tiled=True)
        return jnp.sum(part.astype(f32), axis=0)

    def plane_hops(parts):
        return [hop(part, "row", m + 1) for m, part in enumerate(parts)]

    def line_hops(parts):
        return [hop(part, "ex", k + 1) for k, part in enumerate(parts)]

    def sum_groups(values):
        for axis in ("row", "ex"):
            step = 1
            while step < mesh.shape[axis]:
                values = values + hop(values, axis, step)
                step *= 2
        return values

    def per_device(
        x_in,
        gain_attn,
        w_qkv,
        rel_bias,
        w_out,
        gain_ffn,
        w_router,
        w_up,
        w_down,
        seg_ids,
        expert_ids,
        slot_ids,
        drop_flags,
        d_out,
    ):
        seq_len, width = x_in.shape
        heads_here = rel_bias.shape[1]
        inner = w_qkv.shape[2]
        own_rows = w_qkv.shape[1]
        experts = w_router.shape[1]
        wide = inner + experts_pad(experts)
        half = d_out.shape[1]
        hidden = w_up.shape[2]
        device_at = jnp.stack([lax.axis_index(axis).astype(jnp.int32) for axis in ("ex", "row", "col")])
        device_at, w_qkv = lax.optimization_barrier((device_at, w_qkv))
        cube = whole_cube(own_rows)
        capacity = 5 * seq_len // (4 * experts)
        tight = cube and experts == 16 and capacity == 20 and width == 768
        slots = capacity if tight else -(-capacity // 8) * 8
        slot_total = experts * slots
        packed_slots = (experts, slots * width // 128, 128) if tight else (slot_total, width)
        exchange = packed_slots if tight else (experts, slots, width)
        slot_scratch = (
            pltpu.VMEM((slot_total, width), bf16),
            pltpu.VMEM((slot_total, width), bf16),
            pltpu.VMEM((experts * 24, 128), f32),
        )
        gather_order = GATHER_ORDER if cube else None

        (packed,) = vmem_call(
            pack_weights,
            (shape((own_rows, 3 * inner + wide), bf16),),
            0,
            w_qkv,
            w_out.T,
            w_router.T,
        )
        blocks = gather_blocks(packed)
        normed_turned, normed_mine = vmem_call(
            turn_normed,
            (shape((width, seq_len), bf16), shape((half, seq_len), bf16)),
            0,
            x_in,
            gain_attn[None],
            scalars=(device_at,),
        )
        up_w = w_up[0].astype(bf16)
        down_w = w_down[0].astype(bf16)
        *blocks, up_w, down_w, normed_mine, normed_turned = lax.optimization_barrier(
            (*blocks, up_w, down_w, normed_mine, normed_turned)
        )
        g_peer = swap_cores(d_out)

        span = 2 * seq_len
        offsets = jnp.arange(span, dtype=jnp.int32) - (seq_len - 1)
        offset_hot = (
            bucket_of(offsets)[:, None] == jnp.arange(BUCKETS, dtype=jnp.int32)[None, :]
        ).astype(f32)
        per_offset = jnp.einsum("bh,ob->ho", rel_bias, offset_hot, precision=highest)
        square = seq_len * seq_len * heads_here * HEAD
        attn_part, qkv, probs, context, qkv_w, out_w, router_w = vmem_call(
            functools.partial(attend_forward, gather_order),
            (
                shape((seq_len, width), bf16),
                shape((seq_len, 3 * inner), bf16),
                shape((heads_here, seq_len, seq_len), f32),
                shape((seq_len, inner), bf16),
                shape((width, 3 * inner), bf16),
                shape((width, inner), bf16),
                shape((width, wide - inner), bf16),
            ),
            8 * seq_len * width * inner + 4 * square,
            x_in,
            gain_attn[None],
            per_offset,
            seg_ids,
            *blocks,
            scalars=(device_at,),
        )
        attn_peer = swap_cores(attn_part)
        slot_of = expert_ids * slots + slot_ids
        if tight:
            spare_of = experts * 16 + expert_ids * 4 + slot_ids - 16
            slot_of = jnp.where(slot_ids < 16, expert_ids * 16 + slot_ids, spare_of)
        slot_of = jnp.where(drop_flags == 1, slot_total, slot_of)[None]
        (send,) = vmem_call(
            dispatch,
            (shape(packed_slots, bf16),),
            2 * seq_len * slot_total * width,
            x_in,
            attn_part,
            attn_peer,
            gain_ffn[None],
            slot_of,
            d_out,
            scalars=(device_at,),
        )
        got = lax.all_to_all(send.reshape(exchange), ("ex", "row"), 0, 0, tiled=True).reshape(packed_slots)
        if cube:
            later_normed, got = lax.optimization_barrier((normed_mine, got))
            normed_hops = plane_hops([later_normed] * 2)
        crossing, mine, router_probs, gate_part, rows, d_y, act_b, d_pre = vmem_call(
            functools.partial(run_expert, experts, n_row),
            (
                shape((slot_total, width), bf16),
                shape((slot_total, width), f32),
                shape((slot_total, experts), f32),
                shape((slot_total, 1), f32),
                shape((slot_total, width), bf16),
                shape((slot_total, width), bf16),
                shape((slot_total, hidden), bf16),
                shape((slot_total, hidden), bf16),
            ),
            8 * slot_total * width * hidden,
            got,
            swap_cores(got),
            router_w,
            up_w,
            down_w,
            scalars=(device_at,),
            scratch=(pltpu.VMEM((slot_total, width), f32), *slot_scratch),
        )
        if cube:
            crossing, gate_part, g_peer, *normed_hops = lax.optimization_barrier(
                (crossing, gate_part, g_peer, *normed_hops)
            )
            from_x, from_y = normed_hops
            normed_hops += [hop(from_x[: half // 2], "row", 2), hop(from_y[half // 2 :], "row", 1)]
        back, grad_router = vmem_call(
            functools.partial(settle, n_row),
            (shape(packed_slots, bf16), shape((experts, width), f32)),
            2 * slot_total * half * experts,
            mine,
            swap_cores(crossing),
            router_probs,
            gate_part,
            swap_cores(gate_part),
            router_w,
            rows,
            scalars=(device_at,),
        )
        if cube:
            back, *normed_hops = lax.optimization_barrier((back, *normed_hops))
        home = lax.all_to_all(back.reshape(exchange), ("ex", "row"), 0, 0, tiled=True).reshape(packed_slots)
        layer_out, d_h_mine = vmem_call(
            arrive,
            (shape((seq_len, half), bf16), shape((seq_len, half), bf16)),
            2 * seq_len * slot_total * width,
            home,
            slot_of,
            x_in,
            attn_part,
            attn_peer,
            scalars=(device_at,),
            scratch=slot_scratch[1:],
        )
        def grads_of_expert(rows, d_y, act_b, d_pre):
            return pl.pallas_call(
                expert_grads,
                out_shape=(shape((hidden, width), f32), shape((width, hidden), f32)),
                in_specs=[pl.BlockSpec(memory_space=pltpu.VMEM)] * 4,
                out_specs=[pl.BlockSpec(memory_space=pltpu.HBM)] * 2,
                scratch_shapes=[
                    pltpu.VMEM((3, max(hidden, width) // 3, max(hidden, width)), f32),
                    pltpu.SemaphoreType.DMA((6,)),
                ],
                compiler_params=pltpu.CompilerParams(vmem_limit_bytes=24 * 2**20),
                cost_estimate=pl.CostEstimate(
                    flops=4 * slot_total * width * hidden, bytes_accessed=12 * width * hidden, transcendentals=0
                ),
            )(rows, d_y, act_b, d_pre)

        quarter = (width // 4, 3 * inner // 4) if cube else (width, 3 * inner)
        pieces = 4 if cube else 1
        d_x_one, grad_gain_ffn, d_context, *out_pieces = vmem_call(
            functools.partial(come_home, cube),
            (
                shape((seq_len, width), f32),
                shape((1, width), f32),
                shape((seq_len, inner), bf16),
                *[shape((quarter[0], inner), bf16)] * pieces,
            ),
            4 * seq_len * width * inner,
            d_h_mine,
            swap_cores(d_h_mine),
            x_in,
            attn_part,
            attn_peer,
            d_out,
            g_peer,
            gain_ffn[None],
            out_w,
            context,
            scalars=(device_at,),
            scratch=(pltpu.VMEM((width, inner), bf16),),
        )
        d_h_part, grad_offset, *d_qkv_turned = vmem_call(
            functools.partial(attend_backward, cube),
            (
                shape((seq_len, width), bf16),
                shape((heads_here + 2, span), f32),
                *[shape((quarter[1], seq_len), bf16)] * pieces,
            ),
            6 * seq_len * width * inner + 10 * square,
            d_context,
            qkv,
            probs,
            qkv_w,
            scalars=(device_at,),
            scratch=(pltpu.VMEM((3 * inner, seq_len), bf16),),
        )
        grad_x, small = vmem_call(
            finish,
            (shape((seq_len, width), bf16), shape((heads_here + 2, width), f32)),
            0,
            d_h_part,
            swap_cores(d_h_part),
            x_in,
            d_x_one,
            gain_attn[None],
            grad_gain_ffn,
            grad_offset,
            offset_hot,
        )
        if cube:
            *normed_hops, _ = lax.optimization_barrier((*normed_hops, d_h_part))
            normed_near = jnp.concatenate(normed_hops, axis=0)
            normed_peer = swap_cores(normed_near)
            terms = vmem_call(
                qkv_terms,
                [shape((own_rows + 8, 3 * inner), bf16)] * 4,
                6 * seq_len * width * inner,
                normed_turned,
                small,
                grad_router,
                normed_near,
                normed_peer,
                d_qkv_turned[0],
                *plane_hops(d_qkv_turned[1:]),
                scalars=(device_at,),
                scratch=(pltpu.VMEM((width, quarter[1]), bf16),),
            )
            line = line_hops(terms[1:])
            first_line = line[0]
            rows, d_y, act_b, d_pre, _ = lax.optimization_barrier((rows, d_y, act_b, d_pre, terms[0]))
            grad_down, grad_up = grads_of_expert(rows, d_y, act_b, d_pre)
            *line, grad_down, grad_up = lax.optimization_barrier((*line, grad_down, grad_up))
            split = vmem_call(
                join_line,
                [shape((own_rows, 512), bf16)] * 4,
                0,
                terms[0],
                *line,
                scalars=(device_at,),
            )
            last = plane_hops(split[1:])
            grad_qkv, gain_one, gain_two, grad_rel, grad_router = vmem_call(
                join_plane,
                (
                    shape((3, own_rows, inner), f32),
                    shape((1, width), f32),
                    shape((1, width), f32),
                    shape((heads_here, BUCKETS), f32),
                    shape((experts, own_rows), f32),
                ),
                0,
                split[0],
                *last,
                scalars=(device_at,),
                scratch=(pltpu.VMEM((own_rows, 3 * inner), f32),),
            )
            *out_pieces, _ = lax.optimization_barrier((*out_pieces, first_line))
            out_hops = plane_hops(out_pieces[1:])
            out_blocks = vmem_call(
                join_blocks,
                [shape((own_rows, inner), bf16)] * 4,
                0,
                out_pieces[0],
                *out_hops,
            )
            *out_blocks, _ = lax.optimization_barrier((*out_blocks, last[0]))
            out_blocks = (out_blocks[0], *line_hops(out_blocks[1:]))
            grad_out = sum(part.astype(f32) for part in out_blocks)
        else:
            grad_down, grad_up = grads_of_expert(rows, d_y, act_b, d_pre)
            grad_qkv = scatter_groups(dot(normed_turned, d_qkv_turned[0], 1, 1), own_rows)
            grad_qkv = grad_qkv.reshape(own_rows, 3, inner).transpose(1, 0, 2)
            grad_out = scatter_groups(out_pieces[0], own_rows)
            small = sum_groups(jnp.concatenate([small, grad_router]))
            gain_one, gain_two = small[heads_here], small[heads_here + 1]
            grad_rel = small[:heads_here, :BUCKETS]
            own_at = (device_at[0] * n_row + device_at[1]) * own_rows
            grad_router = lax.dynamic_slice(small, (heads_here + 2, own_at), (experts, own_rows))
        return (
            layer_out,
            grad_x,
            gain_one.reshape(width),
            grad_qkv,
            grad_rel.T,
            grad_out.T,
            gain_two.reshape(width),
            grad_router.T,
            grad_up[None],
            grad_down[None],
        )

    return per_device


def solution(mesh):
    return jax.shard_map(
        make_per_device(mesh),
        mesh=mesh,
        in_specs=(
            P(("ex", "row"), None),
            P(),
            P(None, ("ex", "row"), "col"),
            P(None, "col"),
            P("col", ("ex", "row")),
            P(),
            P(("ex", "row"), None),
            P(("ex", "row"), None, "col"),
            P(("ex", "row"), "col", None),
            P(("ex", "row"), None),
            P(("ex", "row")),
            P(("ex", "row")),
            P(("ex", "row")),
            P(("ex", "row"), "col"),
        ),
        out_specs=(
            P(("ex", "row"), "col"),
            P(("ex", "row"), None),
            P(),
            P(None, ("ex", "row"), "col"),
            P(None, "col"),
            P("col", ("ex", "row")),
            P(),
            P(("ex", "row"), None),
            P(("ex", "row"), None, "col"),
            P(("ex", "row"), "col", None),
        ),
        check_vma=False,
    )
```

```python
import functools
import math

import jax
import jax.numpy as jnp
from jax import lax
from jax.experimental import pallas as pl
from jax.experimental.pallas import tpu as pltpu
from jax.sharding import PartitionSpec as P

HEAD = 64
BUCKETS = 32

norm_eps = 1e-06
bucket_edges = (12, 16, 23, 32, 46, 64, 91)
highest = lax.Precision.HIGHEST
bf16 = jnp.bfloat16
f32 = jnp.float32

GATHER_ORDER = tuple(((k, m),) for m in range(4) for k in range(4))

def bucket_of(offset):
    distance = jnp.abs(offset)
    far_part = jnp.zeros(distance.shape, jnp.int32)
    for edge_at in bucket_edges:
        far_part = far_part + (distance >= edge_at).astype(jnp.int32)
    inside = jnp.where(distance < 8, distance, far_part + jnp.int32(8))
    upper = jnp.where(offset > 0, jnp.int32(BUCKETS // 2), jnp.int32(0))
    return inside + upper


def rms_scale(values):
    return lax.rsqrt(jnp.mean(values * values, axis=-1, keepdims=True) + norm_eps)


def dot(a, b, ca, cb):
    return lax.dot_general(a, b, (((ca,), (cb,)), ((), ())), preferred_element_type=f32)


def swap_cores(values):
    return lax.ppermute(values, "col", [(0, 1), (1, 0)])


def shape(dims, dtype):
    return jax.ShapeDtypeStruct(tuple(dims), dtype)


def vmem_call(kernel, out_shape, flops, *args, scalars=(), scratch=(), limit=12):
    nbytes = sum(math.prod(v.shape) * v.dtype.itemsize for v in (*args, *out_shape))
    spec = pl.BlockSpec(memory_space=pltpu.VMEM)
    limit = limit if nbytes < 16 * 2**20 else 48
    return pl.pallas_call(
        kernel,
        out_shape=out_shape,
        in_specs=[pl.BlockSpec(memory_space=pltpu.SMEM)] * len(scalars) + [spec] * len(args),
        out_specs=[spec] * len(out_shape),
        scratch_shapes=scratch,
        compiler_params=pltpu.CompilerParams(vmem_limit_bytes=limit * 2**20),
        cost_estimate=pl.CostEstimate(flops=flops, bytes_accessed=nbytes, transcendentals=0),
    )(*scalars, *args)


def block_rows(at_ref, order, count):
    if order is None:
        return [pl.ds(0, count)]
    ex_at, row_at = at_ref[0], at_ref[1]
    return [
        pl.ds(pl.multiple_of(((ex_at ^ k) * 4 + (row_at ^ m)) * count, 16), count)
        for part in order
        for k, m in part
    ]


def eye(size):
    dims = (size, size)
    same = lax.broadcasted_iota(jnp.int32, dims, 0) == lax.broadcasted_iota(jnp.int32, dims, 1)
    return same.astype(bf16)


def pack_weights(qkv_ref, out_turned_ref, router_turned_ref, packed_ref):
    inner, experts = qkv_ref.shape[2], router_turned_ref.shape[0]
    for part in range(3):
        packed_ref[:, part * inner : (part + 1) * inner] = qkv_ref[part].astype(bf16)
    packed_ref[:, 3 * inner : 4 * inner] = out_turned_ref[...].astype(bf16)
    packed_ref[:, 4 * inner :] = jnp.zeros((packed_ref.shape[0], packed_ref.shape[1] - 4 * inner), bf16)
    router = dot(router_turned_ref[...].astype(bf16), eye(experts), 0, 0)
    packed_ref[:, 4 * inner : 4 * inner + experts] = router.astype(bf16)


def attend_forward(order, at_ref, x_ref, gain_ref, offset_ref, seg_ref, *refs):
    *block_refs, part_ref, qkv_ref, probs_ref, ctx_ref, w_ref, out_w_ref, router_ref, turned_ref, half_ref = refs
    seq_len = x_ref.shape[0]
    heads, inner = probs_ref.shape[0], ctx_ref.shape[1]
    for rows, block_ref in zip(block_rows(at_ref, order, block_refs[0].shape[0]), block_refs):
        w_ref[rows, :] = block_ref[:, : 3 * inner]
        out_w_ref[rows, :] = block_ref[:, 3 * inner : 4 * inner]
        router_ref[rows, :] = block_ref[:, 4 * inner :]
    x_float = x_ref[...].astype(f32)
    h_one = (x_float * rms_scale(x_float) * gain_ref[...].reshape(1, -1)).astype(bf16)
    turned_ref[...] = dot(h_one, eye(seq_len), 0, 0).astype(bf16)
    half = half_ref.shape[0]
    half_ref[...] = jnp.where(at_ref[2] == 0, turned_ref[:half, :], turned_ref[half:, :])
    documents = lax.broadcasted_iota(jnp.int32, (8, seq_len), 0) == seg_ref[...]
    same_doc = dot(documents.astype(bf16), documents.astype(bf16), 0, 0) > 0.5
    qkv_ref[...] = dot(h_one, w_ref[...], 1, 0).astype(bf16)
    span = offset_ref.shape[1]
    for at in range(heads):
        take = lambda part: qkv_ref[:, part * inner + at * HEAD : part * inner + (at + 1) * HEAD]
        spread = jnp.broadcast_to(offset_ref[at : at + 1, :], (seq_len, span))
        bias = pltpu.roll(spread, span - seq_len + 1, 1, stride=1, stride_axis=0)[:, :seq_len]
        scores = jnp.where(same_doc, dot(take(0), take(1), 1, 1) * 0.125 + bias, -1e30)
        expo = jnp.exp(scores - jnp.max(scores, axis=1, keepdims=True))
        probs = expo / jnp.sum(expo, axis=1, keepdims=True)
        probs_ref[at] = probs
        ctx = dot(probs.astype(bf16), take(2), 1, 0)
        ctx_ref[:, at * HEAD : (at + 1) * HEAD] = ctx.astype(bf16)
    part_ref[...] = dot(ctx_ref[...], out_w_ref[...], 1, 1).astype(bf16)


def spare_rows(experts, chunk):
    dims = (experts * 24, experts * 4)
    row, column = lax.broadcasted_iota(jnp.int32, dims, 0), lax.broadcasted_iota(jnp.int32, dims, 1)
    expert = lax.shift_right_logical(row * 2731, 16)
    inside = row - expert * 24
    wanted = expert * 4 + (inside - chunk * 4)
    return ((column == wanted) & (inside >= chunk * 4) & (inside < chunk * 4 + 4)).astype(bf16)


def pack_slots(values, packed_ref):
    if len(packed_ref.shape) == 2:
        packed_ref[...] = values.astype(bf16)
        return
    experts, chunks = packed_ref.shape[0], values.shape[1] // 128
    values = values.astype(bf16)
    spare = 0.0
    for c in range(chunks):
        chunk = values[:, c * 128 : (c + 1) * 128]
        for e in range(experts):
            packed_ref[e, c * 16 : (c + 1) * 16, :] = chunk[e * 16 : (e + 1) * 16]
        spare = spare + dot(spare_rows(experts, c), chunk[experts * 16 :], 1, 0)
    for e in range(experts):
        packed_ref[e, chunks * 16 :, :] = spare[e * 24 : (e + 1) * 24].astype(bf16)


def unpack_slots(packed_ref, low, target_ref, spare_ref):
    experts, chunks = packed_ref.shape[0], target_ref.shape[1] // 128
    first = (packed_ref.shape[1] - 24) // 16 * 16
    for e in range(experts):
        spare_ref[e * 24 : (e + 1) * 24, :] = packed_ref[e, first:, :].astype(f32)
    spare = spare_ref[...].astype(bf16)
    for c in range(chunks):
        lanes = slice(c * 128, (c + 1) * 128)
        for e in range(experts):
            rows = slice((low + c) * 16, (low + c + 1) * 16)
            target_ref[e * 16 : (e + 1) * 16, lanes] = packed_ref[e, rows, :]
        target_ref[experts * 16 :, lanes] = dot(spare_rows(experts, low + c), spare, 0, 0).astype(bf16)


def dispatch(at_ref, x_ref, part_ref, peer_ref, gain_ref, slot_ref, g_ref, send_ref):
    half = g_ref.shape[1]
    x_one = x_ref[...].astype(f32) + (part_ref[...].astype(f32) + peer_ref[...].astype(f32))
    h_two = (x_one * rms_scale(x_one) * gain_ref[...].reshape(1, -1)).astype(bf16)
    mine = jnp.where(at_ref[2] == 0, h_two[:, :half], h_two[:, half:])
    slots = send_ref.shape[0] * (1 if len(send_ref.shape) == 2 else 20)
    dims = (slots, x_ref.shape[0])
    place = (lax.broadcasted_iota(jnp.int32, dims, 0) == slot_ref[...]).astype(bf16)
    sent = jnp.concatenate([dot(place, mine, 1, 0), dot(place, g_ref[...], 1, 0)], axis=1)
    pack_slots(sent, send_ref)


def run_expert(
    experts, row_size, at_ref, got_ref, peer_ref, router_ref, up_ref, down_ref,
    cross_ref, mine_ref, probs_ref, gate_part_ref, rows_ref, d_y_ref, act_ref, d_pre_ref, d_in_ref,
    got_rows_ref, peer_rows_ref, spare_ref,
):
    half = rows_ref.shape[1] // 2
    if len(got_ref.shape) == 3:
        unpack_slots(got_ref, 0, got_rows_ref, spare_ref)
        unpack_slots(peer_ref, 0, peer_rows_ref, spare_ref)
        got_ref, peer_ref = got_rows_ref, peer_rows_ref
    hidden = up_ref.shape[1]
    first_core = at_ref[2] == 0
    for at, refs in ((0, (got_ref, peer_ref)), (1, (peer_ref, got_ref))):
        pick = lambda lo: jnp.where(first_core, refs[0][:, lo : lo + half], refs[1][:, lo : lo + half])
        rows_ref[:, at * half : (at + 1) * half] = pick(0)
        d_y_ref[:, at * half : (at + 1) * half] = pick(half)
    rows, g_rows = rows_ref[...], d_y_ref[...].astype(f32)
    logits = dot(rows, router_ref[...], 1, 0)[:, :experts]
    expo = jnp.exp(logits - jnp.max(logits, axis=1, keepdims=True))
    probs = expo / jnp.sum(expo, axis=1, keepdims=True)
    probs_ref[...] = probs
    expert_at = at_ref[0] * row_size + at_ref[1]
    chosen = lax.broadcasted_iota(jnp.int32, probs.shape, 1) == expert_at
    gate = jnp.sum(jnp.where(chosen, probs, 0.0), axis=1, keepdims=True)
    d_y_ref[...] = (g_rows * gate).astype(bf16)
    step = 512 if hidden % 512 == 0 else hidden
    y_part = None
    for lo in range(0, hidden, step):
        cols = pl.ds(lo, step)
        pre_act = dot(rows_ref[...], up_ref[:, cols], 1, 0)
        cdf = 0.5 * (1.0 + lax.erf(pre_act * (1.0 / math.sqrt(2.0))))
        pdf = jnp.exp(-0.5 * pre_act * pre_act) * (1.0 / math.sqrt(2.0 * math.pi))
        act = (pre_act * cdf).astype(bf16)
        act_ref[:, cols] = act
        y_more = dot(act, down_ref[cols, :], 1, 0)
        d_pre = (dot(d_y_ref[...], down_ref[cols, :], 1, 1) * (cdf + pre_act * pdf)).astype(bf16)
        d_pre_ref[:, cols] = d_pre
        d_more = dot(d_pre, up_ref[:, cols], 1, 1)
        if lo == 0:
            y_part = y_more
            d_in_ref[...] = d_more
        else:
            y_part = y_part + y_more
            d_in_ref[...] += d_more
    gate_part = jnp.sum(g_rows * y_part, axis=1, keepdims=True)
    high = gate_part.astype(bf16)
    low = (gate_part - high.astype(f32)).astype(bf16)
    gate_part_ref[...] = high.astype(f32) + low.astype(f32)
    lane = lax.broadcasted_iota(jnp.int32, (rows.shape[0], 128), 1)
    beside = jnp.where(lane == 0, high.astype(f32), jnp.where(lane == 1, low.astype(f32), 0.0))
    cross_ref[:, 2 * half :] = beside.astype(bf16)
    d_in = d_in_ref[...]
    mine_ref[:, :half] = jnp.where(first_core, y_part[:, :half], y_part[:, half:])
    mine_ref[:, half:] = jnp.where(first_core, d_in[:, :half], d_in[:, half:])
    cross_ref[:, :half] = jnp.where(first_core, y_part[:, half:], y_part[:, :half]).astype(bf16)
    cross_ref[:, half : 2 * half] = jnp.where(first_core, d_in[:, half:], d_in[:, :half]).astype(bf16)


def settle(
    row_size, at_ref, mine_ref, crossed_ref, probs_ref, gate_part_ref, router_ref, rows_ref,
    back_ref, grad_router_ref,
):
    half = mine_ref.shape[1] // 2
    probs = probs_ref[...]
    expert_at = at_ref[0] * row_size + at_ref[1]
    chosen = (lax.broadcasted_iota(jnp.int32, probs.shape, 1) == expert_at).astype(f32)
    gate = jnp.sum(probs * chosen, axis=1, keepdims=True)
    beside = crossed_ref[:, 2 * half :].astype(f32)
    d_gate = gate_part_ref[...] + (beside[:, 0:1] + beside[:, 1:2])
    d_logits = (d_gate * gate * (chosen - probs)).astype(bf16)
    router_w = router_ref[...][:, : probs.shape[1]]
    router_mine = jnp.where(at_ref[2] == 0, router_w[:half], router_w[half:])
    y_gated = gate * (mine_ref[:, :half] + crossed_ref[:, :half].astype(f32))
    d_in = mine_ref[:, half:] + crossed_ref[:, half : 2 * half].astype(f32) + dot(d_logits, router_mine, 1, 1)
    pack_slots(jnp.concatenate([y_gated, d_in], axis=1), back_ref)
    grad_router_ref[...] = dot(d_logits, rows_ref[...], 0, 0)


def arrive(at_ref, home_ref, slot_ref, x_ref, part_ref, peer_ref, layer_ref, d_h_ref, rows_ref, spare_ref):
    half = layer_ref.shape[1]
    if len(home_ref.shape) == 3:
        unpack_slots(home_ref, 0, rows_ref, spare_ref)
        home_ref = rows_ref
    dims = (home_ref.shape[0], x_ref.shape[0])
    place = (lax.broadcasted_iota(jnp.int32, dims, 0) == slot_ref[...]).astype(bf16)
    d_h_ref[...] = dot(place, home_ref[:, half:], 0, 0).astype(bf16)
    y_home = dot(place, home_ref[:, :half], 0, 0)
    mine = lambda ref: jnp.where(at_ref[2] == 0, ref[:, :half], ref[:, half:]).astype(f32)
    layer_ref[...] = (mine(x_ref) + (mine(part_ref) + mine(peer_ref)) + y_home).astype(bf16)


def come_home(
    cube, at_ref, mine_ref, peer_ref, x_ref, part_ref, part_peer_ref, g_ref, g_peer_ref,
    gain_ref, out_w_ref, ctx_ref, d_x_ref, gain_grad_ref, d_ctx_ref, *refs,
):
    *piece_refs, grads_ref = refs
    first_core = at_ref[2] == 0
    both = lambda a, b: jnp.concatenate(
        [jnp.where(first_core, a, b), jnp.where(first_core, b, a)], axis=1
    )
    d_h = both(mine_ref[...], peer_ref[...]).astype(f32)
    x_one = x_ref[...].astype(f32) + (part_ref[...].astype(f32) + part_peer_ref[...].astype(f32))
    g_full = both(g_ref[...], g_peer_ref[...]).astype(f32)
    scale = rms_scale(x_one)
    normed = x_one * scale
    gain_grad_ref[...] = jnp.sum(d_h * normed, axis=0, keepdims=True)
    d_norm = d_h * gain_ref[...].reshape(1, -1)
    d_x = g_full + scale * (d_norm - normed * jnp.mean(d_norm * normed, axis=-1, keepdims=True))
    d_x_ref[...] = d_x
    d_x_b = d_x.astype(bf16)
    d_ctx_ref[...] = dot(d_x_b, out_w_ref[...], 1, 0).astype(bf16)
    grads_ref[...] = dot(d_x_b, ctx_ref[...], 0, 0).astype(bf16)
    rows = grads_ref.shape[0] // 16
    for m, piece_ref in enumerate(piece_refs):
        if not cube:
            piece_ref[...] = grads_ref[...]
            continue
        for k in range(4):
            start = pl.multiple_of(((at_ref[0] ^ k) * 4 + (at_ref[1] ^ m)) * rows, 16)
            piece_ref[k * rows : (k + 1) * rows, :] = grads_ref[pl.ds(start, rows), :]


def attend_backward(cube, at_ref, d_ctx_ref, qkv_ref, probs_ref, w_ref, d_h_ref, grad_offset_ref, *refs):
    *piece_refs, turned_ref = refs
    heads, seq_len, _ = probs_ref.shape
    inner = d_ctx_ref.shape[1]
    span = grad_offset_ref.shape[1]
    flip = (
        lax.broadcasted_iota(jnp.int32, (seq_len, seq_len), 0)
        + lax.broadcasted_iota(jnp.int32, (seq_len, seq_len), 1)
        == seq_len - 1
    ).astype(bf16)
    grad_offset_ref[...] = jnp.zeros(grad_offset_ref.shape, f32)
    for at in range(heads):
        cols = lambda part: pl.ds(part * inner + at * HEAD, HEAD)
        d_ctx = d_ctx_ref[:, at * HEAD : (at + 1) * HEAD]
        probs = probs_ref[at]
        d_probs = dot(d_ctx, qkv_ref[:, cols(2)], 1, 1)
        row_delta = jnp.sum(probs * d_probs, axis=1, keepdims=True)
        d_scores = (probs * (d_probs - row_delta)).astype(bf16)
        turned_ref[cols(0), :] = (dot(qkv_ref[:, cols(1)], d_scores, 0, 1) * 0.125).astype(bf16)
        turned_ref[cols(1), :] = (dot(qkv_ref[:, cols(0)], d_scores, 0, 0) * 0.125).astype(bf16)
        turned_ref[cols(2), :] = dot(d_ctx, probs.astype(bf16), 0, 0).astype(bf16)
        flipped = jnp.concatenate(
            [dot(flip, d_scores, 1, 0), jnp.zeros((seq_len, span - seq_len), f32)], axis=1
        )
        lined = pltpu.roll(flipped, 0, 1, stride=1, stride_axis=0)
        grad_offset_ref[at : at + 1, :] = jnp.sum(lined, axis=0, keepdims=True)
    size = piece_refs[0].shape[0]
    for m, piece_ref in enumerate(piece_refs):
        start = pl.multiple_of((at_ref[1] ^ m) * size, 16) if cube else 0
        piece_ref[...] = turned_ref[pl.ds(start, size), :]
    d_h_ref[...] = dot(turned_ref[...], w_ref[...], 0, 1).astype(bf16)


def qkv_terms(at_ref, turned_ref, small_ref, router_ref, *refs):
    mine_ref, peer_ref, piece_refs, block_refs, grads_ref = refs[0], refs[1], refs[2:6], refs[6:10], refs[10]
    half = mine_ref.shape[0] // 3
    from_mine = from_peer = 0.0
    for m in range(1, 4):
        rows = slice((m - 1) * half, m * half)
        from_mine = from_mine + dot(mine_ref[rows, :], piece_refs[m][...], 1, 1)
        from_peer = from_peer + dot(peer_ref[rows, :], piece_refs[m][...], 1, 1)
    own = dot(turned_ref[...], piece_refs[0][...], 1, 1)
    first_core = at_ref[2] == 0
    grads_ref[:half, :] = (own[:half] + jnp.where(first_core, from_mine, from_peer)).astype(bf16)
    grads_ref[half:, :] = (own[half:] + jnp.where(first_core, from_peer, from_mine)).astype(bf16)
    rows, size = block_refs[0].shape[0] - 8, grads_ref.shape[1]
    width = small_ref.shape[1]
    part = width // 4
    for k, block_ref in enumerate(block_refs):
        block_ref[rows:, :width] = small_ref[...].astype(bf16)
        router = jnp.zeros((router_ref.shape[0], part), f32)
        for z in range(4):
            router = jnp.where((at_ref[0] ^ k) == z, router_ref[:, z * part : (z + 1) * part], router)
        for i in range(2):
            low = width + i * part
            block_ref[rows:, low : low + part] = router[i * 8 : (i + 1) * 8].astype(bf16)
        for m in range(4):
            start = ((at_ref[0] ^ k) * 4 + (at_ref[1] ^ m)) * rows
            block_ref[:rows, m * size : (m + 1) * size] = grads_ref[pl.ds(pl.multiple_of(start, 16), rows), :]


def pair_sum(refs):
    a, b, c, d = (ref[...].astype(f32) for ref in refs)
    return (a + b) + (c + d)


def join_line(at_ref, *refs):
    total = pair_sum(refs[:4])
    rows = refs[4].shape[0]
    size = total.shape[1] // 4
    width = size * 8 // 3
    part = width // 16
    extra = total[rows:]
    for m, piece_ref in enumerate(refs[4:]):
        piece_ref[...] = jnp.zeros(piece_ref.shape, bf16)
        piece_ref[:, :size] = total[:rows, m * size : (m + 1) * size].astype(bf16)
        for i in range(2):
            for j in range(width // 128):
                line = extra[6 + i : 7 + i, j * 128 : (j + 1) * 128]
                piece_ref[i * 8 + j : i * 8 + j + 1, 384:] = line.astype(bf16)
            router = jnp.zeros((8, part), f32)
            for row in range(4):
                low = width + i * 4 * part + row * part
                router = jnp.where((at_ref[1] ^ m) == row, extra[:, low : low + part], router)
            piece_ref[32 + i * 8 : 40 + i * 8, 384 : 384 + part] = router.astype(bf16)
        piece_ref[16:24, 384:] = extra[:, :128].astype(bf16)


def join_plane(at_ref, *refs):
    piece_refs, (out_ref, gain_one_ref, gain_two_ref, rel_ref, router_ref, line_ref) = refs[:4], refs[4:]
    size = line_ref.shape[1] // 4
    for quarter in range(4):
        piece = 0.0
        for m, piece_ref in enumerate(piece_refs):
            piece = jnp.where((at_ref[1] ^ m) == quarter, piece_ref[:, :size].astype(f32), piece)
        line_ref[:, quarter * size : (quarter + 1) * size] = piece
    inner = out_ref.shape[2]
    for part in range(3):
        out_ref[part] = line_ref[:, part * inner : (part + 1) * inner]
    extra = pair_sum([ref.at[:, 384:] for ref in piece_refs])
    for i, gain_ref in enumerate((gain_one_ref, gain_two_ref)):
        for j in range(gain_ref.shape[0] // 128):
            gain_ref[pl.ds(j * 128, 128)] = extra[i * 8 + j]
    rel_ref[...] = extra[16 : 16 + rel_ref.shape[0], : rel_ref.shape[1]]
    router_ref[...] = extra[32 : 32 + router_ref.shape[0], : router_ref.shape[1]]


def join_blocks(*refs):
    total = pair_sum(refs[:4])
    rows = total.shape[0] // 4
    for k, block_ref in enumerate(refs[4:]):
        block_ref[...] = total[k * rows : (k + 1) * rows].astype(bf16)


def finish(
    d_h_ref, peer_ref, x_ref, d_x_ref, gain_ref, gain_grad_ref, grad_offset_ref, hot_ref, grad_x_ref, small_ref,
):
    d_h = d_h_ref[...].astype(f32) + peer_ref[...].astype(f32)
    x_float = x_ref[...].astype(f32)
    scale = rms_scale(x_float)
    normed = x_float * scale
    d_norm = d_h * gain_ref[...].reshape(1, -1)
    grad_x = d_x_ref[...] + scale * (
        d_norm - normed * jnp.mean(d_norm * normed, axis=-1, keepdims=True)
    )
    grad_x_ref[...] = grad_x.astype(bf16)
    heads, buckets = grad_offset_ref.shape[0] - 2, hot_ref.shape[1]
    small_ref[...] = jnp.zeros(small_ref.shape, f32)
    grad_rel = lax.dot_general(
        grad_offset_ref[...], hot_ref[...], (((1,), (0,)), ((), ())), precision=highest, preferred_element_type=f32
    )
    small_ref[:, :buckets] = grad_rel
    small_ref[heads : heads + 1, :] = jnp.sum(d_h * normed, axis=0, keepdims=True)
    small_ref[heads + 1 : heads + 2, :] = gain_grad_ref[...]


def expert_grads(rows_ref, d_y_ref, act_ref, d_pre_ref, down_ref, up_ref, held_ref, sems):
    (hidden, width), steps = down_ref.shape, 3
    copies = []
    chunk = 0
    for left_ref, right_ref, out_ref in ((act_ref, d_y_ref, down_ref), (rows_ref, d_pre_ref, up_ref)):
        count = out_ref.shape[0] // steps
        for at in range(steps):
            rows = pl.ds(at * count, count)
            slot = chunk % 3
            if chunk >= 3:
                copies[chunk - 3].wait()
            held = held_ref.at[slot, pl.ds(0, count), pl.ds(0, out_ref.shape[1])]
            held[...] = dot(left_ref[:, rows], right_ref[...], 0, 0)
            copies.append(pltpu.make_async_copy(held, out_ref.at[rows, :], sems.at[chunk]))
            copies[-1].start()
            chunk += 1
    for copy in copies[-3:]:
        copy.wait()


def experts_pad(experts):
    return -(-experts // 128) * 128


def make_per_device(mesh):
    n_ex, n_row = mesh.shape["ex"], mesh.shape["row"]
    groups = n_ex * n_row

    def hop(values, axis, step):
        return lax.ppermute(values, axis, [(i, i ^ step) for i in range(mesh.shape[axis])])

    def whole_cube(rows):
        return n_ex == 4 and n_row == 4 and rows == 48

    def gather_blocks(shard, meanwhile):
        rows, width = shard.shape
        if whole_cube(rows):
            near, far, farther = (hop(shard, "ex", k) for k in (1, 2, 3))
            x_own, y_own = hop(shard, "row", 1), hop(shard, "row", 2)
            near, x_own, y_own = lax.optimization_barrier((near, x_own, y_own))
            xs, ys = [x_own, hop(near, "row", 1)], [y_own, hop(near, "row", 2)]
            diagonal = [hop(x_own, "row", 2)]
            beside = meanwhile(near)
            far, farther, diagonal[0], *beside = lax.optimization_barrier((far, farther, diagonal[0], *beside))
            for part in (far, farther):
                xs.append(hop(part, "row", 1))
                ys.append(hop(part, "row", 2))
            diagonal += [hop(ys[1], "row", 1), hop(xs[2], "row", 2), hop(ys[3], "row", 1)]
            return [shard, near, far, farther, *xs, *ys, *diagonal], beside
        part = lax.all_gather(shard, "ex", axis=0)
        part = jnp.broadcast_to(part[None], (n_row, n_ex, rows, width))
        part = lax.all_to_all(part, "row", split_axis=0, concat_axis=0, tiled=True)
        return [part.transpose(1, 0, 2, 3).reshape(groups * rows, width)], meanwhile(shard)

    def scatter_groups(grads, rows):
        part = grads.astype(bf16).reshape(n_ex, n_row, rows, -1).transpose(1, 0, 2, 3)
        part = lax.all_to_all(part, "row", split_axis=0, concat_axis=0, tiled=True)
        part = jnp.sum(part.astype(f32), axis=0).astype(bf16)
        part = lax.all_to_all(part, "ex", split_axis=0, concat_axis=0, tiled=True)
        return jnp.sum(part.astype(f32), axis=0)

    def plane_hops(parts):
        return [hop(part, "row", m + 1) for m, part in enumerate(parts)]

    def line_hops(parts):
        return [hop(part, "ex", k + 1) for k, part in enumerate(parts)]

    def sum_groups(values):
        for axis in ("row", "ex"):
            step = 1
            while step < mesh.shape[axis]:
                values = values + hop(values, axis, step)
                step *= 2
        return values

    def per_device(
        x_in,
        gain_attn,
        w_qkv,
        rel_bias,
        w_out,
        gain_ffn,
        w_router,
        w_up,
        w_down,
        seg_ids,
        expert_ids,
        slot_ids,
        drop_flags,
        d_out,
    ):
        seq_len, width = x_in.shape
        heads_here = rel_bias.shape[1]
        inner = w_qkv.shape[2]
        own_rows = w_qkv.shape[1]
        experts = w_router.shape[1]
        wide = inner + experts_pad(experts)
        half = d_out.shape[1]
        hidden = w_up.shape[2]
        device_at = jnp.stack([lax.axis_index(axis).astype(jnp.int32) for axis in ("ex", "row", "col")])
        device_at, w_qkv = lax.optimization_barrier((device_at, w_qkv))
        cube = whole_cube(own_rows)
        capacity = 5 * seq_len // (4 * experts)
        tight = cube and experts == 16 and capacity == 20 and width == 768
        slots = capacity if tight else -(-capacity // 8) * 8
        slot_total = experts * slots
        packed_slots = (experts, slots * width // 128, 128) if tight else (slot_total, width)
        exchange = packed_slots if tight else (experts, slots, width)
        slot_scratch = (
            pltpu.VMEM((slot_total, width), bf16),
            pltpu.VMEM((slot_total, width), bf16),
            pltpu.VMEM((experts * 24, 128), f32),
        )
        gather_order = GATHER_ORDER if cube else None

        (packed,) = vmem_call(
            pack_weights,
            (shape((own_rows, 3 * inner + wide), bf16),),
            0,
            w_qkv,
            w_out.T,
            w_router.T,
        )

        def round_weights(after):
            late_up, late_down, _ = lax.optimization_barrier((w_up[0], w_down[0], after))
            return [late_up.astype(bf16), late_down.astype(bf16)]

        blocks, (up_w, down_w) = gather_blocks(packed, round_weights)
        g_peer = swap_cores(d_out)

        span = 2 * seq_len
        offsets = jnp.arange(span, dtype=jnp.int32) - (seq_len - 1)
        offset_hot = (
            bucket_of(offsets)[:, None] == jnp.arange(BUCKETS, dtype=jnp.int32)[None, :]
        ).astype(f32)
        per_offset = jnp.einsum("bh,ob->ho", rel_bias, offset_hot, precision=highest)
        square = seq_len * seq_len * heads_here * HEAD
        attn_part, qkv, probs, context, qkv_w, out_w, router_w, normed_turned, normed_mine = vmem_call(
            functools.partial(attend_forward, gather_order),
            (
                shape((seq_len, width), bf16),
                shape((seq_len, 3 * inner), bf16),
                shape((heads_here, seq_len, seq_len), f32),
                shape((seq_len, inner), bf16),
                shape((width, 3 * inner), bf16),
                shape((width, inner), bf16),
                shape((width, wide - inner), bf16),
                shape((width, seq_len), bf16),
                shape((half, seq_len), bf16),
            ),
            8 * seq_len * width * inner + 4 * square,
            x_in,
            gain_attn,
            per_offset,
            seg_ids,
            *blocks,
            scalars=(device_at,),
        )
        attn_peer = swap_cores(attn_part)
        slot_of = expert_ids * slots + slot_ids
        if tight:
            spare_of = experts * 16 + expert_ids * 4 + slot_ids - 16
            slot_of = jnp.where(slot_ids < 16, expert_ids * 16 + slot_ids, spare_of)
        slot_of = jnp.where(drop_flags == 1, slot_total, slot_of)[None]
        (send,) = vmem_call(
            dispatch,
            (shape(packed_slots, bf16),),
            2 * seq_len * slot_total * width,
            x_in,
            attn_part,
            attn_peer,
            gain_ffn,
            slot_of,
            d_out,
            scalars=(device_at,),
        )
        got = lax.all_to_all(send.reshape(exchange), ("ex", "row"), 0, 0, tiled=True).reshape(packed_slots)
        if cube:
            later_normed, got = lax.optimization_barrier((normed_mine, got))
            normed_hops = plane_hops([later_normed] * 2)
        crossing, mine, router_probs, gate_part, rows, d_y, act_b, d_pre = vmem_call(
            functools.partial(run_expert, experts, n_row),
            (
                shape((slot_total, width + 128), bf16),
                shape((slot_total, width), f32),
                shape((slot_total, experts), f32),
                shape((slot_total, 1), f32),
                shape((slot_total, width), bf16),
                shape((slot_total, width), bf16),
                shape((slot_total, hidden), bf16),
                shape((slot_total, hidden), bf16),
            ),
            8 * slot_total * width * hidden,
            got,
            swap_cores(got),
            router_w,
            up_w,
            down_w,
            scalars=(device_at,),
            scratch=(pltpu.VMEM((slot_total, width), f32), *slot_scratch),
        )
        if cube:
            crossing, g_peer, *normed_hops = lax.optimization_barrier((crossing, g_peer, *normed_hops))
        back, grad_router = vmem_call(
            functools.partial(settle, n_row),
            (shape(packed_slots, bf16), shape((experts, width), f32)),
            2 * slot_total * half * experts,
            mine,
            swap_cores(crossing),
            router_probs,
            gate_part,
            router_w,
            rows,
            scalars=(device_at,),
        )
        home = lax.all_to_all(back.reshape(exchange), ("ex", "row"), 0, 0, tiled=True).reshape(packed_slots)
        layer_out, d_h_mine = vmem_call(
            arrive,
            (shape((seq_len, half), bf16), shape((seq_len, half), bf16)),
            2 * seq_len * slot_total * width,
            home,
            slot_of,
            x_in,
            attn_part,
            attn_peer,
            scalars=(device_at,),
            scratch=slot_scratch[1:],
        )
        def grads_of_expert(rows, d_y, act_b, d_pre):
            return pl.pallas_call(
                expert_grads,
                out_shape=(shape((hidden, width), f32), shape((width, hidden), f32)),
                in_specs=[pl.BlockSpec(memory_space=pltpu.VMEM)] * 4,
                out_specs=[pl.BlockSpec(memory_space=pltpu.HBM)] * 2,
                scratch_shapes=[
                    pltpu.VMEM((3, max(hidden, width) // 3, max(hidden, width)), f32),
                    pltpu.SemaphoreType.DMA((6,)),
                ],
                compiler_params=pltpu.CompilerParams(vmem_limit_bytes=24 * 2**20),
                cost_estimate=pl.CostEstimate(
                    flops=4 * slot_total * width * hidden, bytes_accessed=12 * width * hidden, transcendentals=0
                ),
            )(rows, d_y, act_b, d_pre)

        quarter = (width // 4, 3 * inner // 4) if cube else (width, 3 * inner)
        pieces = 4 if cube else 1
        if cube:
            d_h_mine, from_x, from_y = lax.optimization_barrier((d_h_mine, *normed_hops))
            normed_hops += [hop(from_x[: half // 2], "row", 2), hop(from_y[half // 2 :], "row", 1)]
        d_x_one, grad_gain_ffn, d_context, *out_pieces = vmem_call(
            functools.partial(come_home, cube),
            (
                shape((seq_len, width), f32),
                shape((1, width), f32),
                shape((seq_len, inner), bf16),
                *[shape((quarter[0], inner), bf16)] * pieces,
            ),
            4 * seq_len * width * inner,
            d_h_mine,
            swap_cores(d_h_mine),
            x_in,
            attn_part,
            attn_peer,
            d_out,
            g_peer,
            gain_ffn,
            out_w,
            context,
            scalars=(device_at,),
            scratch=(pltpu.VMEM((width, inner), bf16),),
        )
        d_h_part, grad_offset, *d_qkv_turned = vmem_call(
            functools.partial(attend_backward, cube),
            (
                shape((seq_len, width), bf16),
                shape((heads_here + 2, span), f32),
                *[shape((quarter[1], seq_len), bf16)] * pieces,
            ),
            6 * seq_len * width * inner + 10 * square,
            d_context,
            qkv,
            probs,
            qkv_w,
            scalars=(device_at,),
            scratch=(pltpu.VMEM((3 * inner, seq_len), bf16),),
        )
        grad_x, small = vmem_call(
            finish,
            (shape((seq_len, width), bf16), shape((heads_here + 2, width), f32)),
            0,
            d_h_part,
            swap_cores(d_h_part),
            x_in,
            d_x_one,
            gain_attn,
            grad_gain_ffn,
            grad_offset,
            offset_hot,
        )
        if cube:
            *normed_hops, _ = lax.optimization_barrier((*normed_hops, d_h_part))
            normed_near = jnp.concatenate(normed_hops, axis=0)
            normed_peer = swap_cores(normed_near)
            terms = vmem_call(
                qkv_terms,
                [shape((own_rows + 8, 3 * inner), bf16)] * 4,
                6 * seq_len * width * inner,
                normed_turned,
                small,
                grad_router,
                normed_near,
                normed_peer,
                d_qkv_turned[0],
                *plane_hops(d_qkv_turned[1:]),
                scalars=(device_at,),
                scratch=(pltpu.VMEM((width, quarter[1]), bf16),),
            )
            line = line_hops(terms[1:])
            first_line = line[0]
            rows, d_y, act_b, d_pre, _ = lax.optimization_barrier((rows, d_y, act_b, d_pre, terms[0]))
            grad_down, grad_up = grads_of_expert(rows, d_y, act_b, d_pre)
            *line, grad_down, grad_up = lax.optimization_barrier((*line, grad_down, grad_up))
            split = vmem_call(
                join_line,
                [shape((own_rows, 512), bf16)] * 4,
                0,
                terms[0],
                *line,
                scalars=(device_at,),
            )
            last = plane_hops(split[1:])
            grad_qkv, gain_one, gain_two, grad_rel, grad_router = vmem_call(
                join_plane,
                (
                    shape((3, own_rows, inner), f32),
                    shape((width,), f32),
                    shape((width,), f32),
                    shape((heads_here, BUCKETS), f32),
                    shape((experts, own_rows), f32),
                ),
                0,
                split[0],
                *last,
                scalars=(device_at,),
                scratch=(pltpu.VMEM((own_rows, 3 * inner), f32),),
            )
            *out_pieces, _ = lax.optimization_barrier((*out_pieces, first_line))
            out_hops = plane_hops(out_pieces[1:])
            out_blocks = vmem_call(
                join_blocks,
                [shape((own_rows, inner), bf16)] * 4,
                0,
                out_pieces[0],
                *out_hops,
            )
            *out_blocks, _ = lax.optimization_barrier((*out_blocks, last[0]))
            out_blocks = (out_blocks[0], *line_hops(out_blocks[1:]))
            grad_out = sum(part.astype(f32) for part in out_blocks)
        else:
            grad_down, grad_up = grads_of_expert(rows, d_y, act_b, d_pre)
            grad_qkv = scatter_groups(dot(normed_turned, d_qkv_turned[0], 1, 1), own_rows)
            grad_qkv = grad_qkv.reshape(own_rows, 3, inner).transpose(1, 0, 2)
            grad_out = scatter_groups(out_pieces[0], own_rows)
            small = sum_groups(jnp.concatenate([small, grad_router]))
            gain_one, gain_two = small[heads_here], small[heads_here + 1]
            grad_rel = small[:heads_here, :BUCKETS]
            own_at = (device_at[0] * n_row + device_at[1]) * own_rows
            grad_router = lax.dynamic_slice(small, (heads_here + 2, own_at), (experts, own_rows))
        return (
            layer_out,
            grad_x,
            gain_one,
            grad_qkv,
            grad_rel.T,
            grad_out.T,
            gain_two,
            grad_router.T,
            grad_up[None],
            grad_down[None],
        )

    return per_device


def solution(mesh):
    return jax.shard_map(
        make_per_device(mesh),
        mesh=mesh,
        in_specs=(
            P(("ex", "row"), None),
            P(),
            P(None, ("ex", "row"), "col"),
            P(None, "col"),
            P("col", ("ex", "row")),
            P(),
            P(("ex", "row"), None),
            P(("ex", "row"), None, "col"),
            P(("ex", "row"), "col", None),
            P(("ex", "row"), None),
            P(("ex", "row")),
            P(("ex", "row")),
            P(("ex", "row")),
            P(("ex", "row"), "col"),
        ),
        out_specs=(
            P(("ex", "row"), "col"),
            P(("ex", "row"), None),
            P(),
            P(None, ("ex", "row"), "col"),
            P(None, "col"),
            P("col", ("ex", "row")),
            P(),
            P(("ex", "row"), None),
            P(("ex", "row"), None, "col"),
            P(("ex", "row"), "col", None),
        ),
        check_vma=False,
    )
```

```python
import functools
import math

import jax
import jax.numpy as jnp
from jax import lax
from jax.experimental import pallas as pl
from jax.experimental.pallas import tpu as pltpu
from jax.sharding import PartitionSpec as P

HEAD = 64
BUCKETS = 32

norm_eps = 1e-06
bucket_edges = (12, 16, 23, 32, 46, 64, 91)
highest = lax.Precision.HIGHEST
bf16 = jnp.bfloat16
f32 = jnp.float32

GATHER_ORDER = tuple(((k, m),) for m in range(4) for k in range(4))

def bucket_of(offset):
    distance = jnp.abs(offset)
    far_part = jnp.zeros(distance.shape, jnp.int32)
    for edge_at in bucket_edges:
        far_part = far_part + (distance >= edge_at).astype(jnp.int32)
    inside = jnp.where(distance < 8, distance, far_part + jnp.int32(8))
    upper = jnp.where(offset > 0, jnp.int32(BUCKETS // 2), jnp.int32(0))
    return inside + upper


def rms_scale(values):
    return lax.rsqrt(jnp.mean(values * values, axis=-1, keepdims=True) + norm_eps)


def dot(a, b, ca, cb):
    return lax.dot_general(a, b, (((ca,), (cb,)), ((), ())), preferred_element_type=f32)


def swap_cores(values):
    return lax.ppermute(values, "col", [(0, 1), (1, 0)])


def shape(dims, dtype):
    return jax.ShapeDtypeStruct(tuple(dims), dtype)


def vmem_call(kernel, out_shape, flops, *args, scalars=(), scratch=(), limit=12):
    nbytes = sum(math.prod(v.shape) * v.dtype.itemsize for v in (*args, *out_shape))
    spec = pl.BlockSpec(memory_space=pltpu.VMEM)
    limit = limit if nbytes < 16 * 2**20 else 48
    return pl.pallas_call(
        kernel,
        out_shape=out_shape,
        in_specs=[pl.BlockSpec(memory_space=pltpu.SMEM)] * len(scalars) + [spec] * len(args),
        out_specs=[spec] * len(out_shape),
        scratch_shapes=scratch,
        compiler_params=pltpu.CompilerParams(vmem_limit_bytes=limit * 2**20),
        cost_estimate=pl.CostEstimate(flops=flops, bytes_accessed=nbytes, transcendentals=0),
    )(*scalars, *args)


def block_rows(at_ref, order, count):
    if order is None:
        return [pl.ds(0, count)]
    ex_at, row_at = at_ref[0], at_ref[1]
    return [
        pl.ds(pl.multiple_of(((ex_at ^ k) * 4 + (row_at ^ m)) * count, 16), count)
        for part in order
        for k, m in part
    ]


def eye(size):
    dims = (size, size)
    same = lax.broadcasted_iota(jnp.int32, dims, 0) == lax.broadcasted_iota(jnp.int32, dims, 1)
    return same.astype(bf16)


def pack_weights(qkv_ref, out_turned_ref, router_turned_ref, packed_ref):
    inner, experts = qkv_ref.shape[2], router_turned_ref.shape[0]
    for part in range(3):
        packed_ref[:, part * inner : (part + 1) * inner] = qkv_ref[part].astype(bf16)
    packed_ref[:, 3 * inner : 4 * inner] = out_turned_ref[...].astype(bf16)
    packed_ref[:, 4 * inner :] = jnp.zeros((packed_ref.shape[0], packed_ref.shape[1] - 4 * inner), bf16)
    router = dot(router_turned_ref[...].astype(bf16), eye(experts), 0, 0)
    packed_ref[:, 4 * inner : 4 * inner + experts] = router.astype(bf16)


def attend_forward(order, at_ref, x_ref, gain_ref, offset_ref, seg_ref, *refs):
    *block_refs, part_ref, qkv_ref, probs_ref, ctx_ref, w_ref, out_w_ref, router_ref, turned_ref, half_ref = refs
    seq_len = x_ref.shape[0]
    heads, inner = probs_ref.shape[0], ctx_ref.shape[1]
    for rows, block_ref in zip(block_rows(at_ref, order, block_refs[0].shape[0]), block_refs):
        w_ref[rows, :] = block_ref[:, : 3 * inner]
        out_w_ref[rows, :] = block_ref[:, 3 * inner : 4 * inner]
        router_ref[rows, :] = block_ref[:, 4 * inner :]
    x_float = x_ref[...].astype(f32)
    h_one = (x_float * rms_scale(x_float) * gain_ref[...].reshape(1, -1)).astype(bf16)
    turned_ref[...] = dot(h_one, eye(seq_len), 0, 0).astype(bf16)
    half = half_ref.shape[0]
    half_ref[...] = jnp.where(at_ref[2] == 0, turned_ref[:half, :], turned_ref[half:, :])
    documents = lax.broadcasted_iota(jnp.int32, (8, seq_len), 0) == seg_ref[...]
    same_doc = dot(documents.astype(bf16), documents.astype(bf16), 0, 0) > 0.5
    qkv_ref[...] = dot(h_one, w_ref[...], 1, 0).astype(bf16)
    span = offset_ref.shape[1]
    for at in range(heads):
        take = lambda part: qkv_ref[:, part * inner + at * HEAD : part * inner + (at + 1) * HEAD]
        spread = jnp.broadcast_to(offset_ref[at : at + 1, :], (seq_len, span))
        bias = pltpu.roll(spread, span - seq_len + 1, 1, stride=1, stride_axis=0)[:, :seq_len]
        scores = jnp.where(same_doc, dot(take(0), take(1), 1, 1) * 0.125 + bias, -1e30)
        expo = jnp.exp(scores - jnp.max(scores, axis=1, keepdims=True))
        probs = expo / jnp.sum(expo, axis=1, keepdims=True)
        probs_ref[at] = probs
        ctx = dot(probs.astype(bf16), take(2), 1, 0)
        ctx_ref[:, at * HEAD : (at + 1) * HEAD] = ctx.astype(bf16)
    part_ref[...] = dot(ctx_ref[...], out_w_ref[...], 1, 1).astype(bf16)


def spare_rows(experts, chunk):
    dims = (experts * 24, experts * 4)
    row, column = lax.broadcasted_iota(jnp.int32, dims, 0), lax.broadcasted_iota(jnp.int32, dims, 1)
    expert = lax.shift_right_logical(row * 2731, 16)
    inside = row - expert * 24
    wanted = expert * 4 + (inside - chunk * 4)
    return ((column == wanted) & (inside >= chunk * 4) & (inside < chunk * 4 + 4)).astype(bf16)


def pack_slots(values, packed_ref):
    if len(packed_ref.shape) == 2:
        packed_ref[...] = values.astype(bf16)
        return
    experts, chunks = packed_ref.shape[0], values.shape[1] // 128
    values = values.astype(bf16)
    spare = 0.0
    for c in range(chunks):
        chunk = values[:, c * 128 : (c + 1) * 128]
        for e in range(experts):
            packed_ref[e, c * 16 : (c + 1) * 16, :] = chunk[e * 16 : (e + 1) * 16]
        spare = spare + dot(spare_rows(experts, c), chunk[experts * 16 :], 1, 0)
    for e in range(experts):
        packed_ref[e, chunks * 16 :, :] = spare[e * 24 : (e + 1) * 24].astype(bf16)


def unpack_slots(packed_ref, low, target_ref, spare_ref):
    experts, chunks = packed_ref.shape[0], target_ref.shape[1] // 128
    first = (packed_ref.shape[1] - 24) // 16 * 16
    for e in range(experts):
        spare_ref[e * 24 : (e + 1) * 24, :] = packed_ref[e, first:, :].astype(f32)
    spare = spare_ref[...].astype(bf16)
    for c in range(chunks):
        lanes = slice(c * 128, (c + 1) * 128)
        for e in range(experts):
            rows = slice((low + c) * 16, (low + c + 1) * 16)
            target_ref[e * 16 : (e + 1) * 16, lanes] = packed_ref[e, rows, :]
        target_ref[experts * 16 :, lanes] = dot(spare_rows(experts, low + c), spare, 0, 0).astype(bf16)


def dispatch(at_ref, x_ref, part_ref, peer_ref, gain_ref, slot_ref, g_ref, send_ref):
    half = g_ref.shape[1]
    x_one = x_ref[...].astype(f32) + (part_ref[...].astype(f32) + peer_ref[...].astype(f32))
    h_two = (x_one * rms_scale(x_one) * gain_ref[...].reshape(1, -1)).astype(bf16)
    mine = jnp.where(at_ref[2] == 0, h_two[:, :half], h_two[:, half:])
    slots = send_ref.shape[0] * (1 if len(send_ref.shape) == 2 else 20)
    dims = (slots, x_ref.shape[0])
    place = (lax.broadcasted_iota(jnp.int32, dims, 0) == slot_ref[...]).astype(bf16)
    sent = jnp.concatenate([dot(place, mine, 1, 0), dot(place, g_ref[...], 1, 0)], axis=1)
    pack_slots(sent, send_ref)


def run_expert(
    experts, row_size, at_ref, got_ref, peer_ref, router_ref, up_ref, down_ref,
    cross_ref, mine_ref, probs_ref, gate_part_ref, rows_ref, d_y_ref, act_ref, d_pre_ref, d_in_ref,
    got_rows_ref, peer_rows_ref, spare_ref,
):
    half = rows_ref.shape[1] // 2
    if len(got_ref.shape) == 3:
        unpack_slots(got_ref, 0, got_rows_ref, spare_ref)
        unpack_slots(peer_ref, 0, peer_rows_ref, spare_ref)
        got_ref, peer_ref = got_rows_ref, peer_rows_ref
    hidden = up_ref.shape[1]
    first_core = at_ref[2] == 0
    for at, refs in ((0, (got_ref, peer_ref)), (1, (peer_ref, got_ref))):
        pick = lambda lo: jnp.where(first_core, refs[0][:, lo : lo + half], refs[1][:, lo : lo + half])
        rows_ref[:, at * half : (at + 1) * half] = pick(0)
        d_y_ref[:, at * half : (at + 1) * half] = pick(half)
    rows, g_rows = rows_ref[...], d_y_ref[...].astype(f32)
    logits = dot(rows, router_ref[...], 1, 0)[:, :experts]
    expo = jnp.exp(logits - jnp.max(logits, axis=1, keepdims=True))
    probs = expo / jnp.sum(expo, axis=1, keepdims=True)
    probs_ref[...] = probs
    expert_at = at_ref[0] * row_size + at_ref[1]
    chosen = lax.broadcasted_iota(jnp.int32, probs.shape, 1) == expert_at
    gate = jnp.sum(jnp.where(chosen, probs, 0.0), axis=1, keepdims=True)
    d_y_ref[...] = (g_rows * gate).astype(bf16)
    step = 512 if hidden % 512 == 0 else hidden
    y_part = None
    for lo in range(0, hidden, step):
        cols = pl.ds(lo, step)
        pre_act = dot(rows_ref[...], up_ref[:, cols], 1, 0)
        cdf = 0.5 * (1.0 + lax.erf(pre_act * (1.0 / math.sqrt(2.0))))
        pdf = jnp.exp(-0.5 * pre_act * pre_act) * (1.0 / math.sqrt(2.0 * math.pi))
        act = (pre_act * cdf).astype(bf16)
        act_ref[:, cols] = act
        y_more = dot(act, down_ref[cols, :], 1, 0)
        d_pre = (dot(d_y_ref[...], down_ref[cols, :], 1, 1) * (cdf + pre_act * pdf)).astype(bf16)
        d_pre_ref[:, cols] = d_pre
        d_more = dot(d_pre, up_ref[:, cols], 1, 1)
        if lo == 0:
            y_part = y_more
            d_in_ref[...] = d_more
        else:
            y_part = y_part + y_more
            d_in_ref[...] += d_more
    gate_part = jnp.sum(g_rows * y_part, axis=1, keepdims=True)
    high = gate_part.astype(bf16)
    low = (gate_part - high.astype(f32)).astype(bf16)
    gate_part_ref[...] = high.astype(f32) + low.astype(f32)
    lane = lax.broadcasted_iota(jnp.int32, (rows.shape[0], 128), 1)
    beside = jnp.where(lane == 0, high.astype(f32), jnp.where(lane == 1, low.astype(f32), 0.0))
    cross_ref[:, 2 * half :] = beside.astype(bf16)
    d_in = d_in_ref[...]
    mine_ref[:, :half] = jnp.where(first_core, y_part[:, :half], y_part[:, half:])
    mine_ref[:, half:] = jnp.where(first_core, d_in[:, :half], d_in[:, half:])
    cross_ref[:, :half] = jnp.where(first_core, y_part[:, half:], y_part[:, :half]).astype(bf16)
    cross_ref[:, half : 2 * half] = jnp.where(first_core, d_in[:, half:], d_in[:, :half]).astype(bf16)


def settle(
    row_size, at_ref, mine_ref, crossed_ref, probs_ref, gate_part_ref, router_ref, rows_ref,
    back_ref, grad_router_ref,
):
    half = mine_ref.shape[1] // 2
    probs = probs_ref[...]
    expert_at = at_ref[0] * row_size + at_ref[1]
    chosen = (lax.broadcasted_iota(jnp.int32, probs.shape, 1) == expert_at).astype(f32)
    gate = jnp.sum(probs * chosen, axis=1, keepdims=True)
    beside = crossed_ref[:, 2 * half :].astype(f32)
    d_gate = gate_part_ref[...] + (beside[:, 0:1] + beside[:, 1:2])
    d_logits = (d_gate * gate * (chosen - probs)).astype(bf16)
    router_w = router_ref[...][:, : probs.shape[1]]
    router_mine = jnp.where(at_ref[2] == 0, router_w[:half], router_w[half:])
    y_gated = gate * (mine_ref[:, :half] + crossed_ref[:, :half].astype(f32))
    d_in = mine_ref[:, half:] + crossed_ref[:, half : 2 * half].astype(f32) + dot(d_logits, router_mine, 1, 1)
    pack_slots(jnp.concatenate([y_gated, d_in], axis=1), back_ref)
    grad_router_ref[...] = dot(d_logits, rows_ref[...], 0, 0)


def from_slots(home_ref, slot_ref, low, rows_ref, spare_ref):
    if len(home_ref.shape) == 3:
        unpack_slots(home_ref, low, rows_ref, spare_ref)
    else:
        rows_ref[...] = home_ref[:, low * 128 : low * 128 + rows_ref.shape[1]]
    dims = (rows_ref.shape[0], slot_ref.shape[1])
    place = (lax.broadcasted_iota(jnp.int32, dims, 0) == slot_ref[...]).astype(bf16)
    return dot(place, rows_ref[...], 0, 0)


def arrive(home_ref, slot_ref, d_h_ref, rows_ref, spare_ref):
    low = d_h_ref.shape[1] // 128
    d_h_ref[...] = from_slots(home_ref, slot_ref, low, rows_ref, spare_ref).astype(bf16)


def land(at_ref, home_ref, slot_ref, x_ref, part_ref, peer_ref, layer_ref, rows_ref, spare_ref):
    half = layer_ref.shape[1]
    y_home = from_slots(home_ref, slot_ref, 0, rows_ref, spare_ref)
    mine = lambda ref: jnp.where(at_ref[2] == 0, ref[:, :half], ref[:, half:]).astype(f32)
    layer_ref[...] = (mine(x_ref) + (mine(part_ref) + mine(peer_ref)) + y_home).astype(bf16)


def come_home(
    cube, at_ref, mine_ref, peer_ref, x_ref, part_ref, part_peer_ref, g_ref, g_peer_ref,
    gain_ref, out_w_ref, ctx_ref, d_x_ref, gain_grad_ref, d_ctx_ref, *refs,
):
    *piece_refs, grads_ref = refs
    first_core = at_ref[2] == 0
    both = lambda a, b: jnp.concatenate(
        [jnp.where(first_core, a, b), jnp.where(first_core, b, a)], axis=1
    )
    d_h = both(mine_ref[...], peer_ref[...]).astype(f32)
    x_one = x_ref[...].astype(f32) + (part_ref[...].astype(f32) + part_peer_ref[...].astype(f32))
    g_full = both(g_ref[...], g_peer_ref[...]).astype(f32)
    scale = rms_scale(x_one)
    normed = x_one * scale
    gain_grad_ref[...] = jnp.sum(d_h * normed, axis=0, keepdims=True)
    d_norm = d_h * gain_ref[...].reshape(1, -1)
    d_x = g_full + scale * (d_norm - normed * jnp.mean(d_norm * normed, axis=-1, keepdims=True))
    d_x_ref[...] = d_x
    d_x_b = d_x.astype(bf16)
    d_ctx_ref[...] = dot(d_x_b, out_w_ref[...], 1, 0).astype(bf16)
    grads_ref[...] = dot(d_x_b, ctx_ref[...], 0, 0).astype(bf16)
    rows = grads_ref.shape[0] // 16
    for m, piece_ref in enumerate(piece_refs):
        if not cube:
            piece_ref[...] = grads_ref[...]
            continue
        for k in range(4):
            start = pl.multiple_of(((at_ref[0] ^ k) * 4 + (at_ref[1] ^ m)) * rows, 16)
            piece_ref[k * rows : (k + 1) * rows, :] = grads_ref[pl.ds(start, rows), :]


def attend_backward(cube, at_ref, d_ctx_ref, qkv_ref, probs_ref, w_ref, d_h_ref, grad_offset_ref, *refs):
    *piece_refs, turned_ref = refs
    heads, seq_len, _ = probs_ref.shape
    inner = d_ctx_ref.shape[1]
    span = grad_offset_ref.shape[1]
    flip = (
        lax.broadcasted_iota(jnp.int32, (seq_len, seq_len), 0)
        + lax.broadcasted_iota(jnp.int32, (seq_len, seq_len), 1)
        == seq_len - 1
    ).astype(bf16)
    grad_offset_ref[...] = jnp.zeros(grad_offset_ref.shape, f32)
    for at in range(heads):
        cols = lambda part: pl.ds(part * inner + at * HEAD, HEAD)
        d_ctx = d_ctx_ref[:, at * HEAD : (at + 1) * HEAD]
        probs = probs_ref[at]
        d_probs = dot(d_ctx, qkv_ref[:, cols(2)], 1, 1)
        row_delta = jnp.sum(probs * d_probs, axis=1, keepdims=True)
        d_scores = (probs * (d_probs - row_delta)).astype(bf16)
        turned_ref[cols(0), :] = (dot(qkv_ref[:, cols(1)], d_scores, 0, 1) * 0.125).astype(bf16)
        turned_ref[cols(1), :] = (dot(qkv_ref[:, cols(0)], d_scores, 0, 0) * 0.125).astype(bf16)
        turned_ref[cols(2), :] = dot(d_ctx, probs.astype(bf16), 0, 0).astype(bf16)
        flipped = jnp.concatenate(
            [dot(flip, d_scores, 1, 0), jnp.zeros((seq_len, span - seq_len), f32)], axis=1
        )
        lined = pltpu.roll(flipped, 0, 1, stride=1, stride_axis=0)
        grad_offset_ref[at : at + 1, :] = jnp.sum(lined, axis=0, keepdims=True)
    size = piece_refs[0].shape[0]
    for m, piece_ref in enumerate(piece_refs):
        start = pl.multiple_of((at_ref[1] ^ m) * size, 16) if cube else 0
        piece_ref[...] = turned_ref[pl.ds(start, size), :]
    d_h_ref[...] = dot(turned_ref[...], w_ref[...], 0, 1).astype(bf16)


def qkv_terms(at_ref, turned_ref, small_ref, router_ref, *refs):
    mine_ref, peer_ref, piece_refs, block_refs, grads_ref = refs[0], refs[1], refs[2:6], refs[6:10], refs[10]
    half = mine_ref.shape[0] // 3
    from_mine = from_peer = 0.0
    for m in range(1, 4):
        rows = slice((m - 1) * half, m * half)
        from_mine = from_mine + dot(mine_ref[rows, :], piece_refs[m][...], 1, 1)
        from_peer = from_peer + dot(peer_ref[rows, :], piece_refs[m][...], 1, 1)
    own = dot(turned_ref[...], piece_refs[0][...], 1, 1)
    first_core = at_ref[2] == 0
    grads_ref[:half, :] = (own[:half] + jnp.where(first_core, from_mine, from_peer)).astype(bf16)
    grads_ref[half:, :] = (own[half:] + jnp.where(first_core, from_peer, from_mine)).astype(bf16)
    rows, size = block_refs[0].shape[0] - 8, grads_ref.shape[1]
    width = small_ref.shape[1]
    part = width // 4
    for k, block_ref in enumerate(block_refs):
        block_ref[rows:, :width] = small_ref[...].astype(bf16)
        router = jnp.zeros((router_ref.shape[0], part), f32)
        for z in range(4):
            router = jnp.where((at_ref[0] ^ k) == z, router_ref[:, z * part : (z + 1) * part], router)
        for i in range(2):
            low = width + i * part
            block_ref[rows:, low : low + part] = router[i * 8 : (i + 1) * 8].astype(bf16)
        for m in range(4):
            start = ((at_ref[0] ^ k) * 4 + (at_ref[1] ^ m)) * rows
            block_ref[:rows, m * size : (m + 1) * size] = grads_ref[pl.ds(pl.multiple_of(start, 16), rows), :]


def pair_sum(refs):
    a, b, c, d = (ref[...].astype(f32) for ref in refs)
    return (a + b) + (c + d)


def join_line(at_ref, *refs):
    total = pair_sum(refs[:4])
    rows = refs[4].shape[0]
    size = total.shape[1] // 4
    width = size * 8 // 3
    part = width // 16
    extra = total[rows:]
    for m, piece_ref in enumerate(refs[4:]):
        piece_ref[...] = jnp.zeros(piece_ref.shape, bf16)
        piece_ref[:, :size] = total[:rows, m * size : (m + 1) * size].astype(bf16)
        for i in range(2):
            for j in range(width // 128):
                line = extra[6 + i : 7 + i, j * 128 : (j + 1) * 128]
                piece_ref[i * 8 + j : i * 8 + j + 1, 384:] = line.astype(bf16)
            router = jnp.zeros((8, part), f32)
            for row in range(4):
                low = width + i * 4 * part + row * part
                router = jnp.where((at_ref[1] ^ m) == row, extra[:, low : low + part], router)
            piece_ref[32 + i * 8 : 40 + i * 8, 384 : 384 + part] = router.astype(bf16)
        piece_ref[16:24, 384:] = extra[:, :128].astype(bf16)


def join_plane(at_ref, *refs):
    piece_refs, (out_ref, gain_one_ref, gain_two_ref, rel_ref, router_ref, line_ref) = refs[:4], refs[4:]
    size = line_ref.shape[1] // 4
    for quarter in range(4):
        piece = 0.0
        for m, piece_ref in enumerate(piece_refs):
            piece = jnp.where((at_ref[1] ^ m) == quarter, piece_ref[:, :size].astype(f32), piece)
        line_ref[:, quarter * size : (quarter + 1) * size] = piece
    inner = out_ref.shape[2]
    for part in range(3):
        out_ref[part] = line_ref[:, part * inner : (part + 1) * inner]
    extra = pair_sum([ref.at[:, 384:] for ref in piece_refs])
    for i, gain_ref in enumerate((gain_one_ref, gain_two_ref)):
        for j in range(gain_ref.shape[0] // 128):
            gain_ref[pl.ds(j * 128, 128)] = extra[i * 8 + j]
    rel_ref[...] = extra[16 : 16 + rel_ref.shape[0], : rel_ref.shape[1]]
    router_ref[...] = extra[32 : 32 + router_ref.shape[0], : router_ref.shape[1]]


def join_blocks(*refs):
    total = pair_sum(refs[:4])
    rows = total.shape[0] // 4
    for k, block_ref in enumerate(refs[4:]):
        block_ref[...] = total[k * rows : (k + 1) * rows].astype(bf16)


def finish(
    d_h_ref, peer_ref, x_ref, d_x_ref, gain_ref, gain_grad_ref, grad_offset_ref, hot_ref, grad_x_ref, small_ref,
):
    d_h = d_h_ref[...].astype(f32) + peer_ref[...].astype(f32)
    x_float = x_ref[...].astype(f32)
    scale = rms_scale(x_float)
    normed = x_float * scale
    d_norm = d_h * gain_ref[...].reshape(1, -1)
    grad_x = d_x_ref[...] + scale * (
        d_norm - normed * jnp.mean(d_norm * normed, axis=-1, keepdims=True)
    )
    grad_x_ref[...] = grad_x.astype(bf16)
    heads, buckets = grad_offset_ref.shape[0] - 2, hot_ref.shape[1]
    small_ref[...] = jnp.zeros(small_ref.shape, f32)
    grad_rel = lax.dot_general(
        grad_offset_ref[...], hot_ref[...], (((1,), (0,)), ((), ())), precision=highest, preferred_element_type=f32
    )
    small_ref[:, :buckets] = grad_rel
    small_ref[heads : heads + 1, :] = jnp.sum(d_h * normed, axis=0, keepdims=True)
    small_ref[heads + 1 : heads + 2, :] = gain_grad_ref[...]


def expert_grads(left_ref, right_ref, out_ref, held_ref, sems):
    count = held_ref.shape[1]
    copies = []
    for at in range(out_ref.shape[0] // count):
        rows = pl.ds(at * count, count)
        held_ref[at] = dot(left_ref[:, rows], right_ref[...], 0, 0)
        copies.append(pltpu.make_async_copy(held_ref.at[at], out_ref.at[rows, :], sems.at[at]))
        copies[-1].start()
    for copy in copies:
        copy.wait()


def experts_pad(experts):
    return -(-experts // 128) * 128


def make_per_device(mesh):
    n_ex, n_row = mesh.shape["ex"], mesh.shape["row"]
    groups = n_ex * n_row

    def hop(values, axis, step):
        return lax.ppermute(values, axis, [(i, i ^ step) for i in range(mesh.shape[axis])])

    def whole_cube(rows):
        return n_ex == 4 and n_row == 4 and rows == 48

    def gather_blocks(shard, meanwhile):
        rows, width = shard.shape
        if whole_cube(rows):
            near, far, farther = (hop(shard, "ex", k) for k in (1, 2, 3))
            x_own, y_own = hop(shard, "row", 1), hop(shard, "row", 2)
            near, x_own, y_own = lax.optimization_barrier((near, x_own, y_own))
            xs, ys = [x_own, hop(near, "row", 1)], [y_own, hop(near, "row", 2)]
            diagonal = [hop(x_own, "row", 2)]
            beside = meanwhile(near)
            far, farther, diagonal[0], *beside = lax.optimization_barrier((far, farther, diagonal[0], *beside))
            for part in (far, farther):
                xs.append(hop(part, "row", 1))
                ys.append(hop(part, "row", 2))
            diagonal += [hop(ys[1], "row", 1), hop(xs[2], "row", 2), hop(ys[3], "row", 1)]
            return [shard, near, far, farther, *xs, *ys, *diagonal], beside
        part = lax.all_gather(shard, "ex", axis=0)
        part = jnp.broadcast_to(part[None], (n_row, n_ex, rows, width))
        part = lax.all_to_all(part, "row", split_axis=0, concat_axis=0, tiled=True)
        return [part.transpose(1, 0, 2, 3).reshape(groups * rows, width)], meanwhile(shard)

    def scatter_groups(grads, rows):
        part = grads.astype(bf16).reshape(n_ex, n_row, rows, -1).transpose(1, 0, 2, 3)
        part = lax.all_to_all(part, "row", split_axis=0, concat_axis=0, tiled=True)
        part = jnp.sum(part.astype(f32), axis=0).astype(bf16)
        part = lax.all_to_all(part, "ex", split_axis=0, concat_axis=0, tiled=True)
        return jnp.sum(part.astype(f32), axis=0)

    def plane_hops(parts):
        return [hop(part, "row", m + 1) for m, part in enumerate(parts)]

    def line_hops(parts):
        return [hop(part, "ex", k + 1) for k, part in enumerate(parts)]

    def sum_groups(values):
        for axis in ("row", "ex"):
            step = 1
            while step < mesh.shape[axis]:
                values = values + hop(values, axis, step)
                step *= 2
        return values

    def per_device(
        x_in,
        gain_attn,
        w_qkv,
        rel_bias,
        w_out,
        gain_ffn,
        w_router,
        w_up,
        w_down,
        seg_ids,
        expert_ids,
        slot_ids,
        drop_flags,
        d_out,
    ):
        seq_len, width = x_in.shape
        heads_here = rel_bias.shape[1]
        inner = w_qkv.shape[2]
        own_rows = w_qkv.shape[1]
        experts = w_router.shape[1]
        wide = inner + experts_pad(experts)
        half = d_out.shape[1]
        hidden = w_up.shape[2]
        device_at = jnp.stack([lax.axis_index(axis).astype(jnp.int32) for axis in ("ex", "row", "col")])
        device_at, w_qkv = lax.optimization_barrier((device_at, w_qkv))
        cube = whole_cube(own_rows)
        capacity = 5 * seq_len // (4 * experts)
        tight = cube and experts == 16 and capacity == 20 and width == 768
        slots = capacity if tight else -(-capacity // 8) * 8
        slot_total = experts * slots
        packed_slots = (experts, slots * width // 128, 128) if tight else (slot_total, width)
        exchange = packed_slots if tight else (experts, slots, width)
        slot_scratch = (
            pltpu.VMEM((slot_total, width), bf16),
            pltpu.VMEM((slot_total, width), bf16),
            pltpu.VMEM((experts * 24, 128), f32),
        )
        gather_order = GATHER_ORDER if cube else None

        (packed,) = vmem_call(
            pack_weights,
            (shape((own_rows, 3 * inner + wide), bf16),),
            0,
            w_qkv,
            w_out.T,
            w_router.T,
        )

        def round_weights(after):
            late_up, late_down, _ = lax.optimization_barrier((w_up[0], w_down[0], after))
            return [late_up.astype(bf16), late_down.astype(bf16)]

        blocks, (up_w, down_w) = gather_blocks(packed, round_weights)
        g_peer = swap_cores(d_out)

        span = 2 * seq_len
        offsets = jnp.arange(span, dtype=jnp.int32) - (seq_len - 1)
        offset_hot = (
            bucket_of(offsets)[:, None] == jnp.arange(BUCKETS, dtype=jnp.int32)[None, :]
        ).astype(f32)
        per_offset = jnp.einsum("bh,ob->ho", rel_bias, offset_hot, precision=highest)
        square = seq_len * seq_len * heads_here * HEAD
        attn_part, qkv, probs, context, qkv_w, out_w, router_w, normed_turned, normed_mine = vmem_call(
            functools.partial(attend_forward, gather_order),
            (
                shape((seq_len, width), bf16),
                shape((seq_len, 3 * inner), bf16),
                shape((heads_here, seq_len, seq_len), f32),
                shape((seq_len, inner), bf16),
                shape((width, 3 * inner), bf16),
                shape((width, inner), bf16),
                shape((width, wide - inner), bf16),
                shape((width, seq_len), bf16),
                shape((half, seq_len), bf16),
            ),
            8 * seq_len * width * inner + 4 * square,
            x_in,
            gain_attn,
            per_offset,
            seg_ids,
            *blocks,
            scalars=(device_at,),
        )
        attn_peer = swap_cores(attn_part)
        slot_of = expert_ids * slots + slot_ids
        if tight:
            spare_of = experts * 16 + expert_ids * 4 + slot_ids - 16
            slot_of = jnp.where(slot_ids < 16, expert_ids * 16 + slot_ids, spare_of)
        slot_of = jnp.where(drop_flags == 1, slot_total, slot_of)[None]
        (send,) = vmem_call(
            dispatch,
            (shape(packed_slots, bf16),),
            2 * seq_len * slot_total * width,
            x_in,
            attn_part,
            attn_peer,
            gain_ffn,
            slot_of,
            d_out,
            scalars=(device_at,),
        )
        got = lax.all_to_all(send.reshape(exchange), ("ex", "row"), 0, 0, tiled=True).reshape(packed_slots)
        if cube:
            later_normed, got = lax.optimization_barrier((normed_mine, got))
            normed_hops = plane_hops([later_normed] * 2)
        crossing, mine, router_probs, gate_part, rows, d_y, act_b, d_pre = vmem_call(
            functools.partial(run_expert, experts, n_row),
            (
                shape((slot_total, width + 128), bf16),
                shape((slot_total, width), f32),
                shape((slot_total, experts), f32),
                shape((slot_total, 1), f32),
                shape((slot_total, width), bf16),
                shape((slot_total, width), bf16),
                shape((slot_total, hidden), bf16),
                shape((slot_total, hidden), bf16),
            ),
            8 * slot_total * width * hidden,
            got,
            swap_cores(got),
            router_w,
            up_w,
            down_w,
            scalars=(device_at,),
            scratch=(pltpu.VMEM((slot_total, width), f32), *slot_scratch),
        )
        if cube:
            crossing, g_peer, *normed_hops = lax.optimization_barrier((crossing, g_peer, *normed_hops))
        back, grad_router = vmem_call(
            functools.partial(settle, n_row),
            (shape(packed_slots, bf16), shape((experts, width), f32)),
            2 * slot_total * half * experts,
            mine,
            swap_cores(crossing),
            router_probs,
            gate_part,
            router_w,
            rows,
            scalars=(device_at,),
        )
        home = lax.all_to_all(back.reshape(exchange), ("ex", "row"), 0, 0, tiled=True).reshape(packed_slots)
        half_scratch = (pltpu.VMEM((slot_total, half), bf16), slot_scratch[2])
        (d_h_mine,) = vmem_call(
            arrive,
            (shape((seq_len, half), bf16),),
            seq_len * slot_total * width,
            home,
            slot_of,
            scratch=half_scratch,
        )

        def land_at_home(home):
            (layer_out,) = vmem_call(
                land,
                (shape((seq_len, half), bf16),),
                seq_len * slot_total * width,
                home,
                slot_of,
                x_in,
                attn_part,
                attn_peer,
                scalars=(device_at,),
                scratch=half_scratch,
            )
            return layer_out

        def grads_of_expert(left, right):
            dims = (left.shape[1], right.shape[1])
            chunks = dims[0] // 256
            return pl.pallas_call(
                expert_grads,
                out_shape=shape(dims, f32),
                in_specs=[pl.BlockSpec(memory_space=pltpu.VMEM)] * 2,
                out_specs=pl.BlockSpec(memory_space=pltpu.HBM),
                scratch_shapes=[
                    pltpu.VMEM((chunks, dims[0] // chunks, dims[1]), f32),
                    pltpu.SemaphoreType.DMA((chunks,)),
                ],
                compiler_params=pltpu.CompilerParams(vmem_limit_bytes=16 * 2**20),
                cost_estimate=pl.CostEstimate(
                    flops=2 * slot_total * width * hidden, bytes_accessed=6 * width * hidden, transcendentals=0
                ),
            )(left, right)

        quarter = (width // 4, 3 * inner // 4) if cube else (width, 3 * inner)
        pieces = 4 if cube else 1
        if cube:
            d_h_mine, from_x, from_y = lax.optimization_barrier((d_h_mine, *normed_hops))
            normed_hops += [hop(from_x[: half // 2], "row", 2), hop(from_y[half // 2 :], "row", 1)]
        d_x_one, grad_gain_ffn, d_context, *out_pieces = vmem_call(
            functools.partial(come_home, cube),
            (
                shape((seq_len, width), f32),
                shape((1, width), f32),
                shape((seq_len, inner), bf16),
                *[shape((quarter[0], inner), bf16)] * pieces,
            ),
            4 * seq_len * width * inner,
            d_h_mine,
            swap_cores(d_h_mine),
            x_in,
            attn_part,
            attn_peer,
            d_out,
            g_peer,
            gain_ffn,
            out_w,
            context,
            scalars=(device_at,),
            scratch=(pltpu.VMEM((width, inner), bf16),),
        )
        d_h_part, grad_offset, *d_qkv_turned = vmem_call(
            functools.partial(attend_backward, cube),
            (
                shape((seq_len, width), bf16),
                shape((heads_here + 2, span), f32),
                *[shape((quarter[1], seq_len), bf16)] * pieces,
            ),
            6 * seq_len * width * inner + 10 * square,
            d_context,
            qkv,
            probs,
            qkv_w,
            scalars=(device_at,),
            scratch=(pltpu.VMEM((3 * inner, seq_len), bf16),),
        )
        grad_x, small = vmem_call(
            finish,
            (shape((seq_len, width), bf16), shape((heads_here + 2, width), f32)),
            0,
            d_h_part,
            swap_cores(d_h_part),
            x_in,
            d_x_one,
            gain_attn,
            grad_gain_ffn,
            grad_offset,
            offset_hot,
        )
        if cube:
            *normed_hops, _ = lax.optimization_barrier((*normed_hops, d_h_part))
            normed_near = jnp.concatenate(normed_hops, axis=0)
            normed_peer = swap_cores(normed_near)
            late_home, act_b, d_y, _ = lax.optimization_barrier((home, act_b, d_y, small))
            d_qkv_hops = plane_hops(d_qkv_turned[1:])
            *d_qkv_hops, layer_out, grad_down = lax.optimization_barrier(
                (*d_qkv_hops, land_at_home(late_home), grads_of_expert(act_b, d_y))
            )
            terms = vmem_call(
                qkv_terms,
                [shape((own_rows + 8, 3 * inner), bf16)] * 4,
                6 * seq_len * width * inner,
                normed_turned,
                small,
                grad_router,
                normed_near,
                normed_peer,
                d_qkv_turned[0],
                *d_qkv_hops,
                scalars=(device_at,),
                scratch=(pltpu.VMEM((width, quarter[1]), bf16),),
            )
            line = line_hops(terms[1:])
            rows, d_pre, _ = lax.optimization_barrier((rows, d_pre, terms[0]))
            grad_up = grads_of_expert(rows, d_pre)
            *out_pieces, _ = lax.optimization_barrier((*out_pieces, grad_up))
            *line, grad_up = lax.optimization_barrier((*line, grad_up))
            split = vmem_call(
                join_line,
                [shape((own_rows, 512), bf16)] * 4,
                0,
                terms[0],
                *line,
                scalars=(device_at,),
            )
            last = plane_hops(split[1:])
            grad_qkv, gain_one, gain_two, grad_rel, grad_router = vmem_call(
                join_plane,
                (
                    shape((3, own_rows, inner), f32),
                    shape((width,), f32),
                    shape((width,), f32),
                    shape((heads_here, BUCKETS), f32),
                    shape((experts, own_rows), f32),
                ),
                0,
                split[0],
                *last,
                scalars=(device_at,),
                scratch=(pltpu.VMEM((own_rows, 3 * inner), f32),),
            )
            out_hops = plane_hops(out_pieces[1:])
            out_blocks = vmem_call(
                join_blocks,
                [shape((own_rows, inner), bf16)] * 4,
                0,
                out_pieces[0],
                *out_hops,
            )
            *out_blocks, _ = lax.optimization_barrier((*out_blocks, last[0]))
            out_blocks = (out_blocks[0], *line_hops(out_blocks[1:]))
            grad_out = sum(part.astype(f32) for part in out_blocks)
        else:
            layer_out = land_at_home(home)
            grad_down, grad_up = grads_of_expert(act_b, d_y), grads_of_expert(rows, d_pre)
            grad_qkv = scatter_groups(dot(normed_turned, d_qkv_turned[0], 1, 1), own_rows)
            grad_qkv = grad_qkv.reshape(own_rows, 3, inner).transpose(1, 0, 2)
            grad_out = scatter_groups(out_pieces[0], own_rows)
            small = sum_groups(jnp.concatenate([small, grad_router]))
            gain_one, gain_two = small[heads_here], small[heads_here + 1]
            grad_rel = small[:heads_here, :BUCKETS]
            own_at = (device_at[0] * n_row + device_at[1]) * own_rows
            grad_router = lax.dynamic_slice(small, (heads_here + 2, own_at), (experts, own_rows))
        return (
            layer_out,
            grad_x,
            gain_one,
            grad_qkv,
            grad_rel.T,
            grad_out.T,
            gain_two,
            grad_router.T,
            grad_up[None],
            grad_down[None],
        )

    return per_device


def solution(mesh):
    return jax.shard_map(
        make_per_device(mesh),
        mesh=mesh,
        in_specs=(
            P(("ex", "row"), None),
            P(),
            P(None, ("ex", "row"), "col"),
            P(None, "col"),
            P("col", ("ex", "row")),
            P(),
            P(("ex", "row"), None),
            P(("ex", "row"), None, "col"),
            P(("ex", "row"), "col", None),
            P(("ex", "row"), None),
            P(("ex", "row")),
            P(("ex", "row")),
            P(("ex", "row")),
            P(("ex", "row"), "col"),
        ),
        out_specs=(
            P(("ex", "row"), "col"),
            P(("ex", "row"), None),
            P(),
            P(None, ("ex", "row"), "col"),
            P(None, "col"),
            P("col", ("ex", "row")),
            P(),
            P(("ex", "row"), None),
            P(("ex", "row"), None, "col"),
            P(("ex", "row"), "col", None),
        ),
        check_vma=False,
    )
```

```python
import functools
import math

import jax
import jax.numpy as jnp
from jax import lax
from jax.experimental import pallas as pl
from jax.experimental.pallas import tpu as pltpu
from jax.sharding import PartitionSpec as P

HEAD = 64
BUCKETS = 32

norm_eps = 1e-06
bucket_edges = (12, 16, 23, 32, 46, 64, 91)
highest = lax.Precision.HIGHEST
bf16 = jnp.bfloat16
f32 = jnp.float32

GATHER_ORDER = tuple(((k, m),) for m in range(4) for k in range(4))

def bucket_of(offset):
    distance = jnp.abs(offset)
    far_part = jnp.zeros(distance.shape, jnp.int32)
    for edge_at in bucket_edges:
        far_part = far_part + (distance >= edge_at).astype(jnp.int32)
    inside = jnp.where(distance < 8, distance, far_part + jnp.int32(8))
    upper = jnp.where(offset > 0, jnp.int32(BUCKETS // 2), jnp.int32(0))
    return inside + upper


def rms_scale(values):
    return lax.rsqrt(jnp.mean(values * values, axis=-1, keepdims=True) + norm_eps)


def dot(a, b, ca, cb):
    return lax.dot_general(a, b, (((ca,), (cb,)), ((), ())), preferred_element_type=f32)


def swap_cores(values):
    return lax.ppermute(values, "col", [(0, 1), (1, 0)])


def shape(dims, dtype):
    return jax.ShapeDtypeStruct(tuple(dims), dtype)


def vmem_call(kernel, out_shape, flops, *args, scalars=(), scratch=(), limit=12):
    nbytes = sum(math.prod(v.shape) * v.dtype.itemsize for v in (*args, *out_shape))
    spec = pl.BlockSpec(memory_space=pltpu.VMEM)
    limit = limit if nbytes < 16 * 2**20 else 48
    return pl.pallas_call(
        kernel,
        out_shape=out_shape,
        in_specs=[pl.BlockSpec(memory_space=pltpu.SMEM)] * len(scalars) + [spec] * len(args),
        out_specs=[spec] * len(out_shape),
        scratch_shapes=scratch,
        compiler_params=pltpu.CompilerParams(vmem_limit_bytes=limit * 2**20),
        cost_estimate=pl.CostEstimate(flops=flops, bytes_accessed=nbytes, transcendentals=0),
    )(*scalars, *args)


def block_rows(at_ref, order, count):
    if order is None:
        return [pl.ds(0, count)]
    ex_at, row_at = at_ref[0], at_ref[1]
    return [
        pl.ds(pl.multiple_of(((ex_at ^ k) * 4 + (row_at ^ m)) * count, 16), count)
        for part in order
        for k, m in part
    ]


def eye(size):
    dims = (size, size)
    same = lax.broadcasted_iota(jnp.int32, dims, 0) == lax.broadcasted_iota(jnp.int32, dims, 1)
    return same.astype(bf16)


def pack_weights(qkv_in, out_in, router_in, packed_out, qkv_ref, out_turned_ref, router_turned_ref, packed_ref, sems):
    pairs = ((qkv_in, qkv_ref), (out_in, out_turned_ref), (router_in, router_turned_ref))
    copies = [pltpu.make_async_copy(source, target, sems.at[i]) for i, (source, target) in enumerate(pairs)]
    for copy in copies:
        copy.start()
    inner, experts = qkv_ref.shape[2], router_turned_ref.shape[0]
    packed_ref[:, 4 * inner :] = jnp.zeros((packed_ref.shape[0], packed_ref.shape[1] - 4 * inner), bf16)
    for copy in copies:
        copy.wait()
    for part in range(3):
        packed_ref[:, part * inner : (part + 1) * inner] = qkv_ref[part].astype(bf16)
    packed_ref[:, 3 * inner : 4 * inner] = out_turned_ref[...].astype(bf16)
    router = dot(router_turned_ref[...].astype(bf16), eye(experts), 0, 0)
    packed_ref[:, 4 * inner : 4 * inner + experts] = router.astype(bf16)
    copy = pltpu.make_async_copy(packed_ref, packed_out, sems.at[3])
    copy.start()
    copy.wait()


def spread_bias(offset_ref, bias_ref):
    heads, seq_len, _ = bias_ref.shape
    span = offset_ref.shape[1]
    for at in range(heads):
        spread = jnp.broadcast_to(offset_ref[at : at + 1, :], (seq_len, span))
        bias_ref[at] = pltpu.roll(spread, span - seq_len + 1, 1, stride=1, stride_axis=0)[:, :seq_len]


def attend_forward(order, at_ref, x_ref, gain_ref, bias_ref, seg_ref, *refs):
    *block_refs, part_ref, qkv_ref, probs_ref, ctx_ref, w_ref, out_w_ref, router_ref, turned_ref, half_ref = refs
    seq_len = x_ref.shape[0]
    heads, inner = probs_ref.shape[0], ctx_ref.shape[1]
    for rows, block_ref in zip(block_rows(at_ref, order, block_refs[0].shape[0]), block_refs):
        w_ref[rows, :] = block_ref[:, : 3 * inner]
        out_w_ref[rows, :] = block_ref[:, 3 * inner : 4 * inner]
        router_ref[rows, :] = block_ref[:, 4 * inner :]
    x_float = x_ref[...].astype(f32)
    h_one = (x_float * rms_scale(x_float) * gain_ref[...].reshape(1, -1)).astype(bf16)
    turned_ref[...] = dot(h_one, eye(seq_len), 0, 0).astype(bf16)
    half = half_ref.shape[0]
    half_ref[...] = jnp.where(at_ref[2] == 0, turned_ref[:half, :], turned_ref[half:, :])
    documents = lax.broadcasted_iota(jnp.int32, (8, seq_len), 0) == seg_ref[...]
    same_doc = dot(documents.astype(bf16), documents.astype(bf16), 0, 0) > 0.5
    qkv_ref[...] = dot(h_one, w_ref[...], 1, 0).astype(bf16)
    for at in range(heads):
        take = lambda part: qkv_ref[:, part * inner + at * HEAD : part * inner + (at + 1) * HEAD]
        scores = jnp.where(same_doc, dot(take(0), take(1), 1, 1) * 0.125 + bias_ref[at], -1e30)
        expo = jnp.exp(scores - jnp.max(scores, axis=1, keepdims=True))
        probs = expo * (1.0 / jnp.sum(expo, axis=1, keepdims=True))
        probs_ref[at] = probs
        ctx = dot(probs.astype(bf16), take(2), 1, 0)
        ctx_ref[:, at * HEAD : (at + 1) * HEAD] = ctx.astype(bf16)
    part_ref[...] = dot(ctx_ref[...], out_w_ref[...], 1, 1).astype(bf16)


def spare_rows(experts, chunk):
    dims = (experts * 24, experts * 4)
    row, column = lax.broadcasted_iota(jnp.int32, dims, 0), lax.broadcasted_iota(jnp.int32, dims, 1)
    expert = lax.shift_right_logical(row * 2731, 16)
    inside = row - expert * 24
    wanted = expert * 4 + (inside - chunk * 4)
    return ((column == wanted) & (inside >= chunk * 4) & (inside < chunk * 4 + 4)).astype(bf16)


def pack_slots(values, packed_ref):
    if len(packed_ref.shape) == 2:
        packed_ref[...] = values.astype(bf16)
        return
    experts, chunks = packed_ref.shape[0], values.shape[1] // 128
    values = values.astype(bf16)
    spare = 0.0
    for c in range(chunks):
        chunk = values[:, c * 128 : (c + 1) * 128]
        for e in range(experts):
            packed_ref[e, c * 16 : (c + 1) * 16, :] = chunk[e * 16 : (e + 1) * 16]
        spare = spare + dot(spare_rows(experts, c), chunk[experts * 16 :], 1, 0)
    for e in range(experts):
        packed_ref[e, chunks * 16 :, :] = spare[e * 24 : (e + 1) * 24].astype(bf16)


def unpack_slots(packed_ref, low, target_ref, spare_ref):
    experts, chunks = packed_ref.shape[0], target_ref.shape[1] // 128
    first = (packed_ref.shape[1] - 24) // 16 * 16
    for e in range(experts):
        spare_ref[e * 24 : (e + 1) * 24, :] = packed_ref[e, first:, :].astype(f32)
    spare = spare_ref[...].astype(bf16)
    for c in range(chunks):
        lanes = slice(c * 128, (c + 1) * 128)
        for e in range(experts):
            rows = slice((low + c) * 16, (low + c + 1) * 16)
            target_ref[e * 16 : (e + 1) * 16, lanes] = packed_ref[e, rows, :]
        target_ref[experts * 16 :, lanes] = dot(spare_rows(experts, low + c), spare, 0, 0).astype(bf16)


def dispatch(at_ref, x_ref, part_ref, peer_ref, gain_ref, slot_ref, g_ref, send_ref):
    half = g_ref.shape[1]
    x_one = x_ref[...].astype(f32) + (part_ref[...].astype(f32) + peer_ref[...].astype(f32))
    h_two = (x_one * rms_scale(x_one) * gain_ref[...].reshape(1, -1)).astype(bf16)
    mine = jnp.where(at_ref[2] == 0, h_two[:, :half], h_two[:, half:])
    slots = send_ref.shape[0] * (1 if len(send_ref.shape) == 2 else 20)
    dims = (slots, x_ref.shape[0])
    place = (lax.broadcasted_iota(jnp.int32, dims, 0) == slot_ref[...]).astype(bf16)
    sent = jnp.concatenate([dot(place, mine, 1, 0), dot(place, g_ref[...], 1, 0)], axis=1)
    pack_slots(sent, send_ref)


def run_expert(
    experts, row_size, at_ref, got_ref, peer_ref, router_ref, up_ref, down_ref,
    cross_ref, mine_ref, probs_ref, gate_part_ref, rows_ref, d_y_ref, act_ref, d_pre_ref, d_in_ref,
    got_rows_ref, peer_rows_ref, spare_ref,
):
    half = rows_ref.shape[1] // 2
    if len(got_ref.shape) == 3:
        unpack_slots(got_ref, 0, got_rows_ref, spare_ref)
        unpack_slots(peer_ref, 0, peer_rows_ref, spare_ref)
        got_ref, peer_ref = got_rows_ref, peer_rows_ref
    hidden = up_ref.shape[1]
    first_core = at_ref[2] == 0
    for at, refs in ((0, (got_ref, peer_ref)), (1, (peer_ref, got_ref))):
        pick = lambda lo: jnp.where(first_core, refs[0][:, lo : lo + half], refs[1][:, lo : lo + half])
        rows_ref[:, at * half : (at + 1) * half] = pick(0)
        d_y_ref[:, at * half : (at + 1) * half] = pick(half)
    rows, g_rows = rows_ref[...], d_y_ref[...].astype(f32)
    logits = dot(rows, router_ref[...], 1, 0)[:, :experts]
    expo = jnp.exp(logits - jnp.max(logits, axis=1, keepdims=True))
    probs = expo / jnp.sum(expo, axis=1, keepdims=True)
    probs_ref[...] = probs
    expert_at = at_ref[0] * row_size + at_ref[1]
    chosen = lax.broadcasted_iota(jnp.int32, probs.shape, 1) == expert_at
    gate = jnp.sum(jnp.where(chosen, probs, 0.0), axis=1, keepdims=True)
    d_y_ref[...] = (g_rows * gate).astype(bf16)
    step = 768 if hidden % 768 == 0 else hidden
    y_part = None
    for lo in range(0, hidden, step):
        cols = pl.ds(lo, step)
        pre_act = dot(rows_ref[...], up_ref[:, cols], 1, 0)
        cdf = 0.5 * (1.0 + lax.erf(pre_act * (1.0 / math.sqrt(2.0))))
        pdf = jnp.exp(-0.5 * pre_act * pre_act) * (1.0 / math.sqrt(2.0 * math.pi))
        act = (pre_act * cdf).astype(bf16)
        act_ref[:, cols] = act
        y_more = dot(act, down_ref[cols, :], 1, 0)
        d_pre = (dot(d_y_ref[...], down_ref[cols, :], 1, 1) * (cdf + pre_act * pdf)).astype(bf16)
        d_pre_ref[:, cols] = d_pre
        d_more = dot(d_pre, up_ref[:, cols], 1, 1)
        if lo == 0:
            y_part = y_more
            d_in_ref[...] = d_more
        else:
            y_part = y_part + y_more
            d_in_ref[...] += d_more
    gate_part = jnp.sum(g_rows * y_part, axis=1, keepdims=True)
    high = gate_part.astype(bf16)
    low = (gate_part - high.astype(f32)).astype(bf16)
    gate_part_ref[...] = high.astype(f32) + low.astype(f32)
    lane = lax.broadcasted_iota(jnp.int32, (rows.shape[0], 128), 1)
    beside = jnp.where(lane == 0, high.astype(f32), jnp.where(lane == 1, low.astype(f32), 0.0))
    cross_ref[:, 2 * half :] = beside.astype(bf16)
    d_in = d_in_ref[...]
    mine_ref[:, :half] = jnp.where(first_core, y_part[:, :half], y_part[:, half:])
    mine_ref[:, half:] = jnp.where(first_core, d_in[:, :half], d_in[:, half:])
    cross_ref[:, :half] = jnp.where(first_core, y_part[:, half:], y_part[:, :half]).astype(bf16)
    cross_ref[:, half : 2 * half] = jnp.where(first_core, d_in[:, half:], d_in[:, :half]).astype(bf16)


def settle(
    row_size, at_ref, mine_ref, crossed_ref, probs_ref, gate_part_ref, router_ref, rows_ref,
    back_ref, grad_router_ref,
):
    half = mine_ref.shape[1] // 2
    probs = probs_ref[...]
    expert_at = at_ref[0] * row_size + at_ref[1]
    chosen = (lax.broadcasted_iota(jnp.int32, probs.shape, 1) == expert_at).astype(f32)
    gate = jnp.sum(probs * chosen, axis=1, keepdims=True)
    beside = crossed_ref[:, 2 * half :].astype(f32)
    d_gate = gate_part_ref[...] + (beside[:, 0:1] + beside[:, 1:2])
    d_logits = (d_gate * gate * (chosen - probs)).astype(bf16)
    router_w = router_ref[...][:, : probs.shape[1]]
    router_mine = jnp.where(at_ref[2] == 0, router_w[:half], router_w[half:])
    y_gated = gate * (mine_ref[:, :half] + crossed_ref[:, :half].astype(f32))
    d_in = mine_ref[:, half:] + crossed_ref[:, half : 2 * half].astype(f32) + dot(d_logits, router_mine, 1, 1)
    pack_slots(jnp.concatenate([y_gated, d_in], axis=1), back_ref)
    grad_router_ref[...] = dot(d_logits, rows_ref[...], 0, 0)


def from_slots(home_ref, slot_ref, low, rows_ref, spare_ref):
    if len(home_ref.shape) == 3:
        unpack_slots(home_ref, low, rows_ref, spare_ref)
    else:
        rows_ref[...] = home_ref[:, low * 128 : low * 128 + rows_ref.shape[1]]
    dims = (rows_ref.shape[0], slot_ref.shape[1])
    place = (lax.broadcasted_iota(jnp.int32, dims, 0) == slot_ref[...]).astype(bf16)
    return dot(place, rows_ref[...], 0, 0)


def arrive(home_ref, slot_ref, d_h_ref, rows_ref, spare_ref):
    low = d_h_ref.shape[1] // 128
    d_h_ref[...] = from_slots(home_ref, slot_ref, low, rows_ref, spare_ref).astype(bf16)


def land(at_ref, home_ref, slot_ref, x_ref, part_ref, peer_ref, layer_ref, rows_ref, spare_ref):
    half = layer_ref.shape[1]
    y_home = from_slots(home_ref, slot_ref, 0, rows_ref, spare_ref)
    mine = lambda ref: jnp.where(at_ref[2] == 0, ref[:, :half], ref[:, half:]).astype(f32)
    layer_ref[...] = (mine(x_ref) + (mine(part_ref) + mine(peer_ref)) + y_home).astype(bf16)


def come_home(
    cube, at_ref, mine_ref, peer_ref, x_ref, part_ref, part_peer_ref, g_ref, g_peer_ref,
    gain_ref, out_w_ref, ctx_ref, d_x_ref, gain_grad_ref, d_ctx_ref, *refs,
):
    *piece_refs, grads_ref = refs
    first_core = at_ref[2] == 0
    both = lambda a, b: jnp.concatenate(
        [jnp.where(first_core, a, b), jnp.where(first_core, b, a)], axis=1
    )
    d_h = both(mine_ref[...], peer_ref[...]).astype(f32)
    x_one = x_ref[...].astype(f32) + (part_ref[...].astype(f32) + part_peer_ref[...].astype(f32))
    g_full = both(g_ref[...], g_peer_ref[...]).astype(f32)
    scale = rms_scale(x_one)
    normed = x_one * scale
    gain_grad_ref[...] = jnp.sum(d_h * normed, axis=0, keepdims=True)
    d_norm = d_h * gain_ref[...].reshape(1, -1)
    d_x = g_full + scale * (d_norm - normed * jnp.mean(d_norm * normed, axis=-1, keepdims=True))
    d_x_ref[...] = d_x
    d_x_b = d_x.astype(bf16)
    d_ctx_ref[...] = dot(d_x_b, out_w_ref[...], 1, 0).astype(bf16)
    grads_ref[...] = dot(d_x_b, ctx_ref[...], 0, 0).astype(bf16)
    rows = grads_ref.shape[0] // 16
    for m, piece_ref in enumerate(piece_refs):
        if not cube:
            piece_ref[...] = grads_ref[...]
            continue
        for k in range(4):
            start = pl.multiple_of(((at_ref[0] ^ k) * 4 + (at_ref[1] ^ m)) * rows, 16)
            piece_ref[k * rows : (k + 1) * rows, :] = grads_ref[pl.ds(start, rows), :]


def attend_backward(cube, at_ref, d_ctx_ref, qkv_ref, probs_ref, w_ref, d_h_ref, grad_offset_ref, *refs):
    *piece_refs, turned_ref = refs
    heads, seq_len, _ = probs_ref.shape
    inner = d_ctx_ref.shape[1]
    span = grad_offset_ref.shape[1]
    flip = (
        lax.broadcasted_iota(jnp.int32, (seq_len, seq_len), 0)
        + lax.broadcasted_iota(jnp.int32, (seq_len, seq_len), 1)
        == seq_len - 1
    ).astype(bf16)
    grad_offset_ref[...] = jnp.zeros(grad_offset_ref.shape, f32)
    for at in range(heads):
        cols = lambda part: pl.ds(part * inner + at * HEAD, HEAD)
        d_ctx = d_ctx_ref[:, at * HEAD : (at + 1) * HEAD]
        probs = probs_ref[at]
        d_probs = dot(d_ctx, qkv_ref[:, cols(2)], 1, 1)
        row_delta = jnp.sum(probs * d_probs, axis=1, keepdims=True)
        d_scores = (probs * (d_probs - row_delta)).astype(bf16)
        turned_ref[cols(0), :] = (dot(qkv_ref[:, cols(1)], d_scores, 0, 1) * 0.125).astype(bf16)
        turned_ref[cols(1), :] = (dot(qkv_ref[:, cols(0)], d_scores, 0, 0) * 0.125).astype(bf16)
        turned_ref[cols(2), :] = dot(d_ctx, probs.astype(bf16), 0, 0).astype(bf16)
        flipped = jnp.concatenate(
            [dot(flip, d_scores, 1, 0), jnp.zeros((seq_len, span - seq_len), f32)], axis=1
        )
        lined = pltpu.roll(flipped, 0, 1, stride=1, stride_axis=0)
        grad_offset_ref[at : at + 1, :] = jnp.sum(lined, axis=0, keepdims=True)
    size = piece_refs[0].shape[0]
    for m, piece_ref in enumerate(piece_refs):
        start = pl.multiple_of((at_ref[1] ^ m) * size, 16) if cube else 0
        piece_ref[...] = turned_ref[pl.ds(start, size), :]
    d_h_ref[...] = dot(turned_ref[...], w_ref[...], 0, 1).astype(bf16)


def qkv_terms(at_ref, turned_ref, small_ref, router_ref, *refs):
    mine_ref, peer_ref, piece_refs, block_refs, grads_ref = refs[0], refs[1], refs[2:6], refs[6:10], refs[10]
    half = mine_ref.shape[0] // 3
    from_mine = from_peer = 0.0
    for m in range(1, 4):
        rows = slice((m - 1) * half, m * half)
        from_mine = from_mine + dot(mine_ref[rows, :], piece_refs[m][...], 1, 1)
        from_peer = from_peer + dot(peer_ref[rows, :], piece_refs[m][...], 1, 1)
    own = dot(turned_ref[...], piece_refs[0][...], 1, 1)
    first_core = at_ref[2] == 0
    grads_ref[:half, :] = (own[:half] + jnp.where(first_core, from_mine, from_peer)).astype(bf16)
    grads_ref[half:, :] = (own[half:] + jnp.where(first_core, from_peer, from_mine)).astype(bf16)
    rows, size = block_refs[0].shape[0] - 8, grads_ref.shape[1]
    width = small_ref.shape[1]
    part = width // 4
    for k, block_ref in enumerate(block_refs):
        block_ref[rows:, :width] = small_ref[...].astype(bf16)
        router = jnp.zeros((router_ref.shape[0], part), f32)
        for z in range(4):
            router = jnp.where((at_ref[0] ^ k) == z, router_ref[:, z * part : (z + 1) * part], router)
        for i in range(2):
            low = width + i * part
            block_ref[rows:, low : low + part] = router[i * 8 : (i + 1) * 8].astype(bf16)
        for m in range(4):
            start = ((at_ref[0] ^ k) * 4 + (at_ref[1] ^ m)) * rows
            block_ref[:rows, m * size : (m + 1) * size] = grads_ref[pl.ds(pl.multiple_of(start, 16), rows), :]


def pair_sum(refs):
    a, b, c, d = (ref[...].astype(f32) for ref in refs)
    return (a + b) + (c + d)


def join_line(at_ref, *refs):
    total = pair_sum(refs[:4])
    rows = refs[4].shape[0]
    size = total.shape[1] // 4
    width = size * 8 // 3
    part = width // 16
    extra = total[rows:]
    for m, piece_ref in enumerate(refs[4:]):
        piece_ref[...] = jnp.zeros(piece_ref.shape, bf16)
        piece_ref[:, :size] = total[:rows, m * size : (m + 1) * size].astype(bf16)
        for i in range(2):
            for j in range(width // 128):
                line = extra[6 + i : 7 + i, j * 128 : (j + 1) * 128]
                piece_ref[i * 8 + j : i * 8 + j + 1, 384:] = line.astype(bf16)
            router = jnp.zeros((8, part), f32)
            for row in range(4):
                low = width + i * 4 * part + row * part
                router = jnp.where((at_ref[1] ^ m) == row, extra[:, low : low + part], router)
            piece_ref[32 + i * 8 : 40 + i * 8, 384 : 384 + part] = router.astype(bf16)
        piece_ref[16:24, 384:] = extra[:, :128].astype(bf16)


def join_plane(at_ref, *refs):
    piece_refs, (out_ref, gain_one_ref, gain_two_ref, rel_ref, router_ref, line_ref) = refs[:4], refs[4:]
    size = line_ref.shape[1] // 4
    for quarter in range(4):
        piece = 0.0
        for m, piece_ref in enumerate(piece_refs):
            piece = jnp.where((at_ref[1] ^ m) == quarter, piece_ref[:, :size].astype(f32), piece)
        line_ref[:, quarter * size : (quarter + 1) * size] = piece
    inner = out_ref.shape[2]
    for part in range(3):
        out_ref[part] = line_ref[:, part * inner : (part + 1) * inner]
    extra = pair_sum([ref.at[:, 384:] for ref in piece_refs])
    for i, gain_ref in enumerate((gain_one_ref, gain_two_ref)):
        for j in range(gain_ref.shape[0] // 128):
            gain_ref[pl.ds(j * 128, 128)] = extra[i * 8 + j]
    rel_ref[...] = extra[16 : 16 + rel_ref.shape[0], : rel_ref.shape[1]]
    router_ref[...] = extra[32 : 32 + router_ref.shape[0], : router_ref.shape[1]]


def join_blocks(*refs):
    total = pair_sum(refs[:4])
    rows = total.shape[0] // 4
    for k, block_ref in enumerate(refs[4:]):
        block_ref[...] = total[k * rows : (k + 1) * rows].astype(bf16)


def finish(
    d_h_ref, peer_ref, x_ref, d_x_ref, gain_ref, gain_grad_ref, grad_offset_ref, hot_ref, grad_x_ref, small_ref,
):
    d_h = d_h_ref[...].astype(f32) + peer_ref[...].astype(f32)
    x_float = x_ref[...].astype(f32)
    scale = rms_scale(x_float)
    normed = x_float * scale
    d_norm = d_h * gain_ref[...].reshape(1, -1)
    grad_x = d_x_ref[...] + scale * (
        d_norm - normed * jnp.mean(d_norm * normed, axis=-1, keepdims=True)
    )
    grad_x_ref[...] = grad_x.astype(bf16)
    heads, buckets = grad_offset_ref.shape[0] - 2, hot_ref.shape[1]
    small_ref[...] = jnp.zeros(small_ref.shape, f32)
    grad_rel = lax.dot_general(
        grad_offset_ref[...], hot_ref[...], (((1,), (0,)), ((), ())), precision=highest, preferred_element_type=f32
    )
    small_ref[:, :buckets] = grad_rel
    small_ref[heads : heads + 1, :] = jnp.sum(d_h * normed, axis=0, keepdims=True)
    small_ref[heads + 1 : heads + 2, :] = gain_grad_ref[...]


def expert_grads(left_ref, right_ref, out_ref, held_ref, sems):
    count = held_ref.shape[1]
    copies = []
    for at in range(out_ref.shape[0] // count):
        rows = pl.ds(at * count, count)
        held_ref[at] = dot(left_ref[:, rows], right_ref[...], 0, 0)
        copies.append(pltpu.make_async_copy(held_ref.at[at], out_ref.at[rows, :], sems.at[at]))
        copies[-1].start()
    for copy in copies:
        copy.wait()


def experts_pad(experts):
    return -(-experts // 128) * 128


def make_per_device(mesh):
    n_ex, n_row = mesh.shape["ex"], mesh.shape["row"]
    groups = n_ex * n_row

    def hop(values, axis, step):
        return lax.ppermute(values, axis, [(i, i ^ step) for i in range(mesh.shape[axis])])

    def whole_cube(rows):
        return n_ex == 4 and n_row == 4 and rows == 48

    def gather_blocks(shard, meanwhile):
        rows, width = shard.shape
        if whole_cube(rows):
            near, far, farther = (hop(shard, "ex", k) for k in (1, 2, 3))
            x_own, y_own = hop(shard, "row", 1), hop(shard, "row", 2)
            near, x_own, y_own = lax.optimization_barrier((near, x_own, y_own))
            xs, ys = [x_own, hop(near, "row", 1)], [y_own, hop(near, "row", 2)]
            diagonal = [hop(x_own, "row", 2)]
            beside = meanwhile(near)
            far, farther, diagonal[0], *beside = lax.optimization_barrier((far, farther, diagonal[0], *beside))
            for part in (far, farther):
                xs.append(hop(part, "row", 1))
                ys.append(hop(part, "row", 2))
            diagonal += [hop(ys[1], "row", 1), hop(xs[2], "row", 2), hop(ys[3], "row", 1)]
            return [shard, near, far, farther, *xs, *ys, *diagonal], beside
        part = lax.all_gather(shard, "ex", axis=0)
        part = jnp.broadcast_to(part[None], (n_row, n_ex, rows, width))
        part = lax.all_to_all(part, "row", split_axis=0, concat_axis=0, tiled=True)
        return [part.transpose(1, 0, 2, 3).reshape(groups * rows, width)], meanwhile(shard)

    def scatter_groups(grads, rows):
        part = grads.astype(bf16).reshape(n_ex, n_row, rows, -1).transpose(1, 0, 2, 3)
        part = lax.all_to_all(part, "row", split_axis=0, concat_axis=0, tiled=True)
        part = jnp.sum(part.astype(f32), axis=0).astype(bf16)
        part = lax.all_to_all(part, "ex", split_axis=0, concat_axis=0, tiled=True)
        return jnp.sum(part.astype(f32), axis=0)

    def plane_hops(parts):
        return [hop(part, "row", m + 1) for m, part in enumerate(parts)]

    def line_hops(parts):
        return [hop(part, "ex", k + 1) for k, part in enumerate(parts)]

    def sum_groups(values):
        for axis in ("row", "ex"):
            step = 1
            while step < mesh.shape[axis]:
                values = values + hop(values, axis, step)
                step *= 2
        return values

    def per_device(
        x_in,
        gain_attn,
        w_qkv,
        rel_bias,
        w_out,
        gain_ffn,
        w_router,
        w_up,
        w_down,
        seg_ids,
        expert_ids,
        slot_ids,
        drop_flags,
        d_out,
    ):
        seq_len, width = x_in.shape
        heads_here = rel_bias.shape[1]
        inner = w_qkv.shape[2]
        own_rows = w_qkv.shape[1]
        experts = w_router.shape[1]
        wide = inner + experts_pad(experts)
        half = d_out.shape[1]
        hidden = w_up.shape[2]
        device_at = jnp.stack([lax.axis_index(axis).astype(jnp.int32) for axis in ("ex", "row", "col")])
        device_at, w_qkv = lax.optimization_barrier((device_at, w_qkv))
        cube = whole_cube(own_rows)
        capacity = 5 * seq_len // (4 * experts)
        tight = cube and experts == 16 and capacity == 20 and width == 768
        slots = capacity if tight else -(-capacity // 8) * 8
        slot_total = experts * slots
        packed_slots = (experts, slots * width // 128, 128) if tight else (slot_total, width)
        exchange = packed_slots if tight else (experts, slots, width)
        slot_scratch = (
            pltpu.VMEM((slot_total, width), bf16),
            pltpu.VMEM((slot_total, width), bf16),
            pltpu.VMEM((experts * 24, 128), f32),
        )
        gather_order = GATHER_ORDER if cube else None

        turned = (w_qkv, w_out.T, w_router.T)
        packed_shape = shape((own_rows, 3 * inner + wide), bf16)
        packed = pl.pallas_call(
            pack_weights,
            out_shape=packed_shape,
            in_specs=[pl.BlockSpec(memory_space=pltpu.HBM)] * 3,
            out_specs=pl.BlockSpec(memory_space=pltpu.HBM),
            scratch_shapes=[
                *(pltpu.VMEM(v.shape, v.dtype) for v in turned),
                pltpu.VMEM(packed_shape.shape, bf16),
                pltpu.SemaphoreType.DMA((4,)),
            ],
            compiler_params=pltpu.CompilerParams(vmem_limit_bytes=60 * 2**20),
        )(*turned)

        span = 2 * seq_len
        offsets = jnp.arange(span, dtype=jnp.int32) - (seq_len - 1)
        offset_hot = (
            bucket_of(offsets)[:, None] == jnp.arange(BUCKETS, dtype=jnp.int32)[None, :]
        ).astype(f32)
        per_offset = jnp.einsum("bh,ob->ho", rel_bias, offset_hot, precision=highest)

        def prepare(after):
            late_up, late_down, _ = lax.optimization_barrier((w_up[0], w_down[0], after))
            late_offset, _ = lax.optimization_barrier((per_offset, after))
            (bias,) = vmem_call(
                spread_bias, (shape((heads_here, seq_len, seq_len), f32),), 0, late_offset
            )
            return [late_up.astype(bf16), late_down.astype(bf16), bias]

        blocks, (up_w, down_w, bias) = gather_blocks(packed, prepare)
        g_peer = swap_cores(d_out)

        square = seq_len * seq_len * heads_here * HEAD
        attn_part, qkv, probs, context, qkv_w, out_w, router_w, normed_turned, normed_mine = vmem_call(
            functools.partial(attend_forward, gather_order),
            (
                shape((seq_len, width), bf16),
                shape((seq_len, 3 * inner), bf16),
                shape((heads_here, seq_len, seq_len), f32),
                shape((seq_len, inner), bf16),
                shape((width, 3 * inner), bf16),
                shape((width, inner), bf16),
                shape((width, wide - inner), bf16),
                shape((width, seq_len), bf16),
                shape((half, seq_len), bf16),
            ),
            8 * seq_len * width * inner + 4 * square,
            x_in,
            gain_attn,
            bias,
            seg_ids,
            *blocks,
            scalars=(device_at,),
        )
        attn_peer = swap_cores(attn_part)
        slot_of = expert_ids * slots + slot_ids
        if tight:
            spare_of = experts * 16 + expert_ids * 4 + slot_ids - 16
            slot_of = jnp.where(slot_ids < 16, expert_ids * 16 + slot_ids, spare_of)
        slot_of = jnp.where(drop_flags == 1, slot_total, slot_of)[None]
        (send,) = vmem_call(
            dispatch,
            (shape(packed_slots, bf16),),
            2 * seq_len * slot_total * width,
            x_in,
            attn_part,
            attn_peer,
            gain_ffn,
            slot_of,
            d_out,
            scalars=(device_at,),
        )
        got = lax.all_to_all(send.reshape(exchange), ("ex", "row"), 0, 0, tiled=True).reshape(packed_slots)
        if cube:
            later_normed, got = lax.optimization_barrier((normed_mine, got))
            normed_hops = plane_hops([later_normed] * 2)
        crossing, mine, router_probs, gate_part, rows, d_y, act_b, d_pre = vmem_call(
            functools.partial(run_expert, experts, n_row),
            (
                shape((slot_total, width + 128), bf16),
                shape((slot_total, width), f32),
                shape((slot_total, experts), f32),
                shape((slot_total, 1), f32),
                shape((slot_total, width), bf16),
                shape((slot_total, width), bf16),
                shape((slot_total, hidden), bf16),
                shape((slot_total, hidden), bf16),
            ),
            8 * slot_total * width * hidden,
            got,
            swap_cores(got),
            router_w,
            up_w,
            down_w,
            scalars=(device_at,),
            scratch=(pltpu.VMEM((slot_total, width), f32), *slot_scratch),
        )
        if cube:
            crossing, g_peer, *normed_hops = lax.optimization_barrier((crossing, g_peer, *normed_hops))
        back, grad_router = vmem_call(
            functools.partial(settle, n_row),
            (shape(packed_slots, bf16), shape((experts, width), f32)),
            2 * slot_total * half * experts,
            mine,
            swap_cores(crossing),
            router_probs,
            gate_part,
            router_w,
            rows,
            scalars=(device_at,),
        )
        home = lax.all_to_all(back.reshape(exchange), ("ex", "row"), 0, 0, tiled=True).reshape(packed_slots)
        half_scratch = (pltpu.VMEM((slot_total, half), bf16), slot_scratch[2])
        (d_h_mine,) = vmem_call(
            arrive,
            (shape((seq_len, half), bf16),),
            seq_len * slot_total * width,
            home,
            slot_of,
            scratch=half_scratch,
        )

        def land_at_home(home):
            (layer_out,) = vmem_call(
                land,
                (shape((seq_len, half), bf16),),
                seq_len * slot_total * width,
                home,
                slot_of,
                x_in,
                attn_part,
                attn_peer,
                scalars=(device_at,),
                scratch=half_scratch,
            )
            return layer_out

        def grads_of_expert(left, right):
            dims = (left.shape[1], right.shape[1])
            chunks = dims[0] // 256
            return pl.pallas_call(
                expert_grads,
                out_shape=shape(dims, f32),
                in_specs=[pl.BlockSpec(memory_space=pltpu.VMEM)] * 2,
                out_specs=pl.BlockSpec(memory_space=pltpu.HBM),
                scratch_shapes=[
                    pltpu.VMEM((chunks, dims[0] // chunks, dims[1]), f32),
                    pltpu.SemaphoreType.DMA((chunks,)),
                ],
                compiler_params=pltpu.CompilerParams(vmem_limit_bytes=16 * 2**20),
                cost_estimate=pl.CostEstimate(
                    flops=2 * slot_total * width * hidden, bytes_accessed=6 * width * hidden, transcendentals=0
                ),
            )(left, right)

        quarter = (width // 4, 3 * inner // 4) if cube else (width, 3 * inner)
        pieces = 4 if cube else 1
        if cube:
            d_h_mine, from_x, from_y = lax.optimization_barrier((d_h_mine, *normed_hops))
            normed_hops += [hop(from_x[: half // 2], "row", 2), hop(from_y[half // 2 :], "row", 1)]
        d_x_one, grad_gain_ffn, d_context, *out_pieces = vmem_call(
            functools.partial(come_home, cube),
            (
                shape((seq_len, width), f32),
                shape((1, width), f32),
                shape((seq_len, inner), bf16),
                *[shape((quarter[0], inner), bf16)] * pieces,
            ),
            4 * seq_len * width * inner,
            d_h_mine,
            swap_cores(d_h_mine),
            x_in,
            attn_part,
            attn_peer,
            d_out,
            g_peer,
            gain_ffn,
            out_w,
            context,
            scalars=(device_at,),
            scratch=(pltpu.VMEM((width, inner), bf16),),
        )
        d_h_part, grad_offset, *d_qkv_turned = vmem_call(
            functools.partial(attend_backward, cube),
            (
                shape((seq_len, width), bf16),
                shape((heads_here + 2, span), f32),
                *[shape((quarter[1], seq_len), bf16)] * pieces,
            ),
            6 * seq_len * width * inner + 10 * square,
            d_context,
            qkv,
            probs,
            qkv_w,
            scalars=(device_at,),
            scratch=(pltpu.VMEM((3 * inner, seq_len), bf16),),
        )
        grad_x, small = vmem_call(
            finish,
            (shape((seq_len, width), bf16), shape((heads_here + 2, width), f32)),
            0,
            d_h_part,
            swap_cores(d_h_part),
            x_in,
            d_x_one,
            gain_attn,
            grad_gain_ffn,
            grad_offset,
            offset_hot,
        )
        if cube:
            *normed_hops, _ = lax.optimization_barrier((*normed_hops, d_h_part))
            normed_near = jnp.concatenate(normed_hops, axis=0)
            normed_peer = swap_cores(normed_near)
            late_home, act_b, d_y, _ = lax.optimization_barrier((home, act_b, d_y, small))
            d_qkv_hops = plane_hops(d_qkv_turned[1:])
            *d_qkv_hops, layer_out, grad_down = lax.optimization_barrier(
                (*d_qkv_hops, land_at_home(late_home), grads_of_expert(act_b, d_y))
            )
            terms = vmem_call(
                qkv_terms,
                [shape((own_rows + 8, 3 * inner), bf16)] * 4,
                6 * seq_len * width * inner,
                normed_turned,
                small,
                grad_router,
                normed_near,
                normed_peer,
                d_qkv_turned[0],
                *d_qkv_hops,
                scalars=(device_at,),
                scratch=(pltpu.VMEM((width, quarter[1]), bf16),),
            )
            line = line_hops(terms[1:])
            rows, d_pre, _ = lax.optimization_barrier((rows, d_pre, terms[0]))
            grad_up = grads_of_expert(rows, d_pre)
            *out_pieces, _ = lax.optimization_barrier((*out_pieces, grad_up))
            *line, grad_up = lax.optimization_barrier((*line, grad_up))
            split = vmem_call(
                join_line,
                [shape((own_rows, 512), bf16)] * 4,
                0,
                terms[0],
                *line,
                scalars=(device_at,),
            )
            last = plane_hops(split[1:])
            grad_qkv, gain_one, gain_two, grad_rel, grad_router = vmem_call(
                join_plane,
                (
                    shape((3, own_rows, inner), f32),
                    shape((width,), f32),
                    shape((width,), f32),
                    shape((heads_here, BUCKETS), f32),
                    shape((experts, own_rows), f32),
                ),
                0,
                split[0],
                *last,
                scalars=(device_at,),
                scratch=(pltpu.VMEM((own_rows, 3 * inner), f32),),
            )
            out_hops = plane_hops(out_pieces[1:])
            out_blocks = vmem_call(
                join_blocks,
                [shape((own_rows, inner), bf16)] * 4,
                0,
                out_pieces[0],
                *out_hops,
            )
            *out_blocks, _ = lax.optimization_barrier((*out_blocks, last[0]))
            out_blocks = (out_blocks[0], *line_hops(out_blocks[1:]))
            grad_out = sum(part.astype(f32) for part in out_blocks)
        else:
            layer_out = land_at_home(home)
            grad_down, grad_up = grads_of_expert(act_b, d_y), grads_of_expert(rows, d_pre)
            grad_qkv = scatter_groups(dot(normed_turned, d_qkv_turned[0], 1, 1), own_rows)
            grad_qkv = grad_qkv.reshape(own_rows, 3, inner).transpose(1, 0, 2)
            grad_out = scatter_groups(out_pieces[0], own_rows)
            small = sum_groups(jnp.concatenate([small, grad_router]))
            gain_one, gain_two = small[heads_here], small[heads_here + 1]
            grad_rel = small[:heads_here, :BUCKETS]
            own_at = (device_at[0] * n_row + device_at[1]) * own_rows
            grad_router = lax.dynamic_slice(small, (heads_here + 2, own_at), (experts, own_rows))
        return (
            layer_out,
            grad_x,
            gain_one,
            grad_qkv,
            grad_rel.T,
            grad_out.T,
            gain_two,
            grad_router.T,
            grad_up[None],
            grad_down[None],
        )

    return per_device


def solution(mesh):
    return jax.shard_map(
        make_per_device(mesh),
        mesh=mesh,
        in_specs=(
            P(("ex", "row"), None),
            P(),
            P(None, ("ex", "row"), "col"),
            P(None, "col"),
            P("col", ("ex", "row")),
            P(),
            P(("ex", "row"), None),
            P(("ex", "row"), None, "col"),
            P(("ex", "row"), "col", None),
            P(("ex", "row"), None),
            P(("ex", "row")),
            P(("ex", "row")),
            P(("ex", "row")),
            P(("ex", "row"), "col"),
        ),
        out_specs=(
            P(("ex", "row"), "col"),
            P(("ex", "row"), None),
            P(),
            P(None, ("ex", "row"), "col"),
            P(None, "col"),
            P("col", ("ex", "row")),
            P(),
            P(("ex", "row"), None),
            P(("ex", "row"), None, "col"),
            P(("ex", "row"), "col", None),
        ),
        check_vma=False,
    )
```

```python
import functools
import math

import jax
import jax.numpy as jnp
from jax import lax
from jax.experimental import pallas as pl
from jax.experimental.pallas import tpu as pltpu
from jax.sharding import PartitionSpec as P

HEAD = 64
BUCKETS = 32

norm_eps = 1e-06
bucket_edges = (12, 16, 23, 32, 46, 64, 91)
highest = lax.Precision.HIGHEST
bf16 = jnp.bfloat16
f32 = jnp.float32

GATHER_ORDER = tuple(((k, m),) for m in range(4) for k in range(4))

def bucket_of(offset):
    distance = jnp.abs(offset)
    far_part = jnp.zeros(distance.shape, jnp.int32)
    for edge_at in bucket_edges:
        far_part = far_part + (distance >= edge_at).astype(jnp.int32)
    inside = jnp.where(distance < 8, distance, far_part + jnp.int32(8))
    upper = jnp.where(offset > 0, jnp.int32(BUCKETS // 2), jnp.int32(0))
    return inside + upper


def rms_scale(values):
    return lax.rsqrt(jnp.mean(values * values, axis=-1, keepdims=True) + norm_eps)


def dot(a, b, ca, cb):
    return lax.dot_general(a, b, (((ca,), (cb,)), ((), ())), preferred_element_type=f32)


def swap_cores(values):
    return lax.ppermute(values, "col", [(0, 1), (1, 0)])


def shape(dims, dtype):
    return jax.ShapeDtypeStruct(tuple(dims), dtype)


def vmem_call(kernel, out_shape, flops, *args, scalars=(), scratch=(), limit=12):
    nbytes = sum(math.prod(v.shape) * v.dtype.itemsize for v in (*args, *out_shape))
    spec = pl.BlockSpec(memory_space=pltpu.VMEM)
    limit = limit if nbytes < 16 * 2**20 else 48
    return pl.pallas_call(
        kernel,
        out_shape=out_shape,
        in_specs=[pl.BlockSpec(memory_space=pltpu.SMEM)] * len(scalars) + [spec] * len(args),
        out_specs=[spec] * len(out_shape),
        scratch_shapes=scratch,
        compiler_params=pltpu.CompilerParams(vmem_limit_bytes=limit * 2**20),
        cost_estimate=pl.CostEstimate(flops=flops, bytes_accessed=nbytes, transcendentals=0),
    )(*scalars, *args)


def block_rows(at_ref, order, count):
    if order is None:
        return [pl.ds(0, count)]
    ex_at, row_at = at_ref[0], at_ref[1]
    return [
        pl.ds(pl.multiple_of(((ex_at ^ k) * 4 + (row_at ^ m)) * count, 16), count)
        for part in order
        for k, m in part
    ]


def eye(size):
    dims = (size, size)
    same = lax.broadcasted_iota(jnp.int32, dims, 0) == lax.broadcasted_iota(jnp.int32, dims, 1)
    return same.astype(bf16)


def pack_weights(qkv_in, out_in, router_in, packed_out, qkv_ref, out_turned_ref, router_turned_ref, packed_ref, sems):
    pairs = ((qkv_in, qkv_ref), (out_in, out_turned_ref), (router_in, router_turned_ref))
    copies = [pltpu.make_async_copy(source, target, sems.at[i]) for i, (source, target) in enumerate(pairs)]
    for copy in copies:
        copy.start()
    inner, experts = qkv_ref.shape[2], router_turned_ref.shape[0]
    packed_ref[:, 4 * inner :] = jnp.zeros((packed_ref.shape[0], packed_ref.shape[1] - 4 * inner), bf16)
    for copy in copies:
        copy.wait()
    for part in range(3):
        packed_ref[:, part * inner : (part + 1) * inner] = qkv_ref[part].astype(bf16)
    packed_ref[:, 3 * inner : 4 * inner] = out_turned_ref[...].astype(bf16)
    router = dot(router_turned_ref[...].astype(bf16), eye(experts), 0, 0)
    packed_ref[:, 4 * inner : 4 * inner + experts] = router.astype(bf16)
    copy = pltpu.make_async_copy(packed_ref, packed_out, sems.at[3])
    copy.start()
    copy.wait()


def spread_bias(offset_ref, seg_ref, bias_ref):
    heads, seq_len, _ = bias_ref.shape
    span = offset_ref.shape[1]
    documents = lax.broadcasted_iota(jnp.int32, (8, seq_len), 0) == seg_ref[...]
    same_doc = dot(documents.astype(bf16), documents.astype(bf16), 0, 0) > 0.5
    for at in range(heads):
        spread = jnp.broadcast_to(offset_ref[at : at + 1, :], (seq_len, span))
        bias = pltpu.roll(spread, span - seq_len + 1, 1, stride=1, stride_axis=0)[:, :seq_len]
        bias_ref[at] = jnp.where(same_doc, bias, -1e30)


def first_norm(at_ref, x_ref, gain_ref, h_ref, turned_ref, half_ref):
    x_float = x_ref[...].astype(f32)
    h_one = (x_float * rms_scale(x_float) * gain_ref[...].reshape(1, -1)).astype(bf16)
    h_ref[...] = h_one
    turned_ref[...] = dot(h_one, eye(h_one.shape[0]), 0, 0).astype(bf16)
    half = half_ref.shape[0]
    half_ref[...] = jnp.where(at_ref[2] == 0, turned_ref[:half, :], turned_ref[half:, :])


def attend_forward(order, at_ref, h_ref, bias_ref, *refs):
    *block_refs, part_ref, qkv_ref, probs_ref, ctx_ref, w_ref, out_w_ref, router_ref = refs
    heads, inner = probs_ref.shape[0], ctx_ref.shape[1]
    for rows, block_ref in zip(block_rows(at_ref, order, block_refs[0].shape[0]), block_refs):
        w_ref[rows, :] = block_ref[:, : 3 * inner]
        out_w_ref[rows, :] = block_ref[:, 3 * inner : 4 * inner]
        router_ref[rows, :] = block_ref[:, 4 * inner :]
    qkv_ref[...] = dot(h_ref[...], w_ref[...], 1, 0).astype(bf16)
    for at in range(heads):
        take = lambda part: qkv_ref[:, part * inner + at * HEAD : part * inner + (at + 1) * HEAD]
        scores = dot(take(0), take(1), 1, 1) * 0.125 + bias_ref[at]
        expo = jnp.exp(scores - jnp.max(scores, axis=1, keepdims=True))
        probs = expo * (1.0 / jnp.sum(expo, axis=1, keepdims=True))
        probs_ref[at] = probs
        ctx = dot(probs.astype(bf16), take(2), 1, 0)
        ctx_ref[:, at * HEAD : (at + 1) * HEAD] = ctx.astype(bf16)
    part_ref[...] = dot(ctx_ref[...], out_w_ref[...], 1, 1).astype(bf16)


def spare_rows(experts, chunk):
    dims = (experts * 24, experts * 4)
    row, column = lax.broadcasted_iota(jnp.int32, dims, 0), lax.broadcasted_iota(jnp.int32, dims, 1)
    expert = lax.shift_right_logical(row * 2731, 16)
    inside = row - expert * 24
    wanted = expert * 4 + (inside - chunk * 4)
    return ((column == wanted) & (inside >= chunk * 4) & (inside < chunk * 4 + 4)).astype(bf16)


def pack_slots(values, packed_ref, low=0, before=None):
    if len(packed_ref.shape) == 2:
        packed_ref[:, low * 128 : low * 128 + values.shape[1]] = values.astype(bf16)
        return
    experts, chunks = packed_ref.shape[0], values.shape[1] // 128
    first = (packed_ref.shape[1] - 24) // 16 * 16
    values = values.astype(bf16)
    spare = 0.0
    for c in range(chunks):
        chunk = values[:, c * 128 : (c + 1) * 128]
        for e in range(experts):
            packed_ref[e, (low + c) * 16 : (low + c + 1) * 16, :] = chunk[e * 16 : (e + 1) * 16]
        spare = spare + dot(spare_rows(experts, low + c), chunk[experts * 16 :], 1, 0)
    for e in range(experts):
        rows = spare[e * 24 : (e + 1) * 24]
        if before is not None:
            rows = rows + before[e, first:, :].astype(f32)
        packed_ref[e, first:, :] = rows.astype(bf16)


def unpack_slots(packed_ref, low, target_ref, spare_ref):
    experts, chunks = packed_ref.shape[0], target_ref.shape[1] // 128
    first = (packed_ref.shape[1] - 24) // 16 * 16
    for e in range(experts):
        spare_ref[e * 24 : (e + 1) * 24, :] = packed_ref[e, first:, :].astype(f32)
    spare = spare_ref[...].astype(bf16)
    for c in range(chunks):
        lanes = slice(c * 128, (c + 1) * 128)
        for e in range(experts):
            rows = slice((low + c) * 16, (low + c + 1) * 16)
            target_ref[e * 16 : (e + 1) * 16, lanes] = packed_ref[e, rows, :]
        target_ref[experts * 16 :, lanes] = dot(spare_rows(experts, low + c), spare, 0, 0).astype(bf16)


def slot_places(slot_ref, packed_ref):
    slots = packed_ref.shape[0] * (1 if len(packed_ref.shape) == 2 else 20)
    dims = (slots, slot_ref.shape[1])
    return (lax.broadcasted_iota(jnp.int32, dims, 0) == slot_ref[...]).astype(bf16)


def pack_cotangent(g_ref, slot_ref, packed_ref):
    packed_ref[...] = jnp.zeros(packed_ref.shape, bf16)
    pack_slots(dot(slot_places(slot_ref, packed_ref), g_ref[...], 1, 0), packed_ref, g_ref.shape[1] // 128)


def dispatch(at_ref, x_ref, part_ref, peer_ref, gain_ref, slot_ref, before_ref, send_ref):
    half = x_ref.shape[1] // 2
    x_one = x_ref[...].astype(f32) + (part_ref[...].astype(f32) + peer_ref[...].astype(f32))
    h_two = (x_one * rms_scale(x_one) * gain_ref[...].reshape(1, -1)).astype(bf16)
    mine = jnp.where(at_ref[2] == 0, h_two[:, :half], h_two[:, half:])
    if len(send_ref.shape) == 2:
        send_ref[:, half:] = before_ref[:, half:]
    else:
        low, high = half // 128 * 16, half // 64 * 16
        send_ref[:, low:high, :] = before_ref[:, low:high, :]
    pack_slots(dot(slot_places(slot_ref, send_ref), mine, 1, 0), send_ref, 0, before_ref)


def run_expert(
    experts, row_size, at_ref, got_ref, peer_ref, router_ref, up_ref, down_ref,
    cross_ref, mine_ref, probs_ref, gate_part_ref, rows_ref, d_y_ref, act_ref, d_pre_ref, d_in_ref,
    got_rows_ref, peer_rows_ref, spare_ref,
):
    half = rows_ref.shape[1] // 2
    if len(got_ref.shape) == 3:
        unpack_slots(got_ref, 0, got_rows_ref, spare_ref)
        unpack_slots(peer_ref, 0, peer_rows_ref, spare_ref)
        got_ref, peer_ref = got_rows_ref, peer_rows_ref
    hidden = up_ref.shape[1]
    first_core = at_ref[2] == 0
    for at, refs in ((0, (got_ref, peer_ref)), (1, (peer_ref, got_ref))):
        pick = lambda lo: jnp.where(first_core, refs[0][:, lo : lo + half], refs[1][:, lo : lo + half])
        rows_ref[:, at * half : (at + 1) * half] = pick(0)
        d_y_ref[:, at * half : (at + 1) * half] = pick(half)
    rows, g_rows = rows_ref[...], d_y_ref[...].astype(f32)
    logits = dot(rows, router_ref[...], 1, 0)[:, :experts]
    expo = jnp.exp(logits - jnp.max(logits, axis=1, keepdims=True))
    probs = expo / jnp.sum(expo, axis=1, keepdims=True)
    probs_ref[...] = probs
    expert_at = at_ref[0] * row_size + at_ref[1]
    chosen = lax.broadcasted_iota(jnp.int32, probs.shape, 1) == expert_at
    gate = jnp.sum(jnp.where(chosen, probs, 0.0), axis=1, keepdims=True)
    d_y_ref[...] = (g_rows * gate).astype(bf16)
    step = 768 if hidden % 768 == 0 else hidden
    y_part = None
    for lo in range(0, hidden, step):
        cols = pl.ds(lo, step)
        pre_act = dot(rows_ref[...], up_ref[:, cols], 1, 0)
        cdf = 0.5 * (1.0 + lax.erf(pre_act * (1.0 / math.sqrt(2.0))))
        pdf = jnp.exp(-0.5 * pre_act * pre_act) * (1.0 / math.sqrt(2.0 * math.pi))
        act = (pre_act * cdf).astype(bf16)
        act_ref[:, cols] = act
        y_more = dot(act, down_ref[cols, :], 1, 0)
        d_pre = (dot(d_y_ref[...], down_ref[cols, :], 1, 1) * (cdf + pre_act * pdf)).astype(bf16)
        d_pre_ref[:, cols] = d_pre
        d_more = dot(d_pre, up_ref[:, cols], 1, 1)
        if lo == 0:
            y_part = y_more
            d_in_ref[...] = d_more
        else:
            y_part = y_part + y_more
            d_in_ref[...] += d_more
    gate_part = jnp.sum(g_rows * y_part, axis=1, keepdims=True)
    high = gate_part.astype(bf16)
    low = (gate_part - high.astype(f32)).astype(bf16)
    gate_part_ref[...] = high.astype(f32) + low.astype(f32)
    lane = lax.broadcasted_iota(jnp.int32, (rows.shape[0], 128), 1)
    beside = jnp.where(lane == 0, high.astype(f32), jnp.where(lane == 1, low.astype(f32), 0.0))
    cross_ref[:, 2 * half :] = beside.astype(bf16)
    d_in = d_in_ref[...]
    mine_ref[:, :half] = jnp.where(first_core, y_part[:, :half], y_part[:, half:])
    mine_ref[:, half:] = jnp.where(first_core, d_in[:, :half], d_in[:, half:])
    cross_ref[:, :half] = jnp.where(first_core, y_part[:, half:], y_part[:, :half]).astype(bf16)
    cross_ref[:, half : 2 * half] = jnp.where(first_core, d_in[:, half:], d_in[:, :half]).astype(bf16)


def settle(
    row_size, at_ref, mine_ref, crossed_ref, probs_ref, gate_part_ref, router_ref, rows_ref,
    back_ref, grad_router_ref,
):
    half = mine_ref.shape[1] // 2
    probs = probs_ref[...]
    expert_at = at_ref[0] * row_size + at_ref[1]
    chosen = (lax.broadcasted_iota(jnp.int32, probs.shape, 1) == expert_at).astype(f32)
    gate = jnp.sum(probs * chosen, axis=1, keepdims=True)
    beside = crossed_ref[:, 2 * half :].astype(f32)
    d_gate = gate_part_ref[...] + (beside[:, 0:1] + beside[:, 1:2])
    d_logits = (d_gate * gate * (chosen - probs)).astype(bf16)
    router_w = router_ref[...][:, : probs.shape[1]]
    router_mine = jnp.where(at_ref[2] == 0, router_w[:half], router_w[half:])
    y_gated = gate * (mine_ref[:, :half] + crossed_ref[:, :half].astype(f32))
    d_in = mine_ref[:, half:] + crossed_ref[:, half : 2 * half].astype(f32) + dot(d_logits, router_mine, 1, 1)
    pack_slots(jnp.concatenate([y_gated, d_in], axis=1), back_ref)
    grad_router_ref[...] = dot(d_logits, rows_ref[...], 0, 0)


def from_slots(home_ref, slot_ref, low, rows_ref, spare_ref):
    if len(home_ref.shape) == 3:
        unpack_slots(home_ref, low, rows_ref, spare_ref)
    else:
        rows_ref[...] = home_ref[:, low * 128 : low * 128 + rows_ref.shape[1]]
    dims = (rows_ref.shape[0], slot_ref.shape[1])
    place = (lax.broadcasted_iota(jnp.int32, dims, 0) == slot_ref[...]).astype(bf16)
    return dot(place, rows_ref[...], 0, 0)


def arrive(home_ref, slot_ref, d_h_ref, rows_ref, spare_ref):
    low = d_h_ref.shape[1] // 128
    d_h_ref[...] = from_slots(home_ref, slot_ref, low, rows_ref, spare_ref).astype(bf16)


def land(at_ref, home_ref, slot_ref, x_ref, part_ref, peer_ref, layer_ref, rows_ref, spare_ref):
    half = layer_ref.shape[1]
    y_home = from_slots(home_ref, slot_ref, 0, rows_ref, spare_ref)
    mine = lambda ref: jnp.where(at_ref[2] == 0, ref[:, :half], ref[:, half:]).astype(f32)
    layer_ref[...] = (mine(x_ref) + (mine(part_ref) + mine(peer_ref)) + y_home).astype(bf16)


def come_home(
    cube, at_ref, mine_ref, peer_ref, x_ref, part_ref, part_peer_ref, g_ref, g_peer_ref,
    gain_ref, out_w_ref, ctx_ref, d_x_ref, gain_grad_ref, d_ctx_ref, *refs,
):
    *piece_refs, grads_ref = refs
    first_core = at_ref[2] == 0
    both = lambda a, b: jnp.concatenate(
        [jnp.where(first_core, a, b), jnp.where(first_core, b, a)], axis=1
    )
    d_h = both(mine_ref[...], peer_ref[...]).astype(f32)
    x_one = x_ref[...].astype(f32) + (part_ref[...].astype(f32) + part_peer_ref[...].astype(f32))
    g_full = both(g_ref[...], g_peer_ref[...]).astype(f32)
    scale = rms_scale(x_one)
    normed = x_one * scale
    gain_grad_ref[...] = jnp.sum(d_h * normed, axis=0, keepdims=True)
    d_norm = d_h * gain_ref[...].reshape(1, -1)
    d_x = g_full + scale * (d_norm - normed * jnp.mean(d_norm * normed, axis=-1, keepdims=True))
    d_x_ref[...] = d_x
    d_x_b = d_x.astype(bf16)
    d_ctx_ref[...] = dot(d_x_b, out_w_ref[...], 1, 0).astype(bf16)
    grads_ref[...] = dot(d_x_b, ctx_ref[...], 0, 0).astype(bf16)
    rows = grads_ref.shape[0] // 16
    for m, piece_ref in enumerate(piece_refs):
        if not cube:
            piece_ref[...] = grads_ref[...]
            continue
        for k in range(4):
            start = pl.multiple_of(((at_ref[0] ^ k) * 4 + (at_ref[1] ^ m)) * rows, 16)
            piece_ref[k * rows : (k + 1) * rows, :] = grads_ref[pl.ds(start, rows), :]


def attend_backward(cube, at_ref, d_ctx_ref, qkv_ref, probs_ref, w_ref, d_h_ref, grad_offset_ref, *refs):
    *piece_refs, turned_ref = refs
    heads, seq_len, _ = probs_ref.shape
    inner = d_ctx_ref.shape[1]
    span = grad_offset_ref.shape[1]
    flip = (
        lax.broadcasted_iota(jnp.int32, (seq_len, seq_len), 0)
        + lax.broadcasted_iota(jnp.int32, (seq_len, seq_len), 1)
        == seq_len - 1
    ).astype(bf16)
    grad_offset_ref[...] = jnp.zeros(grad_offset_ref.shape, f32)
    for at in range(heads):
        cols = lambda part: pl.ds(part * inner + at * HEAD, HEAD)
        d_ctx = d_ctx_ref[:, at * HEAD : (at + 1) * HEAD]
        probs = probs_ref[at]
        d_probs = dot(d_ctx, qkv_ref[:, cols(2)], 1, 1)
        row_delta = jnp.sum(probs * d_probs, axis=1, keepdims=True)
        d_scores = (probs * (d_probs - row_delta)).astype(bf16)
        turned_ref[cols(0), :] = (dot(qkv_ref[:, cols(1)], d_scores, 0, 1) * 0.125).astype(bf16)
        turned_ref[cols(1), :] = (dot(qkv_ref[:, cols(0)], d_scores, 0, 0) * 0.125).astype(bf16)
        turned_ref[cols(2), :] = dot(d_ctx, probs.astype(bf16), 0, 0).astype(bf16)
        flipped = jnp.concatenate(
            [dot(flip, d_scores, 1, 0), jnp.zeros((seq_len, span - seq_len), f32)], axis=1
        )
        lined = pltpu.roll(flipped, 0, 1, stride=1, stride_axis=0)
        grad_offset_ref[at : at + 1, :] = jnp.sum(lined, axis=0, keepdims=True)
    size = piece_refs[0].shape[0]
    for m, piece_ref in enumerate(piece_refs):
        start = pl.multiple_of((at_ref[1] ^ m) * size, 16) if cube else 0
        piece_ref[...] = turned_ref[pl.ds(start, size), :]
    d_h_ref[...] = dot(turned_ref[...], w_ref[...], 0, 1).astype(bf16)


def qkv_terms(at_ref, turned_ref, small_ref, router_ref, *refs):
    mine_ref, peer_ref, piece_refs, block_refs, grads_ref = refs[0], refs[1], refs[2:6], refs[6:10], refs[10]
    half = mine_ref.shape[0] // 3
    from_mine = from_peer = 0.0
    for m in range(1, 4):
        rows = slice((m - 1) * half, m * half)
        from_mine = from_mine + dot(mine_ref[rows, :], piece_refs[m][...], 1, 1)
        from_peer = from_peer + dot(peer_ref[rows, :], piece_refs[m][...], 1, 1)
    own = dot(turned_ref[...], piece_refs[0][...], 1, 1)
    first_core = at_ref[2] == 0
    grads_ref[:half, :] = (own[:half] + jnp.where(first_core, from_mine, from_peer)).astype(bf16)
    grads_ref[half:, :] = (own[half:] + jnp.where(first_core, from_peer, from_mine)).astype(bf16)
    rows, size = block_refs[0].shape[0] - 8, grads_ref.shape[1]
    width = small_ref.shape[1]
    part = width // 4
    for k, block_ref in enumerate(block_refs):
        block_ref[rows:, :width] = small_ref[...].astype(bf16)
        router = jnp.zeros((router_ref.shape[0], part), f32)
        for z in range(4):
            router = jnp.where((at_ref[0] ^ k) == z, router_ref[:, z * part : (z + 1) * part], router)
        for i in range(2):
            low = width + i * part
            block_ref[rows:, low : low + part] = router[i * 8 : (i + 1) * 8].astype(bf16)
        for m in range(4):
            start = ((at_ref[0] ^ k) * 4 + (at_ref[1] ^ m)) * rows
            block_ref[:rows, m * size : (m + 1) * size] = grads_ref[pl.ds(pl.multiple_of(start, 16), rows), :]


def pair_sum(refs):
    a, b, c, d = (ref[...].astype(f32) for ref in refs)
    return (a + b) + (c + d)


def join_line(at_ref, *refs):
    total = pair_sum(refs[:4])
    rows = refs[4].shape[0]
    size = total.shape[1] // 4
    width = size * 8 // 3
    part = width // 16
    extra = total[rows:]
    for m, piece_ref in enumerate(refs[4:]):
        piece_ref[...] = jnp.zeros(piece_ref.shape, bf16)
        piece_ref[:, :size] = total[:rows, m * size : (m + 1) * size].astype(bf16)
        for i in range(2):
            for j in range(width // 128):
                line = extra[6 + i : 7 + i, j * 128 : (j + 1) * 128]
                piece_ref[i * 8 + j : i * 8 + j + 1, 384:] = line.astype(bf16)
            router = jnp.zeros((8, part), f32)
            for row in range(4):
                low = width + i * 4 * part + row * part
                router = jnp.where((at_ref[1] ^ m) == row, extra[:, low : low + part], router)
            piece_ref[32 + i * 8 : 40 + i * 8, 384 : 384 + part] = router.astype(bf16)
        piece_ref[16:24, 384:] = extra[:, :128].astype(bf16)


def join_plane(at_ref, *refs):
    piece_refs, (out_ref, gain_one_ref, gain_two_ref, rel_ref, router_ref, line_ref) = refs[:4], refs[4:]
    size = line_ref.shape[1] // 4
    for quarter in range(4):
        piece = 0.0
        for m, piece_ref in enumerate(piece_refs):
            piece = jnp.where((at_ref[1] ^ m) == quarter, piece_ref[:, :size].astype(f32), piece)
        line_ref[:, quarter * size : (quarter + 1) * size] = piece
    inner = out_ref.shape[2]
    for part in range(3):
        out_ref[part] = line_ref[:, part * inner : (part + 1) * inner]
    extra = pair_sum([ref.at[:, 384:] for ref in piece_refs])
    for i, gain_ref in enumerate((gain_one_ref, gain_two_ref)):
        for j in range(gain_ref.shape[0] // 128):
            gain_ref[pl.ds(j * 128, 128)] = extra[i * 8 + j]
    rel_ref[...] = extra[16 : 16 + rel_ref.shape[0], : rel_ref.shape[1]]
    router_ref[...] = extra[32 : 32 + router_ref.shape[0], : router_ref.shape[1]]


def join_blocks(*refs):
    total = pair_sum(refs[:4])
    rows = total.shape[0] // 4
    for k, block_ref in enumerate(refs[4:]):
        block_ref[...] = total[k * rows : (k + 1) * rows].astype(bf16)


def finish(
    d_h_ref, peer_ref, x_ref, d_x_ref, gain_ref, gain_grad_ref, grad_offset_ref, hot_ref, grad_x_ref, small_ref,
):
    d_h = d_h_ref[...].astype(f32) + peer_ref[...].astype(f32)
    x_float = x_ref[...].astype(f32)
    scale = rms_scale(x_float)
    normed = x_float * scale
    d_norm = d_h * gain_ref[...].reshape(1, -1)
    grad_x = d_x_ref[...] + scale * (
        d_norm - normed * jnp.mean(d_norm * normed, axis=-1, keepdims=True)
    )
    grad_x_ref[...] = grad_x.astype(bf16)
    heads, buckets = grad_offset_ref.shape[0] - 2, hot_ref.shape[1]
    small_ref[...] = jnp.zeros(small_ref.shape, f32)
    grad_rel = lax.dot_general(
        grad_offset_ref[...], hot_ref[...], (((1,), (0,)), ((), ())), precision=highest, preferred_element_type=f32
    )
    small_ref[:, :buckets] = grad_rel
    small_ref[heads : heads + 1, :] = jnp.sum(d_h * normed, axis=0, keepdims=True)
    small_ref[heads + 1 : heads + 2, :] = gain_grad_ref[...]


def expert_grads(left_ref, right_ref, out_ref, held_ref, sems):
    count = held_ref.shape[1]
    copies = []
    for at in range(out_ref.shape[0] // count):
        rows = pl.ds(at * count, count)
        held_ref[at] = dot(left_ref[:, rows], right_ref[...], 0, 0)
        copies.append(pltpu.make_async_copy(held_ref.at[at], out_ref.at[rows, :], sems.at[at]))
        copies[-1].start()
    for copy in copies:
        copy.wait()


def experts_pad(experts):
    return -(-experts // 128) * 128


def make_per_device(mesh):
    n_ex, n_row = mesh.shape["ex"], mesh.shape["row"]
    groups = n_ex * n_row

    def hop(values, axis, step):
        return lax.ppermute(values, axis, [(i, i ^ step) for i in range(mesh.shape[axis])])

    def whole_cube(rows):
        return n_ex == 4 and n_row == 4 and rows == 48

    def gather_blocks(shard, meanwhile):
        rows, width = shard.shape
        if whole_cube(rows):
            near, far, farther = (hop(shard, "ex", k) for k in (1, 2, 3))
            x_own, y_own = hop(shard, "row", 1), hop(shard, "row", 2)
            near, x_own, y_own = lax.optimization_barrier((near, x_own, y_own))
            xs, ys = [x_own, hop(near, "row", 1)], [y_own, hop(near, "row", 2)]
            diagonal = [hop(x_own, "row", 2)]
            beside = meanwhile(near)
            far, farther, diagonal[0], *beside = lax.optimization_barrier((far, farther, diagonal[0], *beside))
            for part in (far, farther):
                xs.append(hop(part, "row", 1))
                ys.append(hop(part, "row", 2))
            diagonal += [hop(ys[1], "row", 1), hop(xs[2], "row", 2), hop(ys[3], "row", 1)]
            return [shard, near, far, farther, *xs, *ys, *diagonal], beside
        part = lax.all_gather(shard, "ex", axis=0)
        part = jnp.broadcast_to(part[None], (n_row, n_ex, rows, width))
        part = lax.all_to_all(part, "row", split_axis=0, concat_axis=0, tiled=True)
        return [part.transpose(1, 0, 2, 3).reshape(groups * rows, width)], meanwhile(shard)

    def scatter_groups(grads, rows):
        part = grads.astype(bf16).reshape(n_ex, n_row, rows, -1).transpose(1, 0, 2, 3)
        part = lax.all_to_all(part, "row", split_axis=0, concat_axis=0, tiled=True)
        part = jnp.sum(part.astype(f32), axis=0).astype(bf16)
        part = lax.all_to_all(part, "ex", split_axis=0, concat_axis=0, tiled=True)
        return jnp.sum(part.astype(f32), axis=0)

    def plane_hops(parts):
        return [hop(part, "row", m + 1) for m, part in enumerate(parts)]

    def line_hops(parts):
        return [hop(part, "ex", k + 1) for k, part in enumerate(parts)]

    def sum_groups(values):
        for axis in ("row", "ex"):
            step = 1
            while step < mesh.shape[axis]:
                values = values + hop(values, axis, step)
                step *= 2
        return values

    def per_device(
        x_in,
        gain_attn,
        w_qkv,
        rel_bias,
        w_out,
        gain_ffn,
        w_router,
        w_up,
        w_down,
        seg_ids,
        expert_ids,
        slot_ids,
        drop_flags,
        d_out,
    ):
        seq_len, width = x_in.shape
        heads_here = rel_bias.shape[1]
        inner = w_qkv.shape[2]
        own_rows = w_qkv.shape[1]
        experts = w_router.shape[1]
        wide = inner + experts_pad(experts)
        half = d_out.shape[1]
        hidden = w_up.shape[2]
        device_at = jnp.stack([lax.axis_index(axis).astype(jnp.int32) for axis in ("ex", "row", "col")])
        device_at, w_qkv = lax.optimization_barrier((device_at, w_qkv))
        cube = whole_cube(own_rows)
        capacity = 5 * seq_len // (4 * experts)
        tight = cube and experts == 16 and capacity == 20 and width == 768
        slots = capacity if tight else -(-capacity // 8) * 8
        slot_total = experts * slots
        packed_slots = (experts, slots * width // 128, 128) if tight else (slot_total, width)
        exchange = packed_slots if tight else (experts, slots, width)
        slot_scratch = (
            pltpu.VMEM((slot_total, width), bf16),
            pltpu.VMEM((slot_total, width), bf16),
            pltpu.VMEM((experts * 24, 128), f32),
        )
        gather_order = GATHER_ORDER if cube else None

        turned = (w_qkv, w_out.T, w_router.T)
        packed_shape = shape((own_rows, 3 * inner + wide), bf16)
        packed = pl.pallas_call(
            pack_weights,
            out_shape=packed_shape,
            in_specs=[pl.BlockSpec(memory_space=pltpu.HBM)] * 3,
            out_specs=pl.BlockSpec(memory_space=pltpu.HBM),
            scratch_shapes=[
                *(pltpu.VMEM(v.shape, v.dtype) for v in turned),
                pltpu.VMEM(packed_shape.shape, bf16),
                pltpu.SemaphoreType.DMA((4,)),
            ],
            compiler_params=pltpu.CompilerParams(vmem_limit_bytes=60 * 2**20),
        )(*turned)

        span = 2 * seq_len
        offsets = jnp.arange(span, dtype=jnp.int32) - (seq_len - 1)
        offset_hot = (
            bucket_of(offsets)[:, None] == jnp.arange(BUCKETS, dtype=jnp.int32)[None, :]
        ).astype(f32)
        per_offset = jnp.einsum("bh,ob->ho", rel_bias, offset_hot, precision=highest)

        slot_of = expert_ids * slots + slot_ids
        if tight:
            spare_of = experts * 16 + expert_ids * 4 + slot_ids - 16
            slot_of = jnp.where(slot_ids < 16, expert_ids * 16 + slot_ids, spare_of)
        slot_of = jnp.where(drop_flags == 1, slot_total, slot_of)[None]

        def prepare(after):
            late_up, late_down, _ = lax.optimization_barrier((w_up[0], w_down[0], after))
            late_offset, late_x, _ = lax.optimization_barrier((per_offset, x_in, after))
            (bias,) = vmem_call(
                spread_bias, (shape((heads_here, seq_len, seq_len), f32),), 0, late_offset, seg_ids
            )
            normed = vmem_call(
                first_norm,
                (shape((seq_len, width), bf16), shape((width, seq_len), bf16), shape((half, seq_len), bf16)),
                0,
                late_x,
                gain_attn,
                scalars=(device_at,),
            )
            return [late_up.astype(bf16), late_down.astype(bf16), bias, *normed]

        blocks, beside = gather_blocks(packed, prepare)
        up_w, down_w, bias, h_one, normed_turned, normed_mine = beside
        g_peer = swap_cores(d_out)

        square = seq_len * seq_len * heads_here * HEAD
        attn_part, qkv, probs, context, qkv_w, out_w, router_w = vmem_call(
            functools.partial(attend_forward, gather_order),
            (
                shape((seq_len, width), bf16),
                shape((seq_len, 3 * inner), bf16),
                shape((heads_here, seq_len, seq_len), f32),
                shape((seq_len, inner), bf16),
                shape((width, 3 * inner), bf16),
                shape((width, inner), bf16),
                shape((width, wide - inner), bf16),
            ),
            8 * seq_len * width * inner + 4 * square,
            h_one,
            bias,
            *blocks,
            scalars=(device_at,),
        )
        attn_peer = swap_cores(attn_part)
        late_g, _ = lax.optimization_barrier((d_out, attn_part))
        (g_packed,) = vmem_call(pack_cotangent, (shape(packed_slots, bf16),), 0, late_g, slot_of)
        (send,) = vmem_call(
            dispatch,
            (shape(packed_slots, bf16),),
            2 * seq_len * slot_total * width,
            x_in,
            attn_part,
            attn_peer,
            gain_ffn,
            slot_of,
            g_packed,
            scalars=(device_at,),
        )
        got = lax.all_to_all(send.reshape(exchange), ("ex", "row"), 0, 0, tiled=True).reshape(packed_slots)
        if cube:
            later_normed, got = lax.optimization_barrier((normed_mine, got))
            normed_hops = plane_hops([later_normed] * 2)
        crossing, mine, router_probs, gate_part, rows, d_y, act_b, d_pre = vmem_call(
            functools.partial(run_expert, experts, n_row),
            (
                shape((slot_total, width + 128), bf16),
                shape((slot_total, width), f32),
                shape((slot_total, experts), f32),
                shape((slot_total, 1), f32),
                shape((slot_total, width), bf16),
                shape((slot_total, width), bf16),
                shape((slot_total, hidden), bf16),
                shape((slot_total, hidden), bf16),
            ),
            8 * slot_total * width * hidden,
            got,
            swap_cores(got),
            router_w,
            up_w,
            down_w,
            scalars=(device_at,),
            scratch=(pltpu.VMEM((slot_total, width), f32), *slot_scratch),
        )
        if cube:
            crossing, g_peer, *normed_hops = lax.optimization_barrier((crossing, g_peer, *normed_hops))
        back, grad_router = vmem_call(
            functools.partial(settle, n_row),
            (shape(packed_slots, bf16), shape((experts, width), f32)),
            2 * slot_total * half * experts,
            mine,
            swap_cores(crossing),
            router_probs,
            gate_part,
            router_w,
            rows,
            scalars=(device_at,),
        )
        home = lax.all_to_all(back.reshape(exchange), ("ex", "row"), 0, 0, tiled=True).reshape(packed_slots)
        half_scratch = (pltpu.VMEM((slot_total, half), bf16), slot_scratch[2])
        (d_h_mine,) = vmem_call(
            arrive,
            (shape((seq_len, half), bf16),),
            seq_len * slot_total * width,
            home,
            slot_of,
            scratch=half_scratch,
        )

        def land_at_home(home):
            (layer_out,) = vmem_call(
                land,
                (shape((seq_len, half), bf16),),
                seq_len * slot_total * width,
                home,
                slot_of,
                x_in,
                attn_part,
                attn_peer,
                scalars=(device_at,),
                scratch=half_scratch,
            )
            return layer_out

        def grads_of_expert(left, right):
            dims = (left.shape[1], right.shape[1])
            chunks = dims[0] // 256
            return pl.pallas_call(
                expert_grads,
                out_shape=shape(dims, f32),
                in_specs=[pl.BlockSpec(memory_space=pltpu.VMEM)] * 2,
                out_specs=pl.BlockSpec(memory_space=pltpu.HBM),
                scratch_shapes=[
                    pltpu.VMEM((chunks, dims[0] // chunks, dims[1]), f32),
                    pltpu.SemaphoreType.DMA((chunks,)),
                ],
                compiler_params=pltpu.CompilerParams(vmem_limit_bytes=16 * 2**20),
                cost_estimate=pl.CostEstimate(
                    flops=2 * slot_total * width * hidden, bytes_accessed=6 * width * hidden, transcendentals=0
                ),
            )(left, right)

        quarter = (width // 4, 3 * inner // 4) if cube else (width, 3 * inner)
        pieces = 4 if cube else 1
        if cube:
            d_h_mine, from_x, from_y = lax.optimization_barrier((d_h_mine, *normed_hops))
            normed_hops += [hop(from_x[: half // 2], "row", 2), hop(from_y[half // 2 :], "row", 1)]
        d_x_one, grad_gain_ffn, d_context, *out_pieces = vmem_call(
            functools.partial(come_home, cube),
            (
                shape((seq_len, width), f32),
                shape((1, width), f32),
                shape((seq_len, inner), bf16),
                *[shape((quarter[0], inner), bf16)] * pieces,
            ),
            4 * seq_len * width * inner,
            d_h_mine,
            swap_cores(d_h_mine),
            x_in,
            attn_part,
            attn_peer,
            d_out,
            g_peer,
            gain_ffn,
            out_w,
            context,
            scalars=(device_at,),
            scratch=(pltpu.VMEM((width, inner), bf16),),
        )
        d_h_part, grad_offset, *d_qkv_turned = vmem_call(
            functools.partial(attend_backward, cube),
            (
                shape((seq_len, width), bf16),
                shape((heads_here + 2, span), f32),
                *[shape((quarter[1], seq_len), bf16)] * pieces,
            ),
            6 * seq_len * width * inner + 10 * square,
            d_context,
            qkv,
            probs,
            qkv_w,
            scalars=(device_at,),
            scratch=(pltpu.VMEM((3 * inner, seq_len), bf16),),
        )
        grad_x, small = vmem_call(
            finish,
            (shape((seq_len, width), bf16), shape((heads_here + 2, width), f32)),
            0,
            d_h_part,
            swap_cores(d_h_part),
            x_in,
            d_x_one,
            gain_attn,
            grad_gain_ffn,
            grad_offset,
            offset_hot,
        )
        if cube:
            *normed_hops, _ = lax.optimization_barrier((*normed_hops, d_h_part))
            normed_near = jnp.concatenate(normed_hops, axis=0)
            normed_peer = swap_cores(normed_near)
            late_home, act_b, d_y, _ = lax.optimization_barrier((home, act_b, d_y, small))
            d_qkv_hops = plane_hops(d_qkv_turned[1:])
            *d_qkv_hops, layer_out, grad_down = lax.optimization_barrier(
                (*d_qkv_hops, land_at_home(late_home), grads_of_expert(act_b, d_y))
            )
            terms = vmem_call(
                qkv_terms,
                [shape((own_rows + 8, 3 * inner), bf16)] * 4,
                6 * seq_len * width * inner,
                normed_turned,
                small,
                grad_router,
                normed_near,
                normed_peer,
                d_qkv_turned[0],
                *d_qkv_hops,
                scalars=(device_at,),
                scratch=(pltpu.VMEM((width, quarter[1]), bf16),),
            )
            line = line_hops(terms[1:])
            rows, d_pre, _ = lax.optimization_barrier((rows, d_pre, terms[0]))
            grad_up = grads_of_expert(rows, d_pre)
            *out_pieces, _ = lax.optimization_barrier((*out_pieces, grad_up))
            *line, grad_up = lax.optimization_barrier((*line, grad_up))
            split = vmem_call(
                join_line,
                [shape((own_rows, 512), bf16)] * 4,
                0,
                terms[0],
                *line,
                scalars=(device_at,),
            )
            last = plane_hops(split[1:])
            grad_qkv, gain_one, gain_two, grad_rel, grad_router = vmem_call(
                join_plane,
                (
                    shape((3, own_rows, inner), f32),
                    shape((width,), f32),
                    shape((width,), f32),
                    shape((heads_here, BUCKETS), f32),
                    shape((experts, own_rows), f32),
                ),
                0,
                split[0],
                *last,
                scalars=(device_at,),
                scratch=(pltpu.VMEM((own_rows, 3 * inner), f32),),
            )
            out_hops = plane_hops(out_pieces[1:])
            out_blocks = vmem_call(
                join_blocks,
                [shape((own_rows, inner), bf16)] * 4,
                0,
                out_pieces[0],
                *out_hops,
            )
            *out_blocks, _ = lax.optimization_barrier((*out_blocks, last[0]))
            out_blocks = (out_blocks[0], *line_hops(out_blocks[1:]))
            grad_out = sum(part.astype(f32) for part in out_blocks)
        else:
            layer_out = land_at_home(home)
            grad_down, grad_up = grads_of_expert(act_b, d_y), grads_of_expert(rows, d_pre)
            grad_qkv = scatter_groups(dot(normed_turned, d_qkv_turned[0], 1, 1), own_rows)
            grad_qkv = grad_qkv.reshape(own_rows, 3, inner).transpose(1, 0, 2)
            grad_out = scatter_groups(out_pieces[0], own_rows)
            small = sum_groups(jnp.concatenate([small, grad_router]))
            gain_one, gain_two = small[heads_here], small[heads_here + 1]
            grad_rel = small[:heads_here, :BUCKETS]
            own_at = (device_at[0] * n_row + device_at[1]) * own_rows
            grad_router = lax.dynamic_slice(small, (heads_here + 2, own_at), (experts, own_rows))
        return (
            layer_out,
            grad_x,
            gain_one,
            grad_qkv,
            grad_rel.T,
            grad_out.T,
            gain_two,
            grad_router.T,
            grad_up[None],
            grad_down[None],
        )

    return per_device


def solution(mesh):
    return jax.shard_map(
        make_per_device(mesh),
        mesh=mesh,
        in_specs=(
            P(("ex", "row"), None),
            P(),
            P(None, ("ex", "row"), "col"),
            P(None, "col"),
            P("col", ("ex", "row")),
            P(),
            P(("ex", "row"), None),
            P(("ex", "row"), None, "col"),
            P(("ex", "row"), "col", None),
            P(("ex", "row"), None),
            P(("ex", "row")),
            P(("ex", "row")),
            P(("ex", "row")),
            P(("ex", "row"), "col"),
        ),
        out_specs=(
            P(("ex", "row"), "col"),
            P(("ex", "row"), None),
            P(),
            P(None, ("ex", "row"), "col"),
            P(None, "col"),
            P("col", ("ex", "row")),
            P(),
            P(("ex", "row"), None),
            P(("ex", "row"), None, "col"),
            P(("ex", "row"), "col", None),
        ),
        check_vma=False,
    )
```

```python
import functools
import math

import jax
import jax.numpy as jnp
from jax import lax
from jax.experimental import pallas as pl
from jax.experimental.pallas import tpu as pltpu
from jax.sharding import PartitionSpec as P

HEAD = 64
BUCKETS = 32

norm_eps = 1e-06
bucket_edges = (12, 16, 23, 32, 46, 64, 91)
highest = lax.Precision.HIGHEST
bf16 = jnp.bfloat16
f32 = jnp.float32

GATHER_ORDER = tuple(((k, m),) for m in range(4) for k in range(4))

def bucket_of(offset):
    distance = jnp.abs(offset)
    far_part = jnp.zeros(distance.shape, jnp.int32)
    for edge_at in bucket_edges:
        far_part = far_part + (distance >= edge_at).astype(jnp.int32)
    inside = jnp.where(distance < 8, distance, far_part + jnp.int32(8))
    upper = jnp.where(offset > 0, jnp.int32(BUCKETS // 2), jnp.int32(0))
    return inside + upper


def rms_scale(values):
    return lax.rsqrt(jnp.mean(values * values, axis=-1, keepdims=True) + norm_eps)


def dot(a, b, ca, cb):
    return lax.dot_general(a, b, (((ca,), (cb,)), ((), ())), preferred_element_type=f32)


def swap_cores(values):
    return lax.ppermute(values, "col", [(0, 1), (1, 0)])


def shape(dims, dtype):
    return jax.ShapeDtypeStruct(tuple(dims), dtype)


def vmem_call(kernel, out_shape, flops, *args, scalars=(), scratch=(), limit=12):
    nbytes = sum(math.prod(v.shape) * v.dtype.itemsize for v in (*args, *out_shape))
    spec = pl.BlockSpec(memory_space=pltpu.VMEM)
    limit = limit if nbytes < 16 * 2**20 else 48
    return pl.pallas_call(
        kernel,
        out_shape=out_shape,
        in_specs=[pl.BlockSpec(memory_space=pltpu.SMEM)] * len(scalars) + [spec] * len(args),
        out_specs=[spec] * len(out_shape),
        scratch_shapes=scratch,
        compiler_params=pltpu.CompilerParams(vmem_limit_bytes=limit * 2**20),
        cost_estimate=pl.CostEstimate(flops=flops, bytes_accessed=nbytes, transcendentals=0),
    )(*scalars, *args)


def block_rows(at_ref, order, count):
    if order is None:
        return [pl.ds(0, count)]
    ex_at, row_at = at_ref[0], at_ref[1]
    return [
        pl.ds(pl.multiple_of(((ex_at ^ k) * 4 + (row_at ^ m)) * count, 16), count)
        for part in order
        for k, m in part
    ]


def eye(size):
    dims = (size, size)
    same = lax.broadcasted_iota(jnp.int32, dims, 0) == lax.broadcasted_iota(jnp.int32, dims, 1)
    return same.astype(bf16)


def pack_weights(qkv_in, out_in, router_in, packed_out, qkv_ref, out_turned_ref, router_turned_ref, packed_ref, sems):
    pairs = ((qkv_in, qkv_ref), (out_in, out_turned_ref), (router_in, router_turned_ref))
    copies = [pltpu.make_async_copy(source, target, sems.at[i]) for i, (source, target) in enumerate(pairs)]
    for copy in copies:
        copy.start()
    inner, experts = qkv_ref.shape[2], router_turned_ref.shape[0]
    packed_ref[:, 4 * inner :] = jnp.zeros((packed_ref.shape[0], packed_ref.shape[1] - 4 * inner), bf16)
    for copy in copies:
        copy.wait()
    for part in range(3):
        packed_ref[:, part * inner : (part + 1) * inner] = qkv_ref[part].astype(bf16)
    packed_ref[:, 3 * inner : 4 * inner] = out_turned_ref[...].astype(bf16)
    router = dot(router_turned_ref[...].astype(bf16), eye(experts), 0, 0)
    packed_ref[:, 4 * inner : 4 * inner + experts] = router.astype(bf16)
    copy = pltpu.make_async_copy(packed_ref, packed_out, sems.at[3])
    copy.start()
    copy.wait()


def spread_bias(offset_ref, seg_ref, bias_ref):
    heads, seq_len, _ = bias_ref.shape
    span = offset_ref.shape[1]
    documents = lax.broadcasted_iota(jnp.int32, (8, seq_len), 0) == seg_ref[...]
    same_doc = dot(documents.astype(bf16), documents.astype(bf16), 0, 0) > 0.5
    for at in range(heads):
        spread = jnp.broadcast_to(offset_ref[at : at + 1, :], (seq_len, span))
        bias = pltpu.roll(spread, span - seq_len + 1, 1, stride=1, stride_axis=0)[:, :seq_len]
        bias_ref[at] = jnp.where(same_doc, bias, -1e30)


def first_norm(at_ref, x_ref, gain_ref, h_ref, turned_ref, half_ref):
    x_float = x_ref[...].astype(f32)
    h_one = (x_float * rms_scale(x_float) * gain_ref[...].reshape(1, -1)).astype(bf16)
    h_ref[...] = h_one
    turned_ref[...] = dot(h_one, eye(h_one.shape[0]), 0, 0).astype(bf16)
    half = half_ref.shape[0]
    half_ref[...] = jnp.where(at_ref[2] == 0, turned_ref[:half, :], turned_ref[half:, :])


def attend_forward(order, at_ref, h_ref, bias_ref, *refs):
    *block_refs, part_ref, qkv_ref, probs_ref, ctx_ref, w_ref, out_w_ref, router_ref = refs
    heads, inner = probs_ref.shape[0], ctx_ref.shape[1]
    for rows, block_ref in zip(block_rows(at_ref, order, block_refs[0].shape[0]), block_refs):
        w_ref[rows, :] = block_ref[:, : 3 * inner]
        out_w_ref[rows, :] = block_ref[:, 3 * inner : 4 * inner]
        router_ref[rows, :] = block_ref[:, 4 * inner :]
    qkv_ref[...] = dot(h_ref[...], w_ref[...], 1, 0).astype(bf16)
    for at in range(heads):
        take = lambda part: qkv_ref[:, part * inner + at * HEAD : part * inner + (at + 1) * HEAD]
        scores = dot(take(0), take(1), 1, 1) * 0.125 + bias_ref[at]
        expo = jnp.exp(scores - jnp.max(scores, axis=1, keepdims=True))
        probs = expo * (1.0 / jnp.sum(expo, axis=1, keepdims=True))
        probs_ref[at] = probs
        ctx = dot(probs.astype(bf16), take(2), 1, 0)
        ctx_ref[:, at * HEAD : (at + 1) * HEAD] = ctx.astype(bf16)
    part_ref[...] = dot(ctx_ref[...], out_w_ref[...], 1, 1).astype(bf16)


def spare_rows(experts, chunk):
    dims = (experts * 24, experts * 4)
    row, column = lax.broadcasted_iota(jnp.int32, dims, 0), lax.broadcasted_iota(jnp.int32, dims, 1)
    expert = lax.shift_right_logical(row * 2731, 16)
    inside = row - expert * 24
    wanted = expert * 4 + (inside - chunk * 4)
    return ((column == wanted) & (inside >= chunk * 4) & (inside < chunk * 4 + 4)).astype(bf16)


def pack_slots(values, packed_ref, low=0, before=None):
    if len(packed_ref.shape) == 2:
        packed_ref[:, low * 128 : low * 128 + values.shape[1]] = values.astype(bf16)
        return
    experts, chunks = packed_ref.shape[0], values.shape[1] // 128
    first = (packed_ref.shape[1] - 24) // 16 * 16
    values = values.astype(bf16)
    spare = 0.0
    for c in range(chunks):
        chunk = values[:, c * 128 : (c + 1) * 128]
        for e in range(experts):
            packed_ref[e, (low + c) * 16 : (low + c + 1) * 16, :] = chunk[e * 16 : (e + 1) * 16]
        spare = spare + dot(spare_rows(experts, low + c), chunk[experts * 16 :], 1, 0)
    for e in range(experts):
        rows = spare[e * 24 : (e + 1) * 24]
        if before is not None:
            rows = rows + before[e, first:, :].astype(f32)
        packed_ref[e, first:, :] = rows.astype(bf16)


def unpack_slots(packed_ref, low, target_ref, spare_ref):
    experts, chunks = packed_ref.shape[0], target_ref.shape[1] // 128
    first = (packed_ref.shape[1] - 24) // 16 * 16
    for e in range(experts):
        spare_ref[e * 24 : (e + 1) * 24, :] = packed_ref[e, first:, :].astype(f32)
    spare = spare_ref[...].astype(bf16)
    for c in range(chunks):
        lanes = slice(c * 128, (c + 1) * 128)
        for e in range(experts):
            rows = slice((low + c) * 16, (low + c + 1) * 16)
            target_ref[e * 16 : (e + 1) * 16, lanes] = packed_ref[e, rows, :]
        target_ref[experts * 16 :, lanes] = dot(spare_rows(experts, low + c), spare, 0, 0).astype(bf16)


def slot_places(slot_ref, packed_ref):
    slots = packed_ref.shape[0] * (1 if len(packed_ref.shape) == 2 else 20)
    dims = (slots, slot_ref.shape[1])
    return (lax.broadcasted_iota(jnp.int32, dims, 0) == slot_ref[...]).astype(bf16)


def pack_cotangent(g_ref, slot_ref, packed_ref):
    packed_ref[...] = jnp.zeros(packed_ref.shape, bf16)
    pack_slots(dot(slot_places(slot_ref, packed_ref), g_ref[...], 1, 0), packed_ref, g_ref.shape[1] // 128)


def dispatch(at_ref, x_ref, part_ref, peer_ref, gain_ref, slot_ref, before_ref, send_ref):
    half = x_ref.shape[1] // 2
    x_one = x_ref[...].astype(f32) + (part_ref[...].astype(f32) + peer_ref[...].astype(f32))
    h_two = (x_one * rms_scale(x_one) * gain_ref[...].reshape(1, -1)).astype(bf16)
    mine = jnp.where(at_ref[2] == 0, h_two[:, :half], h_two[:, half:])
    if len(send_ref.shape) == 2:
        send_ref[:, half:] = before_ref[:, half:]
    else:
        low, high = half // 128 * 16, half // 64 * 16
        send_ref[:, low:high, :] = before_ref[:, low:high, :]
    pack_slots(dot(slot_places(slot_ref, send_ref), mine, 1, 0), send_ref, 0, before_ref)


def run_expert(
    experts, row_size, at_ref, got_ref, peer_ref, router_ref, up_ref, down_ref,
    cross_ref, mine_ref, probs_ref, gate_part_ref, rows_ref, d_y_ref, act_ref, d_pre_ref, d_in_ref,
    got_rows_ref, peer_rows_ref, spare_ref,
):
    half = rows_ref.shape[1] // 2
    if len(got_ref.shape) == 3:
        unpack_slots(got_ref, 0, got_rows_ref, spare_ref)
        unpack_slots(peer_ref, 0, peer_rows_ref, spare_ref)
        got_ref, peer_ref = got_rows_ref, peer_rows_ref
    hidden = up_ref.shape[1]
    first_core = at_ref[2] == 0
    for at, refs in ((0, (got_ref, peer_ref)), (1, (peer_ref, got_ref))):
        pick = lambda lo: jnp.where(first_core, refs[0][:, lo : lo + half], refs[1][:, lo : lo + half])
        rows_ref[:, at * half : (at + 1) * half] = pick(0)
        d_y_ref[:, at * half : (at + 1) * half] = pick(half)
    rows, g_rows = rows_ref[...], d_y_ref[...].astype(f32)
    logits = dot(rows, router_ref[...], 1, 0)[:, :experts]
    expo = jnp.exp(logits - jnp.max(logits, axis=1, keepdims=True))
    probs = expo / jnp.sum(expo, axis=1, keepdims=True)
    probs_ref[...] = probs
    expert_at = at_ref[0] * row_size + at_ref[1]
    chosen = lax.broadcasted_iota(jnp.int32, probs.shape, 1) == expert_at
    gate = jnp.sum(jnp.where(chosen, probs, 0.0), axis=1, keepdims=True)
    d_y_ref[...] = (g_rows * gate).astype(bf16)
    step = 768 if hidden % 768 == 0 else hidden
    y_part = None
    for lo in range(0, hidden, step):
        cols = pl.ds(lo, step)
        pre_act = dot(rows_ref[...], up_ref[:, cols], 1, 0)
        cdf = 0.5 * (1.0 + lax.erf(pre_act * (1.0 / math.sqrt(2.0))))
        pdf = jnp.exp(-0.5 * pre_act * pre_act) * (1.0 / math.sqrt(2.0 * math.pi))
        act = (pre_act * cdf).astype(bf16)
        act_ref[:, cols] = act
        y_more = dot(act, down_ref[cols, :], 1, 0)
        d_pre = (dot(d_y_ref[...], down_ref[cols, :], 1, 1) * (cdf + pre_act * pdf)).astype(bf16)
        d_pre_ref[:, cols] = d_pre
        d_more = dot(d_pre, up_ref[:, cols], 1, 1)
        if lo == 0:
            y_part = y_more
            d_in_ref[...] = d_more
        else:
            y_part = y_part + y_more
            d_in_ref[...] += d_more
    gate_part = jnp.sum(g_rows * y_part, axis=1, keepdims=True)
    high = gate_part.astype(bf16)
    low = (gate_part - high.astype(f32)).astype(bf16)
    gate_part_ref[...] = high.astype(f32) + low.astype(f32)
    lane = lax.broadcasted_iota(jnp.int32, (rows.shape[0], 128), 1)
    beside = jnp.where(lane == 0, high.astype(f32), jnp.where(lane == 1, low.astype(f32), 0.0))
    cross_ref[:, 2 * half :] = beside.astype(bf16)
    d_in = d_in_ref[...]
    mine_ref[:, :half] = jnp.where(first_core, y_part[:, :half], y_part[:, half:])
    mine_ref[:, half:] = jnp.where(first_core, d_in[:, :half], d_in[:, half:])
    cross_ref[:, :half] = jnp.where(first_core, y_part[:, half:], y_part[:, :half]).astype(bf16)
    cross_ref[:, half : 2 * half] = jnp.where(first_core, d_in[:, half:], d_in[:, :half]).astype(bf16)


def settle(
    row_size, at_ref, mine_ref, crossed_ref, probs_ref, gate_part_ref, router_ref, rows_ref,
    back_ref, grad_router_ref,
):
    half = mine_ref.shape[1] // 2
    probs = probs_ref[...]
    expert_at = at_ref[0] * row_size + at_ref[1]
    chosen = (lax.broadcasted_iota(jnp.int32, probs.shape, 1) == expert_at).astype(f32)
    gate = jnp.sum(probs * chosen, axis=1, keepdims=True)
    beside = crossed_ref[:, 2 * half :].astype(f32)
    d_gate = gate_part_ref[...] + (beside[:, 0:1] + beside[:, 1:2])
    d_logits = (d_gate * gate * (chosen - probs)).astype(bf16)
    router_w = router_ref[...][:, : probs.shape[1]]
    router_mine = jnp.where(at_ref[2] == 0, router_w[:half], router_w[half:])
    y_gated = gate * (mine_ref[:, :half] + crossed_ref[:, :half].astype(f32))
    d_in = mine_ref[:, half:] + crossed_ref[:, half : 2 * half].astype(f32) + dot(d_logits, router_mine, 1, 1)
    pack_slots(jnp.concatenate([y_gated, d_in], axis=1), back_ref)
    grad_router_ref[...] = dot(d_logits, rows_ref[...], 0, 0)


def from_slots(home_ref, slot_ref, low, rows_ref, spare_ref):
    if len(home_ref.shape) == 3:
        unpack_slots(home_ref, low, rows_ref, spare_ref)
    else:
        rows_ref[...] = home_ref[:, low * 128 : low * 128 + rows_ref.shape[1]]
    dims = (rows_ref.shape[0], slot_ref.shape[1])
    place = (lax.broadcasted_iota(jnp.int32, dims, 0) == slot_ref[...]).astype(bf16)
    return dot(place, rows_ref[...], 0, 0)


def arrive(home_ref, slot_ref, d_h_ref, rows_ref, spare_ref):
    low = d_h_ref.shape[1] // 128
    d_h_ref[...] = from_slots(home_ref, slot_ref, low, rows_ref, spare_ref).astype(bf16)


def land(at_ref, home_ref, slot_ref, x_ref, part_ref, peer_ref, layer_ref, rows_ref, spare_ref):
    half = layer_ref.shape[1]
    y_home = from_slots(home_ref, slot_ref, 0, rows_ref, spare_ref)
    mine = lambda ref: jnp.where(at_ref[2] == 0, ref[:, :half], ref[:, half:]).astype(f32)
    layer_ref[...] = (mine(x_ref) + (mine(part_ref) + mine(peer_ref)) + y_home).astype(bf16)


def come_home(
    cube, at_ref, mine_ref, peer_ref, x_ref, part_ref, part_peer_ref, g_ref, g_peer_ref,
    gain_ref, out_w_ref, ctx_ref, d_x_ref, gain_grad_ref, d_ctx_ref, *refs,
):
    *piece_refs, grads_ref = refs
    first_core = at_ref[2] == 0
    both = lambda a, b: jnp.concatenate(
        [jnp.where(first_core, a, b), jnp.where(first_core, b, a)], axis=1
    )
    d_h = both(mine_ref[...], peer_ref[...]).astype(f32)
    x_one = x_ref[...].astype(f32) + (part_ref[...].astype(f32) + part_peer_ref[...].astype(f32))
    g_full = both(g_ref[...], g_peer_ref[...]).astype(f32)
    scale = rms_scale(x_one)
    normed = x_one * scale
    gain_grad_ref[...] = jnp.sum(d_h * normed, axis=0, keepdims=True)
    d_norm = d_h * gain_ref[...].reshape(1, -1)
    d_x = g_full + scale * (d_norm - normed * jnp.mean(d_norm * normed, axis=-1, keepdims=True))
    d_x_ref[...] = d_x
    d_x_b = d_x.astype(bf16)
    d_ctx_ref[...] = dot(d_x_b, out_w_ref[...], 1, 0).astype(bf16)
    grads_ref[...] = dot(d_x_b, ctx_ref[...], 0, 0).astype(bf16)
    rows = grads_ref.shape[0] // 16
    for m, piece_ref in enumerate(piece_refs):
        if not cube:
            piece_ref[...] = grads_ref[...]
            continue
        for k in range(4):
            start = pl.multiple_of(((at_ref[0] ^ k) * 4 + (at_ref[1] ^ m)) * rows, 16)
            piece_ref[k * rows : (k + 1) * rows, :] = grads_ref[pl.ds(start, rows), :]


def attend_backward(cube, at_ref, d_ctx_ref, qkv_ref, probs_ref, w_ref, d_h_ref, grad_offset_ref, *refs):
    *piece_refs, turned_ref = refs
    heads, seq_len, _ = probs_ref.shape
    inner = d_ctx_ref.shape[1]
    span = grad_offset_ref.shape[1]
    flip = (
        lax.broadcasted_iota(jnp.int32, (seq_len, seq_len), 0)
        + lax.broadcasted_iota(jnp.int32, (seq_len, seq_len), 1)
        == seq_len - 1
    ).astype(bf16)
    grad_offset_ref[...] = jnp.zeros(grad_offset_ref.shape, f32)
    for at in range(heads):
        cols = lambda part: pl.ds(part * inner + at * HEAD, HEAD)
        d_ctx = d_ctx_ref[:, at * HEAD : (at + 1) * HEAD]
        probs = probs_ref[at]
        d_probs = dot(d_ctx, qkv_ref[:, cols(2)], 1, 1)
        row_delta = jnp.sum(probs * d_probs, axis=1, keepdims=True)
        d_scores = (probs * (d_probs - row_delta)).astype(bf16)
        turned_ref[cols(0), :] = (dot(qkv_ref[:, cols(1)], d_scores, 0, 1) * 0.125).astype(bf16)
        turned_ref[cols(1), :] = (dot(qkv_ref[:, cols(0)], d_scores, 0, 0) * 0.125).astype(bf16)
        turned_ref[cols(2), :] = dot(d_ctx, probs.astype(bf16), 0, 0).astype(bf16)
        flipped = jnp.concatenate(
            [dot(flip, d_scores, 1, 0), jnp.zeros((seq_len, span - seq_len), f32)], axis=1
        )
        lined = pltpu.roll(flipped, 0, 1, stride=1, stride_axis=0)
        grad_offset_ref[at : at + 1, :] = jnp.sum(lined, axis=0, keepdims=True)
    size = piece_refs[0].shape[0]
    for m, piece_ref in enumerate(piece_refs):
        start = pl.multiple_of((at_ref[1] ^ m) * size, 16) if cube else 0
        piece_ref[...] = turned_ref[pl.ds(start, size), :]
    d_h_ref[...] = dot(turned_ref[...], w_ref[...], 0, 1).astype(bf16)


def qkv_terms(at_ref, turned_ref, small_ref, router_ref, *refs):
    mine_ref, peer_ref, piece_refs, block_refs, grads_ref = refs[0], refs[1], refs[2:6], refs[6:10], refs[10]
    half = mine_ref.shape[0] // 3
    from_mine = from_peer = 0.0
    for m in range(1, 4):
        rows = slice((m - 1) * half, m * half)
        from_mine = from_mine + dot(mine_ref[rows, :], piece_refs[m][...], 1, 1)
        from_peer = from_peer + dot(peer_ref[rows, :], piece_refs[m][...], 1, 1)
    own = dot(turned_ref[...], piece_refs[0][...], 1, 1)
    first_core = at_ref[2] == 0
    grads_ref[:half, :] = (own[:half] + jnp.where(first_core, from_mine, from_peer)).astype(bf16)
    grads_ref[half:, :] = (own[half:] + jnp.where(first_core, from_peer, from_mine)).astype(bf16)
    rows, size = block_refs[0].shape[0] - 8, grads_ref.shape[1]
    width = small_ref.shape[1]
    part = width // 4
    for k, block_ref in enumerate(block_refs):
        block_ref[rows:, :width] = small_ref[...].astype(bf16)
        router = jnp.zeros((router_ref.shape[0], part), f32)
        for z in range(4):
            router = jnp.where((at_ref[0] ^ k) == z, router_ref[:, z * part : (z + 1) * part], router)
        for i in range(2):
            low = width + i * part
            block_ref[rows:, low : low + part] = router[i * 8 : (i + 1) * 8].astype(bf16)
        for m in range(4):
            start = ((at_ref[0] ^ k) * 4 + (at_ref[1] ^ m)) * rows
            block_ref[:rows, m * size : (m + 1) * size] = grads_ref[pl.ds(pl.multiple_of(start, 16), rows), :]


def pair_sum(refs):
    a, b, c, d = (ref[...].astype(f32) for ref in refs)
    return (a + b) + (c + d)


def join_line(at_ref, *refs):
    total = pair_sum(refs[:4])
    rows = refs[4].shape[0]
    size = total.shape[1] // 4
    width = size * 8 // 3
    part = width // 16
    extra = total[rows:]
    for m, piece_ref in enumerate(refs[4:]):
        piece_ref[...] = jnp.zeros(piece_ref.shape, bf16)
        piece_ref[:, :size] = total[:rows, m * size : (m + 1) * size].astype(bf16)
        for i in range(2):
            for j in range(width // 128):
                line = extra[6 + i : 7 + i, j * 128 : (j + 1) * 128]
                piece_ref[i * 8 + j : i * 8 + j + 1, 384:] = line.astype(bf16)
            router = jnp.zeros((8, part), f32)
            for row in range(4):
                low = width + i * 4 * part + row * part
                router = jnp.where((at_ref[1] ^ m) == row, extra[:, low : low + part], router)
            piece_ref[32 + i * 8 : 40 + i * 8, 384 : 384 + part] = router.astype(bf16)
        piece_ref[16:24, 384:] = extra[:, :128].astype(bf16)


def join_plane(at_ref, *refs):
    piece_refs, (out_ref, gain_one_ref, gain_two_ref, rel_ref, router_ref, line_ref) = refs[:4], refs[4:]
    size = line_ref.shape[1] // 4
    for quarter in range(4):
        piece = 0.0
        for m, piece_ref in enumerate(piece_refs):
            piece = jnp.where((at_ref[1] ^ m) == quarter, piece_ref[:, :size].astype(f32), piece)
        line_ref[:, quarter * size : (quarter + 1) * size] = piece
    inner = out_ref.shape[2]
    for part in range(3):
        out_ref[part] = line_ref[:, part * inner : (part + 1) * inner]
    extra = pair_sum([ref.at[:, 384:] for ref in piece_refs])
    for i, gain_ref in enumerate((gain_one_ref, gain_two_ref)):
        for j in range(gain_ref.shape[0] // 128):
            gain_ref[pl.ds(j * 128, 128)] = extra[i * 8 + j]
    rel_ref[...] = extra[16 : 16 + rel_ref.shape[0], : rel_ref.shape[1]]
    router_ref[...] = extra[32 : 32 + router_ref.shape[0], : router_ref.shape[1]]


def join_blocks(*refs):
    total = pair_sum(refs[:4])
    rows = total.shape[0] // 4
    for k, block_ref in enumerate(refs[4:]):
        block_ref[...] = total[k * rows : (k + 1) * rows].astype(bf16)


def finish(
    d_h_ref, peer_ref, x_ref, d_x_ref, gain_ref, gain_grad_ref, grad_offset_ref, hot_ref, grad_x_ref, small_ref,
):
    d_h = d_h_ref[...].astype(f32) + peer_ref[...].astype(f32)
    x_float = x_ref[...].astype(f32)
    scale = rms_scale(x_float)
    normed = x_float * scale
    d_norm = d_h * gain_ref[...].reshape(1, -1)
    grad_x = d_x_ref[...] + scale * (
        d_norm - normed * jnp.mean(d_norm * normed, axis=-1, keepdims=True)
    )
    grad_x_ref[...] = grad_x.astype(bf16)
    heads, buckets = grad_offset_ref.shape[0] - 2, hot_ref.shape[1]
    small_ref[...] = jnp.zeros(small_ref.shape, f32)
    grad_rel = lax.dot_general(
        grad_offset_ref[...], hot_ref[...], (((1,), (0,)), ((), ())), precision=highest, preferred_element_type=f32
    )
    small_ref[:, :buckets] = grad_rel
    small_ref[heads : heads + 1, :] = jnp.sum(d_h * normed, axis=0, keepdims=True)
    small_ref[heads + 1 : heads + 2, :] = gain_grad_ref[...]


def expert_grads(left_ref, right_ref, out_ref, held_ref, sems):
    count = held_ref.shape[1]
    copies = []
    for at in range(out_ref.shape[0] // count):
        rows = pl.ds(at * count, count)
        held_ref[at] = dot(left_ref[:, rows], right_ref[...], 0, 0)
        copies.append(pltpu.make_async_copy(held_ref.at[at], out_ref.at[rows, :], sems.at[at]))
        copies[-1].start()
    for copy in copies:
        copy.wait()


def experts_pad(experts):
    return -(-experts // 128) * 128


def make_per_device(mesh):
    n_ex, n_row = mesh.shape["ex"], mesh.shape["row"]
    groups = n_ex * n_row

    def hop(values, axis, step):
        return lax.ppermute(values, axis, [(i, i ^ step) for i in range(mesh.shape[axis])])

    def whole_cube(rows):
        return n_ex == 4 and n_row == 4 and rows == 48

    def gather_blocks(shard, meanwhile):
        rows, width = shard.shape
        if whole_cube(rows):
            near, far, farther = (hop(shard, "ex", k) for k in (1, 2, 3))
            x_own, y_own = hop(shard, "row", 1), hop(shard, "row", 2)
            near, x_own, y_own = lax.optimization_barrier((near, x_own, y_own))
            xs, ys = [x_own, hop(near, "row", 1)], [y_own, hop(near, "row", 2)]
            diagonal = [hop(x_own, "row", 2)]
            beside = meanwhile(near)
            far, farther, diagonal[0], *beside = lax.optimization_barrier((far, farther, diagonal[0], *beside))
            for part in (far, farther):
                xs.append(hop(part, "row", 1))
                ys.append(hop(part, "row", 2))
            diagonal += [hop(ys[1], "row", 1), hop(xs[2], "row", 2), hop(ys[3], "row", 1)]
            return [shard, near, far, farther, *xs, *ys, *diagonal], beside
        part = lax.all_gather(shard, "ex", axis=0)
        part = jnp.broadcast_to(part[None], (n_row, n_ex, rows, width))
        part = lax.all_to_all(part, "row", split_axis=0, concat_axis=0, tiled=True)
        return [part.transpose(1, 0, 2, 3).reshape(groups * rows, width)], meanwhile(shard)

    def scatter_groups(grads, rows):
        part = grads.astype(bf16).reshape(n_ex, n_row, rows, -1).transpose(1, 0, 2, 3)
        part = lax.all_to_all(part, "row", split_axis=0, concat_axis=0, tiled=True)
        part = jnp.sum(part.astype(f32), axis=0).astype(bf16)
        part = lax.all_to_all(part, "ex", split_axis=0, concat_axis=0, tiled=True)
        return jnp.sum(part.astype(f32), axis=0)

    def plane_hops(parts):
        return [hop(part, "row", m + 1) for m, part in enumerate(parts)]

    def line_hops(parts):
        return [hop(part, "ex", k + 1) for k, part in enumerate(parts)]

    def sum_groups(values):
        for axis in ("row", "ex"):
            step = 1
            while step < mesh.shape[axis]:
                values = values + hop(values, axis, step)
                step *= 2
        return values

    def per_device(
        x_in,
        gain_attn,
        w_qkv,
        rel_bias,
        w_out,
        gain_ffn,
        w_router,
        w_up,
        w_down,
        seg_ids,
        expert_ids,
        slot_ids,
        drop_flags,
        d_out,
    ):
        seq_len, width = x_in.shape
        heads_here = rel_bias.shape[1]
        inner = w_qkv.shape[2]
        own_rows = w_qkv.shape[1]
        experts = w_router.shape[1]
        wide = inner + experts_pad(experts)
        half = d_out.shape[1]
        hidden = w_up.shape[2]
        device_at = jnp.stack([lax.axis_index(axis).astype(jnp.int32) for axis in ("ex", "row", "col")])
        device_at, w_qkv = lax.optimization_barrier((device_at, w_qkv))
        cube = whole_cube(own_rows)
        capacity = 5 * seq_len // (4 * experts)
        tight = cube and experts == 16 and capacity == 20 and width == 768
        slots = capacity if tight else -(-capacity // 8) * 8
        slot_total = experts * slots
        packed_slots = (experts, slots * width // 128, 128) if tight else (slot_total, width)
        exchange = packed_slots if tight else (experts, slots, width)
        slot_scratch = (
            pltpu.VMEM((slot_total, width), bf16),
            pltpu.VMEM((slot_total, width), bf16),
            pltpu.VMEM((experts * 24, 128), f32),
        )
        gather_order = GATHER_ORDER if cube else None

        turned = (w_qkv, w_out.T, w_router.T)
        packed_shape = shape((own_rows, 3 * inner + wide), bf16)
        packed = pl.pallas_call(
            pack_weights,
            out_shape=packed_shape,
            in_specs=[pl.BlockSpec(memory_space=pltpu.HBM)] * 3,
            out_specs=pl.BlockSpec(memory_space=pltpu.HBM),
            scratch_shapes=[
                *(pltpu.VMEM(v.shape, v.dtype) for v in turned),
                pltpu.VMEM(packed_shape.shape, bf16),
                pltpu.SemaphoreType.DMA((4,)),
            ],
            compiler_params=pltpu.CompilerParams(vmem_limit_bytes=60 * 2**20),
        )(*turned)

        span = 2 * seq_len
        offsets = jnp.arange(span, dtype=jnp.int32) - (seq_len - 1)
        offset_hot = (
            bucket_of(offsets)[:, None] == jnp.arange(BUCKETS, dtype=jnp.int32)[None, :]
        ).astype(f32)
        per_offset = jnp.einsum("bh,ob->ho", rel_bias, offset_hot, precision=highest)

        slot_of = expert_ids * slots + slot_ids
        if tight:
            spare_of = experts * 16 + expert_ids * 4 + slot_ids - 16
            slot_of = jnp.where(slot_ids < 16, expert_ids * 16 + slot_ids, spare_of)
        slot_of = jnp.where(drop_flags == 1, slot_total, slot_of)[None]

        def prepare(after):
            late_up, late_down, _ = lax.optimization_barrier((w_up[0], w_down[0], after))
            late_offset, late_x, _ = lax.optimization_barrier((per_offset, x_in, after))
            (bias,) = vmem_call(
                spread_bias, (shape((heads_here, seq_len, seq_len), f32),), 0, late_offset, seg_ids
            )
            normed = vmem_call(
                first_norm,
                (shape((seq_len, width), bf16), shape((width, seq_len), bf16), shape((half, seq_len), bf16)),
                0,
                late_x,
                gain_attn,
                scalars=(device_at,),
            )
            return [late_up.astype(bf16), late_down.astype(bf16), bias, *normed]

        blocks, beside = gather_blocks(packed, prepare)
        up_w, down_w, bias, h_one, normed_turned, normed_mine = beside
        g_peer = swap_cores(d_out)

        square = seq_len * seq_len * heads_here * HEAD
        attn_part, qkv, probs, context, qkv_w, out_w, router_w = vmem_call(
            functools.partial(attend_forward, gather_order),
            (
                shape((seq_len, width), bf16),
                shape((seq_len, 3 * inner), bf16),
                shape((heads_here, seq_len, seq_len), f32),
                shape((seq_len, inner), bf16),
                shape((width, 3 * inner), bf16),
                shape((width, inner), bf16),
                shape((width, wide - inner), bf16),
            ),
            8 * seq_len * width * inner + 4 * square,
            h_one,
            bias,
            *blocks,
            scalars=(device_at,),
        )
        attn_peer = swap_cores(attn_part)
        late_g, _ = lax.optimization_barrier((d_out, attn_part))
        (g_packed,) = vmem_call(pack_cotangent, (shape(packed_slots, bf16),), 0, late_g, slot_of)
        (send,) = vmem_call(
            dispatch,
            (shape(packed_slots, bf16),),
            2 * seq_len * slot_total * width,
            x_in,
            attn_part,
            attn_peer,
            gain_ffn,
            slot_of,
            g_packed,
            scalars=(device_at,),
        )
        got = lax.all_to_all(send.reshape(exchange), ("ex", "row"), 0, 0, tiled=True).reshape(packed_slots)
        if cube:
            later_normed, got = lax.optimization_barrier((normed_mine, got))
            normed_hops = plane_hops([later_normed] * 2)
        crossing, mine, router_probs, gate_part, rows, d_y, act_b, d_pre = vmem_call(
            functools.partial(run_expert, experts, n_row),
            (
                shape((slot_total, width + 128), bf16),
                shape((slot_total, width), f32),
                shape((slot_total, experts), f32),
                shape((slot_total, 1), f32),
                shape((slot_total, width), bf16),
                shape((slot_total, width), bf16),
                shape((slot_total, hidden), bf16),
                shape((slot_total, hidden), bf16),
            ),
            8 * slot_total * width * hidden,
            got,
            swap_cores(got),
            router_w,
            up_w,
            down_w,
            scalars=(device_at,),
            scratch=(pltpu.VMEM((slot_total, width), f32), *slot_scratch),
        )
        if cube:
            crossing, g_peer, *normed_hops = lax.optimization_barrier((crossing, g_peer, *normed_hops))
        back, grad_router = vmem_call(
            functools.partial(settle, n_row),
            (shape(packed_slots, bf16), shape((experts, width), f32)),
            2 * slot_total * half * experts,
            mine,
            swap_cores(crossing),
            router_probs,
            gate_part,
            router_w,
            rows,
            scalars=(device_at,),
        )
        home = lax.all_to_all(back.reshape(exchange), ("ex", "row"), 0, 0, tiled=True).reshape(packed_slots)
        half_scratch = (pltpu.VMEM((slot_total, half), bf16), slot_scratch[2])
        (d_h_mine,) = vmem_call(
            arrive,
            (shape((seq_len, half), bf16),),
            seq_len * slot_total * width,
            home,
            slot_of,
            scratch=half_scratch,
        )

        def land_at_home(home):
            (layer_out,) = vmem_call(
                land,
                (shape((seq_len, half), bf16),),
                seq_len * slot_total * width,
                home,
                slot_of,
                x_in,
                attn_part,
                attn_peer,
                scalars=(device_at,),
                scratch=half_scratch,
            )
            return layer_out

        def grads_of_expert(left, right):
            dims = (left.shape[1], right.shape[1])
            chunks = dims[0] // 256
            return pl.pallas_call(
                expert_grads,
                out_shape=shape(dims, f32),
                in_specs=[pl.BlockSpec(memory_space=pltpu.VMEM)] * 2,
                out_specs=pl.BlockSpec(memory_space=pltpu.HBM),
                scratch_shapes=[
                    pltpu.VMEM((chunks, dims[0] // chunks, dims[1]), f32),
                    pltpu.SemaphoreType.DMA((chunks,)),
                ],
                compiler_params=pltpu.CompilerParams(vmem_limit_bytes=16 * 2**20),
                cost_estimate=pl.CostEstimate(
                    flops=2 * slot_total * width * hidden, bytes_accessed=6 * width * hidden, transcendentals=0
                ),
            )(left, right)

        quarter = (width // 4, 3 * inner // 4) if cube else (width, 3 * inner)
        pieces = 4 if cube else 1
        if cube:
            d_h_mine, from_x, from_y = lax.optimization_barrier((d_h_mine, *normed_hops))
            normed_hops += [hop(from_x[: half // 2], "row", 2), hop(from_y[half // 2 :], "row", 1)]
        d_x_one, grad_gain_ffn, d_context, *out_pieces = vmem_call(
            functools.partial(come_home, cube),
            (
                shape((seq_len, width), f32),
                shape((1, width), f32),
                shape((seq_len, inner), bf16),
                *[shape((quarter[0], inner), bf16)] * pieces,
            ),
            4 * seq_len * width * inner,
            d_h_mine,
            swap_cores(d_h_mine),
            x_in,
            attn_part,
            attn_peer,
            d_out,
            g_peer,
            gain_ffn,
            out_w,
            context,
            scalars=(device_at,),
            scratch=(pltpu.VMEM((width, inner), bf16),),
        )
        d_h_part, grad_offset, *d_qkv_turned = vmem_call(
            functools.partial(attend_backward, cube),
            (
                shape((seq_len, width), bf16),
                shape((heads_here + 2, span), f32),
                *[shape((quarter[1], seq_len), bf16)] * pieces,
            ),
            6 * seq_len * width * inner + 10 * square,
            d_context,
            qkv,
            probs,
            qkv_w,
            scalars=(device_at,),
            scratch=(pltpu.VMEM((3 * inner, seq_len), bf16),),
        )
        grad_x, small = vmem_call(
            finish,
            (shape((seq_len, width), bf16), shape((heads_here + 2, width), f32)),
            0,
            d_h_part,
            swap_cores(d_h_part),
            x_in,
            d_x_one,
            gain_attn,
            grad_gain_ffn,
            grad_offset,
            offset_hot,
        )
        if cube:
            *normed_hops, _ = lax.optimization_barrier((*normed_hops, d_h_part))
            normed_near = jnp.concatenate(normed_hops, axis=0)
            normed_peer = swap_cores(normed_near)
            act_b, d_y, _ = lax.optimization_barrier((act_b, d_y, small))
            d_qkv_hops = plane_hops(d_qkv_turned[1:])
            *d_qkv_hops, grad_down = lax.optimization_barrier((*d_qkv_hops, grads_of_expert(act_b, d_y)))
            terms = vmem_call(
                qkv_terms,
                [shape((own_rows + 8, 3 * inner), bf16)] * 4,
                6 * seq_len * width * inner,
                normed_turned,
                small,
                grad_router,
                normed_near,
                normed_peer,
                d_qkv_turned[0],
                *d_qkv_hops,
                scalars=(device_at,),
                scratch=(pltpu.VMEM((width, quarter[1]), bf16),),
            )
            line = line_hops(terms[1:])
            rows, d_pre, _ = lax.optimization_barrier((rows, d_pre, terms[0]))
            grad_up = grads_of_expert(rows, d_pre)
            *out_pieces, late_home, _ = lax.optimization_barrier((*out_pieces, home, grad_up))
            *line, grad_up, layer_out = lax.optimization_barrier((*line, grad_up, land_at_home(late_home)))
            split = vmem_call(
                join_line,
                [shape((own_rows, 512), bf16)] * 4,
                0,
                terms[0],
                *line,
                scalars=(device_at,),
            )
            last = plane_hops(split[1:])
            grad_qkv, gain_one, gain_two, grad_rel, grad_router = vmem_call(
                join_plane,
                (
                    shape((3, own_rows, inner), f32),
                    shape((width,), f32),
                    shape((width,), f32),
                    shape((heads_here, BUCKETS), f32),
                    shape((experts, own_rows), f32),
                ),
                0,
                split[0],
                *last,
                scalars=(device_at,),
                scratch=(pltpu.VMEM((own_rows, 3 * inner), f32),),
            )
            out_hops = plane_hops(out_pieces[1:])
            out_blocks = vmem_call(
                join_blocks,
                [shape((own_rows, inner), bf16)] * 4,
                0,
                out_pieces[0],
                *out_hops,
            )
            *out_blocks, _ = lax.optimization_barrier((*out_blocks, last[0]))
            out_blocks = (out_blocks[0], *line_hops(out_blocks[1:]))
            grad_out = sum(part.astype(f32) for part in out_blocks)
        else:
            layer_out = land_at_home(home)
            grad_down, grad_up = grads_of_expert(act_b, d_y), grads_of_expert(rows, d_pre)
            grad_qkv = scatter_groups(dot(normed_turned, d_qkv_turned[0], 1, 1), own_rows)
            grad_qkv = grad_qkv.reshape(own_rows, 3, inner).transpose(1, 0, 2)
            grad_out = scatter_groups(out_pieces[0], own_rows)
            small = sum_groups(jnp.concatenate([small, grad_router]))
            gain_one, gain_two = small[heads_here], small[heads_here + 1]
            grad_rel = small[:heads_here, :BUCKETS]
            own_at = (device_at[0] * n_row + device_at[1]) * own_rows
            grad_router = lax.dynamic_slice(small, (heads_here + 2, own_at), (experts, own_rows))
        return (
            layer_out,
            grad_x,
            gain_one,
            grad_qkv,
            grad_rel.T,
            grad_out.T,
            gain_two,
            grad_router.T,
            grad_up[None],
            grad_down[None],
        )

    return per_device


def solution(mesh):
    return jax.shard_map(
        make_per_device(mesh),
        mesh=mesh,
        in_specs=(
            P(("ex", "row"), None),
            P(),
            P(None, ("ex", "row"), "col"),
            P(None, "col"),
            P("col", ("ex", "row")),
            P(),
            P(("ex", "row"), None),
            P(("ex", "row"), None, "col"),
            P(("ex", "row"), "col", None),
            P(("ex", "row"), None),
            P(("ex", "row")),
            P(("ex", "row")),
            P(("ex", "row")),
            P(("ex", "row"), "col"),
        ),
        out_specs=(
            P(("ex", "row"), "col"),
            P(("ex", "row"), None),
            P(),
            P(None, ("ex", "row"), "col"),
            P(None, "col"),
            P("col", ("ex", "row")),
            P(),
            P(("ex", "row"), None),
            P(("ex", "row"), None, "col"),
            P(("ex", "row"), "col", None),
        ),
        check_vma=False,
    )
```
